32 devices in a mesh: view: 16 (over z, x, core), row: 2 (over y).
Axes of the slice: x: 2, y: 2, z: 4, core: 2. Of those that a mesh axis runs over, the one named last changes fastest.
Arguments:
- layers: bfloat16 [3, 3, 96, 1024], P(None, None, 'row'), may hold values from 0.19921875 to 1
- target: bfloat16 [16, 96, 1024], P('view', 'row'), may hold values from 0.049804688 to 0.5
- shifts: int32 [16, 3, 2], P('view'), may hold values from -8 to 8, as said below
Outputs:
- updated: float32 [3, 3, 96, 1024], P(None, None, 'row')
The draws below stay inside these ranges and needn't reach their ends.
Inputs may be any that keep to these rules, and one draw needn't show every extreme that they name: `shifts`: for every layer and each of the two components, one view has shift 8 and another view has shift -8.
All inputs are finite; a program needn't handle non-finite values.
Results may differ from the reference program's by a relative error of at most 0.0003.
Values may be sent and summed in bfloat16 or wider, within the bound.
A program may use at most 64 MiB of HBM per device.

```python
import jax
import jax.numpy as jnp
from jax import lax

COLS = 1024
LAYERS = 3
FRAMES = 3
HALO = 8
VIEWS = 16
ROWS = 96


def draw_shifts(key, part):
    key = jax.random.fold_in(key, 7)
    key_base, key_high, key_step = jax.random.split(key, 3)
    base = jax.random.randint(key_base, (VIEWS, LAYERS, 2), -HALO, HALO + 1)
    high = jax.random.randint(key_high, (LAYERS, 2), 0, VIEWS)
    step = jax.random.randint(key_step, (LAYERS, 2), 1, VIEWS)
    low = (high + step) % VIEWS
    view_ids = jnp.arange(VIEWS)[:, None, None]
    base = jnp.where(view_ids == high[None], HALO, base)
    base = jnp.where(view_ids == low[None], -HALO, base)
    return base.astype(jnp.int32)


def steps_of(key, extent, cuts, least, top_value):
    def one(axis_at, blocks):
        draws = jax.random.uniform(jax.random.fold_in(jax.random.fold_in(key, 6), axis_at), (blocks,), jnp.float32, least / len(cuts), top_value / len(cuts))
        return jnp.repeat(jnp.exp(draws), extent[axis_at] // blocks).reshape((-1,) + (1,) * (len(extent) - axis_at - 1))

    factor_of = one(*cuts[0])
    for cut in cuts[1:]:
        factor_of = factor_of * one(*cut)
    return factor_of


def setup_inputs(seed: int = 0) -> dict:
    key_list = jax.random.split(jax.random.key(seed), 4)
    layers = jnp.clip(0.19921875 + 0.80078125 * jax.random.uniform(key_list[0], (FRAMES, LAYERS, ROWS, COLS), jnp.float32) ** steps_of(key_list[0], (FRAMES, LAYERS, ROWS, COLS), ((2, 2),), -0.2, 0.2), 0.19921875, 1.0).astype(jnp.bfloat16)
    target = jnp.clip(0.049804688 + 0.4501953 * jax.random.uniform(key_list[1], (VIEWS, ROWS, COLS), jnp.float32) ** steps_of(key_list[1], (VIEWS, ROWS, COLS), ((0, 16), (1, 2)), -0.2, 0.2), 0.049804688, 0.5).astype(jnp.bfloat16)
    shifts = draw_shifts(jax.random.fold_in(key_list[3], 71), 0)
    return dict(layers=layers, target=target, shifts=shifts)


regular = 0.05


def project_view(padded, shift_pair, frame_count, row_count, col_count):
    pieces = []
    for layer in range(LAYERS):
        start_row = (HALO + shift_pair[layer, 0]).astype(jnp.int32)
        start_col = (HALO + shift_pair[layer, 1]).astype(jnp.int32)
        zero = jnp.zeros((), jnp.int32)
        piece = lax.dynamic_slice(padded[:, layer], (zero, start_row, start_col), (frame_count, row_count, col_count))
        pieces.append(piece.astype(jnp.float32))
    return pieces


def product_except(pieces, skip):
    result = None
    for layer in range(len(pieces)):
        if layer != skip:
            result = pieces[layer] if result is None else result * pieces[layer]
    return result


def reference(layers, target, shifts):
    frame_count, layer_count, row_count, col_count = layers.shape
    padded = jnp.pad(layers, ((0, 0), (0, 0), (HALO, HALO), (HALO, HALO)))

    def one_view(carry, inputs):
        upper, lower = carry
        image, shift_pair = inputs
        pieces = project_view(padded, shift_pair, frame_count, row_count, col_count)
        whole_product = pieces[0]
        for layer in range(1, layer_count):
            whole_product = whole_product * pieces[layer]
        shown = jnp.sum(whole_product, axis=0) / frame_count
        image_f = image.astype(jnp.float32)
        uppers = []
        lowers = []
        for layer in range(layer_count):
            others = product_except(pieces, layer)
            terms = jnp.stack([image_f[None] * others, shown[None] * others])
            terms = jnp.pad(terms, ((0, 0), (0, 0), (HALO, HALO), (HALO, HALO)))
            start_row = (HALO - shift_pair[layer, 0]).astype(jnp.int32)
            start_col = (HALO - shift_pair[layer, 1]).astype(jnp.int32)
            zero = jnp.zeros((), jnp.int32)
            back = lax.dynamic_slice(terms, (zero, zero, start_row, start_col), (2, frame_count, row_count, col_count))
            uppers.append(back[0])
            lowers.append(back[1])
        upper = upper + jnp.stack(uppers, axis=1)
        lower = lower + jnp.stack(lowers, axis=1)
        return (upper, lower), None

    start = jnp.zeros(layers.shape, jnp.float32)
    (upper, lower), _ = lax.scan(one_view, (start, start), (target, shifts))
    return layers.astype(jnp.float32) * (upper + regular) / (lower + regular)
```

```python
import functools
import math

import jax
import jax.numpy as jnp
from jax import lax
from jax.experimental import pallas as pl
from jax.experimental.pallas import tpu as pltpu
from jax.sharding import PartitionSpec as P

HALO = 8
LANES = 128
EDGE = 16
MARGIN = 32
REGULAR = 0.05
MESH = pl.DeviceIdType.MESH


def split_views(views):
    across = 1
    while (2 * across) ** 2 * 2 <= views:
        across *= 2
    return views // (2 * across), across


def code_range(views):
    low = math.log(REGULAR / (views + REGULAR))
    high = math.log((0.5 * views + REGULAR) / REGULAR)
    return 0.5 * (low + high), (high - low) / 65000.0


def kernel(
    views, rows_of, shifts_ref, layers_ref, target_ref, out_ref,
    send_win, recv_win, shift_out, shift_in, shift_smem, halo_out, halo_in,
    layer_win, target_win, others_win, shown_win, third_win, upper, lower, packed, slots,
    win_send, win_recv, up_send, up_recv, down_send, down_recv,
    shift_send, shift_recv, smem_sem, lh_send, lh_recv,
    col_send, x_send, core_send, slot_recv,
):
    frames, layer_count, rows, cols = layers_ref.shape
    strip = cols // views
    planes = frames * layer_count
    height = rows + 2 * EDGE
    inner = rows + 2 * HALO
    depth, across = split_views(views)
    groups = 2 if strip == 64 else 1
    short = rows // groups
    tiles = cols // LANES
    middle, step = code_range(views)

    me = lax.axis_index("view")
    row = lax.axis_index("row")
    above, below = row > 0, row < rows_of - 1

    barrier = pltpu.get_barrier_semaphore()

    def greet(j, carry):
        partner = lax.rem(me + j, views)

        @pl.when(j > 0)
        def _():
            pl.semaphore_signal(barrier, inc=1, device_id=(partner, row), device_id_type=MESH)

        @pl.when(above)
        def _():
            pl.semaphore_signal(barrier, inc=1, device_id=(partner, row - 1), device_id_type=MESH)

        @pl.when(below)
        def _():
            pl.semaphore_signal(barrier, inc=1, device_id=(partner, row + 1), device_id_type=MESH)

        return carry

    lax.fori_loop(0, views, greet, 0)

    lane = lax.broadcasted_iota(jnp.int32, (1, LANES), 1)

    def window(load, index):
        start = strip * index - MARGIN
        tile = (start + LANES) // LANES - 1
        offset = start - tile * LANES
        first = load(jnp.maximum(tile, 0))
        second = load(jnp.minimum(tile + 1, tiles - 1))
        turn = lax.rem(LANES - offset, LANES)
        first = pltpu.roll(first, turn, 1)
        second = pltpu.roll(second, turn, 1)
        both = jnp.where(lane < LANES - offset, first, second)
        col = start + lane
        return jnp.where((col >= 0) & (col < cols), both, 0.0)

    place = lax.broadcasted_iota(jnp.int32, (8, LANES), 1)
    block = jnp.zeros((8, LANES), jnp.int32)
    for k in range(layer_count):
        for axis in range(2):
            block = jnp.where(place == 2 * k + axis, shifts_ref[0, k, axis], block)
    shift_out[...] = block
    shift_in[me] = block

    def fill(c, carry):
        def load(tile):
            where = pl.ds(pl.multiple_of(tile * LANES, LANES), LANES)
            return target_ref[0, :, where].astype(jnp.float32)

        send_win[c] = window(load, c).astype(jnp.bfloat16)
        return carry

    lax.fori_loop(0, views, fill, 0)
    recv_win[me, EDGE : EDGE + rows, :] = send_win[me]

    for f in range(frames):
        for k in range(layer_count):
            def load(tile):
                where = pl.ds(pl.multiple_of(tile * LANES, LANES), LANES)
                return layers_ref[f, k, :, where].astype(jnp.float32)

            plane = window(load, me)
            at = f * layer_count + k
            layer_win[at, EDGE : EDGE + rows, :] = plane
            halo_out[0, at] = plane[:EDGE].astype(jnp.bfloat16)
            halo_out[1, at] = plane[rows - EDGE :].astype(jnp.bfloat16)

    def shift_copy(j):
        partner = lax.rem(me + j, views)
        return pltpu.make_async_remote_copy(
            src_ref=shift_out, dst_ref=shift_in.at[me], send_sem=shift_send.at[j],
            recv_sem=shift_recv.at[me], device_id=(partner, row), device_id_type=MESH,
        )

    def win_copy(j):
        partner = lax.rem(me + j, views)
        return pltpu.make_async_remote_copy(
            src_ref=send_win.at[partner], dst_ref=recv_win.at[me, pl.ds(EDGE, rows)],
            send_sem=win_send.at[j], recv_sem=win_recv.at[me],
            device_id=(partner, row), device_id_type=MESH,
        )

    def up_copy(j):
        partner = lax.rem(me + j, views)
        return pltpu.make_async_remote_copy(
            src_ref=send_win.at[partner, pl.ds(0, EDGE)],
            dst_ref=recv_win.at[me, pl.ds(EDGE + rows, EDGE)],
            send_sem=up_send.at[j], recv_sem=up_recv.at[me],
            device_id=(partner, row - 1), device_id_type=MESH,
        )

    def down_copy(j):
        partner = lax.rem(me + j, views)
        return pltpu.make_async_remote_copy(
            src_ref=send_win.at[partner, pl.ds(rows - EDGE, EDGE)],
            dst_ref=recv_win.at[me, pl.ds(0, EDGE)],
            send_sem=down_send.at[j], recv_sem=down_recv.at[me],
            device_id=(partner, row + 1), device_id_type=MESH,
        )

    def layer_copy(up):
        return pltpu.make_async_remote_copy(
            src_ref=halo_out.at[0 if up else 1], dst_ref=halo_in.at[1 if up else 0],
            send_sem=lh_send.at[0 if up else 1], recv_sem=lh_recv.at[1 if up else 0],
            device_id=(me, row - 1 if up else row + 1), device_id_type=MESH,
        )

    def arrived(dst, sem):
        return pltpu.make_async_remote_copy(
            src_ref=dst, dst_ref=dst, send_sem=sem, recv_sem=sem,
            device_id=(me, row), device_id_type=MESH,
        ).wait_recv()

    pl.semaphore_wait(
        barrier, views - 1 + views * (above.astype(jnp.int32) + below.astype(jnp.int32))
    )

    def send_shift(j, carry):
        shift_copy(j).start()
        return carry

    lax.fori_loop(1, views, send_shift, 0)

    @pl.when(above)
    def _():
        layer_copy(True).start()

    @pl.when(below)
    def _():
        layer_copy(False).start()

    def send_all(j, carry):
        @pl.when(j > 0)
        def _():
            win_copy(j).start()

        @pl.when(above)
        def _():
            up_copy(j).start()

        @pl.when(below)
        def _():
            down_copy(j).start()

        return carry

    lax.fori_loop(0, views, send_all, 0)

    @pl.when(jnp.logical_not(above))
    def _():
        recv_win[:, :EDGE, :] = jnp.zeros((views, EDGE, LANES), jnp.bfloat16)
        layer_win[:, :EDGE, :] = jnp.zeros((planes, EDGE, LANES), jnp.float32)

    @pl.when(jnp.logical_not(below))
    def _():
        recv_win[:, EDGE + rows :, :] = jnp.zeros((views, EDGE, LANES), jnp.bfloat16)
        layer_win[:, EDGE + rows :, :] = jnp.zeros((planes, EDGE, LANES), jnp.float32)

    at_row = rows * row - HALO + lax.broadcasted_iota(jnp.int32, (inner, LANES), 0)
    at_col = strip * me - MARGIN + lax.broadcasted_iota(jnp.int32, (inner, LANES), 1)
    inside = (at_row >= 0) & (at_row < rows * rows_of) & (at_col >= 0) & (at_col < cols)
    third_win[...] = jnp.where(inside, 1.0 / frames, 0.0)
    upper[...] = jnp.zeros_like(upper)
    lower[...] = jnp.zeros_like(lower)

    def wait_shift(j, carry):
        source = lax.rem(me + views - j, views)
        arrived(shift_in.at[source], shift_recv.at[source])
        return carry

    lax.fori_loop(1, views, wait_shift, 0)
    to_smem = pltpu.make_async_copy(shift_in, shift_smem, smem_sem)
    to_smem.start()

    @pl.when(above)
    def _():
        arrived(halo_in.at[0], lh_recv.at[0])
        layer_win[:, :EDGE, :] = halo_in[0].astype(jnp.float32)

    @pl.when(below)
    def _():
        arrived(halo_in.at[1], lh_recv.at[1])
        layer_win[:, EDGE + rows :, :] = halo_in[1].astype(jnp.float32)

    to_smem.wait()

    def one_view(j, carry):
        view = lax.rem(me + views - j, views)

        @pl.when(j > 0)
        def _():
            arrived(recv_win.at[view, pl.ds(EDGE, rows)], win_recv.at[view])

        @pl.when(above)
        def _():
            arrived(recv_win.at[view, pl.ds(0, EDGE)], down_recv.at[view])

        @pl.when(below)
        def _():
            arrived(recv_win.at[view, pl.ds(EDGE + rows, EDGE)], up_recv.at[view])

        target_win[...] = recv_win[view].astype(jnp.float32)
        row_shift = [shift_smem[view, 0, 2 * k] for k in range(layer_count)]
        col_shift = [shift_smem[view, 0, 2 * k + 1] for k in range(layer_count)]
        there = [lax.rem(LANES - c, LANES) for c in col_shift]
        back = [lax.rem(LANES + c, LANES) for c in col_shift]

        total = None
        for f in range(frames):
            seen = [
                pltpu.roll(
                    layer_win[f * layer_count + k, pl.ds(EDGE - HALO + row_shift[k], inner), :],
                    there[k], 1,
                )
                for k in range(layer_count)
            ]
            for k in range(layer_count):
                rest = None
                for i in range(layer_count):
                    if i != k:
                        rest = seen[i] if rest is None else rest * seen[i]
                others_win[f * layer_count + k] = rest
                if k == layer_count - 1:
                    whole = rest * seen[k]
                    total = whole if total is None else total + whole
        shown_win[...] = total * third_win[...]

        for k in range(layer_count):
            image = pltpu.roll(target_win[pl.ds(EDGE - row_shift[k], rows), :], back[k], 1)
            model = pltpu.roll(shown_win[pl.ds(HALO - row_shift[k], rows), :], back[k], 1)
            for f in range(frames):
                at = f * layer_count + k
                rest = pltpu.roll(
                    others_win[at, pl.ds(HALO - row_shift[k], rows), :], back[k], 1
                )
                upper[at] += image * rest
                lower[at] += model * rest
        return carry

    lax.fori_loop(0, views, one_view, 0)

    spare = packed.shape[0] - planes * short
    if spare:
        packed[planes * short :, :] = jnp.zeros((spare, LANES), jnp.float32)
    for at in range(planes):
        ratio = (upper[at] + REGULAR) / (lower[at] + REGULAR)
        value = (jnp.log(ratio) - middle) * (1.0 / step)
        merged = pltpu.roll(value[:short], LANES - MARGIN, 1)
        if groups == 2:
            merged = jnp.where(lane < strip, merged, pltpu.roll(value[short:], strip - MARGIN, 1))
        packed[at * short : (at + 1) * short, :] = merged
    slots[me] = jnp.round(packed[...]).astype(jnp.int32).astype(jnp.int16)

    core = lax.rem(me, 2)
    x = lax.rem(me // 2, across)
    z = me // (2 * across)

    def index(zz, xx, cc):
        return (zz * across + xx) * 2 + cc

    def slot_copy(slot, to, sem):
        return pltpu.make_async_remote_copy(
            src_ref=slots.at[slot], dst_ref=slots.at[slot], send_sem=sem,
            recv_sem=slot_recv.at[slot], device_id=(to, row), device_id_type=MESH,
        )

    def to_column(dz):
        return slot_copy(me, index(lax.rem(z + dz, depth), x, core), col_send.at[dz])

    def to_across(dz, dx):
        slot = index(lax.rem(z + depth - dz, depth), x, core)
        return slot_copy(slot, index(z, lax.rem(x + dx, across), core), x_send.at[dz, dx])

    def to_core(dz, dx):
        slot = index(lax.rem(z + depth - dz, depth), lax.rem(x + across - dx, across), core)
        return slot_copy(slot, index(z, x, 1 - core), core_send.at[dz, dx])

    for dz in range(1, depth):
        to_column(dz).start()
    for dx in range(1, across):
        to_across(0, dx).start()
    to_core(0, 0).start()
    for dz in range(1, depth):
        slot = index(lax.rem(z + depth - dz, depth), x, core)
        arrived(slots.at[slot], slot_recv.at[slot])
        for dx in range(1, across):
            to_across(dz, dx).start()
        to_core(dz, 0).start()
    for dz in range(depth):
        for dx in range(1, across):
            slot = index(lax.rem(z + depth - dz, depth), lax.rem(x + across - dx, across), core)
            arrived(slots.at[slot], slot_recv.at[slot])
            to_core(dz, dx).start()

    def wait_twin(n, carry):
        slot = 2 * n + 1 - core
        arrived(slots.at[slot], slot_recv.at[slot])
        return carry

    lax.fori_loop(0, views // 2, wait_twin, 0)

    per_tile = LANES // strip

    def unpack(tile, carry):
        where = pl.ds(pl.multiple_of(tile * LANES, LANES), LANES)
        parts = []
        for i in range(per_tile):
            code = slots[tile * per_tile + i].astype(jnp.int32).astype(jnp.float32)
            parts.append(jnp.exp(code * step + middle))
        for f in range(frames):
            for k in range(layer_count):
                at = f * layer_count + k
                for g in range(groups):
                    ratio = None
                    for i in range(per_tile):
                        part = parts[i][at * short : (at + 1) * short]
                        turn = (strip * (i - g)) % LANES
                        if turn:
                            part = pltpu.roll(part, turn, 1)
                        ratio = part if ratio is None else jnp.where(lane < strip * i, ratio, part)
                    span = slice(g * short, (g + 1) * short)
                    out_ref[f, k, span, where] = (
                        layers_ref[f, k, span, where].astype(jnp.float32) * ratio
                    )
        return carry

    lax.fori_loop(0, tiles, unpack, 0)

    for dz in range(1, depth):
        to_column(dz).wait_send()
    for dz in range(depth):
        for dx in range(across):
            if dx:
                to_across(dz, dx).wait_send()
            to_core(dz, dx).wait_send()

    @pl.when(above)
    def _():
        layer_copy(True).wait_send()

    @pl.when(below)
    def _():
        layer_copy(False).wait_send()

    def finish(j, carry):
        @pl.when(j > 0)
        def _():
            shift_copy(j).wait_send()
            win_copy(j).wait_send()

        @pl.when(above)
        def _():
            up_copy(j).wait_send()

        @pl.when(below)
        def _():
            down_copy(j).wait_send()

        return carry

    lax.fori_loop(0, views, finish, 0)


def body(views, rows_of, layers, target, shifts):
    frames, layer_count, rows, cols = layers.shape
    planes = frames * layer_count
    strip = cols // views
    groups = 2 if strip == 64 else 1
    depth, across = split_views(views)
    packed_rows = -(-planes * (rows // groups) // 16) * 16
    height, inner = rows + 2 * EDGE, rows + 2 * HALO
    dma = pltpu.SemaphoreType.DMA
    f32, bf16 = jnp.float32, jnp.bfloat16
    return pl.pallas_call(
        functools.partial(kernel, views, rows_of),
        out_shape=jax.ShapeDtypeStruct(layers.shape, f32),
        in_specs=[
            pl.BlockSpec(memory_space=pltpu.SMEM),
            pl.BlockSpec(memory_space=pltpu.VMEM),
            pl.BlockSpec(memory_space=pltpu.VMEM),
        ],
        out_specs=pl.BlockSpec(memory_space=pltpu.VMEM),
        scratch_shapes=[
            pltpu.VMEM((views, rows, LANES), bf16),
            pltpu.VMEM((views, height, LANES), bf16),
            pltpu.VMEM((8, LANES), jnp.int32),
            pltpu.VMEM((views, 8, LANES), jnp.int32),
            pltpu.SMEM((views, 8, LANES), jnp.int32),
            pltpu.VMEM((2, planes, EDGE, LANES), bf16),
            pltpu.VMEM((2, planes, EDGE, LANES), bf16),
            pltpu.VMEM((planes, height, LANES), f32),
            pltpu.VMEM((height, LANES), f32),
            pltpu.VMEM((planes, inner, LANES), f32),
            pltpu.VMEM((inner, LANES), f32),
            pltpu.VMEM((inner, LANES), f32),
            pltpu.VMEM((planes, rows, LANES), f32),
            pltpu.VMEM((planes, rows, LANES), f32),
            pltpu.VMEM((packed_rows, LANES), f32),
            pltpu.VMEM((views, packed_rows, LANES), jnp.int16),
            dma((views,)), dma((views,)), dma((views,)), dma((views,)), dma((views,)), dma((views,)),
            dma((views,)), dma((views,)), dma, dma((2,)), dma((2,)),
            dma((depth,)), dma((depth, across)), dma((depth, across)), dma((views,)),
        ],
        compiler_params=pltpu.CompilerParams(
            collective_id=0, has_side_effects=True, vmem_limit_bytes=40 * 1024 * 1024
        ),
        name="light_field_update",
    )(shifts, layers, target)


def solution(mesh):
    placed = (P(None, None, "row", None), P("view", "row", None), P("view", None, None))
    return jax.shard_map(
        functools.partial(body, mesh.shape["view"], mesh.shape["row"]),
        mesh=mesh, in_specs=placed, out_specs=P(None, None, "row", None), check_vma=False,
    )
```

```python
import functools
import math

import jax
import jax.numpy as jnp
from jax import lax
from jax.experimental import pallas as pl
from jax.experimental.pallas import tpu as pltpu
from jax.sharding import PartitionSpec as P

HALO = 8
LANES = 128
EDGE = 16
MARGIN = 32
REGULAR = 0.05
MESH = pl.DeviceIdType.MESH


def split_views(views):
    across = 1
    while (2 * across) ** 2 * 2 <= views:
        across *= 2
    return views // (2 * across), across


def code_range(views):
    low = math.log(REGULAR / (views + REGULAR))
    high = math.log((0.5 * views + REGULAR) / REGULAR)
    return 0.5 * (low + high), (high - low) / 65000.0


def kernel(
    views, rows_of, shifts_hbm, layers_hbm, target_hbm, out_ref,
    shifts_ref, layers_ref, target_ref, fetch_sem,
    send_win, recv_win, shift_out, shift_in, shift_smem, halo_out, halo_in,
    layer_win, target_win, others_win, shown_win, third_win, upper, lower, packed, slots,
    win_send, win_recv, up_send, up_recv, down_send, down_recv,
    shift_send, shift_recv, smem_sem, lh_send, lh_recv,
    col_send, x_send, core_send, slot_recv,
):
    fetch_shifts = pltpu.make_async_copy(shifts_hbm, shifts_ref, fetch_sem.at[0])
    fetch_target = pltpu.make_async_copy(target_hbm, target_ref, fetch_sem.at[1])
    fetch_layers = pltpu.make_async_copy(layers_hbm, layers_ref, fetch_sem.at[2])
    fetch_shifts.start()
    fetch_target.start()
    fetch_layers.start()

    frames, layer_count, rows, cols = layers_ref.shape
    strip = cols // views
    planes = frames * layer_count
    height = rows + 2 * EDGE
    inner = rows + 2 * HALO
    depth, across = split_views(views)
    groups = 2 if strip == 64 else 1
    short = rows // groups
    tiles = cols // LANES
    middle, step = code_range(views)

    me = lax.axis_index("view")
    row = lax.axis_index("row")
    above, below = row > 0, row < rows_of - 1

    barrier = pltpu.get_barrier_semaphore()

    def greet(j, carry):
        partner = lax.rem(me + j, views)

        @pl.when(j > 0)
        def _():
            pl.semaphore_signal(barrier, inc=1, device_id=(partner, row), device_id_type=MESH)

        @pl.when(above)
        def _():
            pl.semaphore_signal(barrier, inc=1, device_id=(partner, row - 1), device_id_type=MESH)

        @pl.when(below)
        def _():
            pl.semaphore_signal(barrier, inc=1, device_id=(partner, row + 1), device_id_type=MESH)

        return carry

    lax.fori_loop(0, views, greet, 0)

    lane = lax.broadcasted_iota(jnp.int32, (1, LANES), 1)

    def window(load, index):
        start = strip * index - MARGIN
        tile = (start + LANES) // LANES - 1
        offset = start - tile * LANES
        first = load(jnp.maximum(tile, 0))
        second = load(jnp.minimum(tile + 1, tiles - 1))
        turn = lax.rem(LANES - offset, LANES)
        first = pltpu.roll(first, turn, 1)
        second = pltpu.roll(second, turn, 1)
        both = jnp.where(lane < LANES - offset, first, second)
        col = start + lane
        return jnp.where((col >= 0) & (col < cols), both, 0.0)

    fetch_shifts.wait()
    place = lax.broadcasted_iota(jnp.int32, (8, LANES), 1)
    block = jnp.zeros((8, LANES), jnp.int32)
    for k in range(layer_count):
        for axis in range(2):
            block = jnp.where(place == 2 * k + axis, shifts_ref[0, axis, k], block)
    shift_out[...] = block
    shift_in[me] = block

    fetch_target.wait()

    def fill(c, carry):
        def load(tile):
            where = pl.ds(pl.multiple_of(tile * LANES, LANES), LANES)
            return target_ref[0, :, where].astype(jnp.float32)

        send_win[c] = window(load, c).astype(jnp.bfloat16)
        return carry

    lax.fori_loop(0, views, fill, 0)
    recv_win[me, EDGE : EDGE + rows, :] = send_win[me]

    fetch_layers.wait()
    for f in range(frames):
        for k in range(layer_count):
            def load(tile):
                where = pl.ds(pl.multiple_of(tile * LANES, LANES), LANES)
                return layers_ref[f, k, :, where].astype(jnp.float32)

            plane = window(load, me)
            at = f * layer_count + k
            layer_win[at, EDGE : EDGE + rows, :] = plane
            halo_out[0, at] = plane[:EDGE].astype(jnp.bfloat16)
            halo_out[1, at] = plane[rows - EDGE :].astype(jnp.bfloat16)

    def shift_copy(j):
        partner = lax.rem(me + j, views)
        return pltpu.make_async_remote_copy(
            src_ref=shift_out, dst_ref=shift_in.at[me], send_sem=shift_send.at[j],
            recv_sem=shift_recv.at[me], device_id=(partner, row), device_id_type=MESH,
        )

    def win_copy(j):
        partner = lax.rem(me + j, views)
        return pltpu.make_async_remote_copy(
            src_ref=send_win.at[partner], dst_ref=recv_win.at[me, pl.ds(EDGE, rows)],
            send_sem=win_send.at[j], recv_sem=win_recv.at[me],
            device_id=(partner, row), device_id_type=MESH,
        )

    def up_copy(j):
        partner = lax.rem(me + j, views)
        return pltpu.make_async_remote_copy(
            src_ref=send_win.at[partner, pl.ds(0, EDGE)],
            dst_ref=recv_win.at[me, pl.ds(EDGE + rows, EDGE)],
            send_sem=up_send.at[j], recv_sem=up_recv.at[me],
            device_id=(partner, row - 1), device_id_type=MESH,
        )

    def down_copy(j):
        partner = lax.rem(me + j, views)
        return pltpu.make_async_remote_copy(
            src_ref=send_win.at[partner, pl.ds(rows - EDGE, EDGE)],
            dst_ref=recv_win.at[me, pl.ds(0, EDGE)],
            send_sem=down_send.at[j], recv_sem=down_recv.at[me],
            device_id=(partner, row + 1), device_id_type=MESH,
        )

    def layer_copy(up):
        return pltpu.make_async_remote_copy(
            src_ref=halo_out.at[0 if up else 1], dst_ref=halo_in.at[1 if up else 0],
            send_sem=lh_send.at[0 if up else 1], recv_sem=lh_recv.at[1 if up else 0],
            device_id=(me, row - 1 if up else row + 1), device_id_type=MESH,
        )

    def arrived(dst, sem):
        return pltpu.make_async_remote_copy(
            src_ref=dst, dst_ref=dst, send_sem=sem, recv_sem=sem,
            device_id=(me, row), device_id_type=MESH,
        ).wait_recv()

    pl.semaphore_wait(
        barrier, views - 1 + views * (above.astype(jnp.int32) + below.astype(jnp.int32))
    )

    def send_shift(j, carry):
        shift_copy(j).start()
        return carry

    lax.fori_loop(1, views, send_shift, 0)

    @pl.when(above)
    def _():
        layer_copy(True).start()

    @pl.when(below)
    def _():
        layer_copy(False).start()

    def send_all(j, carry):
        @pl.when(j > 0)
        def _():
            win_copy(j).start()

        @pl.when(above)
        def _():
            up_copy(j).start()

        @pl.when(below)
        def _():
            down_copy(j).start()

        return carry

    lax.fori_loop(0, views, send_all, 0)

    @pl.when(jnp.logical_not(above))
    def _():
        recv_win[:, :EDGE, :] = jnp.zeros((views, EDGE, LANES), jnp.bfloat16)
        layer_win[:, :EDGE, :] = jnp.zeros((planes, EDGE, LANES), jnp.float32)

    @pl.when(jnp.logical_not(below))
    def _():
        recv_win[:, EDGE + rows :, :] = jnp.zeros((views, EDGE, LANES), jnp.bfloat16)
        layer_win[:, EDGE + rows :, :] = jnp.zeros((planes, EDGE, LANES), jnp.float32)

    at_row = rows * row - HALO + lax.broadcasted_iota(jnp.int32, (inner, LANES), 0)
    at_col = strip * me - MARGIN + lax.broadcasted_iota(jnp.int32, (inner, LANES), 1)
    inside = (at_row >= 0) & (at_row < rows * rows_of) & (at_col >= 0) & (at_col < cols)
    third_win[...] = jnp.where(inside, 1.0 / frames, 0.0)
    upper[...] = jnp.zeros_like(upper)
    lower[...] = jnp.zeros_like(lower)

    def wait_shift(j, carry):
        source = lax.rem(me + views - j, views)
        arrived(shift_in.at[source], shift_recv.at[source])
        return carry

    lax.fori_loop(1, views, wait_shift, 0)
    to_smem = pltpu.make_async_copy(shift_in, shift_smem, smem_sem)
    to_smem.start()

    @pl.when(above)
    def _():
        arrived(halo_in.at[0], lh_recv.at[0])
        layer_win[:, :EDGE, :] = halo_in[0].astype(jnp.float32)

    @pl.when(below)
    def _():
        arrived(halo_in.at[1], lh_recv.at[1])
        layer_win[:, EDGE + rows :, :] = halo_in[1].astype(jnp.float32)

    to_smem.wait()

    def one_view(j, carry):
        view = lax.rem(me + views - j, views)

        @pl.when(j > 0)
        def _():
            arrived(recv_win.at[view, pl.ds(EDGE, rows)], win_recv.at[view])

        @pl.when(above)
        def _():
            arrived(recv_win.at[view, pl.ds(0, EDGE)], down_recv.at[view])

        @pl.when(below)
        def _():
            arrived(recv_win.at[view, pl.ds(EDGE + rows, EDGE)], up_recv.at[view])

        target_win[...] = recv_win[view].astype(jnp.float32)
        row_shift = [shift_smem[view, 0, 2 * k] for k in range(layer_count)]
        col_shift = [shift_smem[view, 0, 2 * k + 1] for k in range(layer_count)]
        there = [lax.rem(LANES - c, LANES) for c in col_shift]
        back = [lax.rem(LANES + c, LANES) for c in col_shift]

        total = None
        for f in range(frames):
            seen = [
                pltpu.roll(
                    layer_win[f * layer_count + k, pl.ds(EDGE - HALO + row_shift[k], inner), :],
                    there[k], 1,
                )
                for k in range(layer_count)
            ]
            for k in range(layer_count):
                rest = None
                for i in range(layer_count):
                    if i != k:
                        rest = seen[i] if rest is None else rest * seen[i]
                others_win[f * layer_count + k] = rest
                if k == layer_count - 1:
                    whole = rest * seen[k]
                    total = whole if total is None else total + whole
        shown_win[...] = total * third_win[...]

        for k in range(layer_count):
            image = pltpu.roll(target_win[pl.ds(EDGE - row_shift[k], rows), :], back[k], 1)
            model = pltpu.roll(shown_win[pl.ds(HALO - row_shift[k], rows), :], back[k], 1)
            for f in range(frames):
                at = f * layer_count + k
                rest = pltpu.roll(
                    others_win[at, pl.ds(HALO - row_shift[k], rows), :], back[k], 1
                )
                upper[at] += image * rest
                lower[at] += model * rest
        return carry

    lax.fori_loop(0, views, one_view, 0)

    spare = packed.shape[0] - planes * short
    if spare:
        packed[planes * short :, :] = jnp.zeros((spare, LANES), jnp.float32)
    for at in range(planes):
        ratio = (upper[at] + REGULAR) / (lower[at] + REGULAR)
        value = (jnp.log(ratio) - middle) * (1.0 / step)
        merged = pltpu.roll(value[:short], LANES - MARGIN, 1)
        if groups == 2:
            merged = jnp.where(lane < strip, merged, pltpu.roll(value[short:], strip - MARGIN, 1))
        packed[at * short : (at + 1) * short, :] = merged
    slots[me] = jnp.round(packed[...]).astype(jnp.int32).astype(jnp.int16)

    core = lax.rem(me, 2)
    x = lax.rem(me // 2, across)
    z = me // (2 * across)

    def index(zz, xx, cc):
        return (zz * across + xx) * 2 + cc

    def slot_copy(slot, to, sem):
        return pltpu.make_async_remote_copy(
            src_ref=slots.at[slot], dst_ref=slots.at[slot], send_sem=sem,
            recv_sem=slot_recv.at[slot], device_id=(to, row), device_id_type=MESH,
        )

    def along(d):
        return index(z + d, x, core)

    def to_next(d, way):
        return slot_copy(along(d), index(z + way, x, core), col_send.at[depth + d, (way + 1) // 2])

    def to_across(d, dx):
        return slot_copy(
            along(d), index(z, lax.rem(x + dx, across), core), x_send.at[depth + d, dx]
        )

    def to_core(d, dx):
        slot = index(z + d, lax.rem(x + across - dx, across), core)
        return slot_copy(slot, index(z, x, 1 - core), core_send.at[depth + d, dx])

    def exists(d):
        return (z + d >= 0) & (z + d < depth)

    def outward(d):
        return [d // abs(d) * -1] if d else [-1, 1]

    def visit(d, act):
        if d:
            pl.when(exists(d))(act)
        else:
            act()

    def both_ways(d):
        return (-d, d) if d else (0,)

    def each_copy(d, act):
        for way in outward(d):
            pl.when(exists(way))(lambda: act(to_next(d, way)))
        for dx in range(1, across):
            act(to_across(d, dx))
        act(to_core(d, 0))

    def column_step(d):
        def act():
            if d:
                slot = along(d)
                arrived(slots.at[slot], slot_recv.at[slot])
            each_copy(d, lambda copy: copy.start())

        visit(d, act)

    def across_step(d):
        def act():
            for dx in range(1, across):
                slot = index(z + d, lax.rem(x + across - dx, across), core)
                arrived(slots.at[slot], slot_recv.at[slot])
                to_core(d, dx).start()

        visit(d, act)

    column_step(0)
    for distance in range(1, depth):
        for d in both_ways(distance):
            column_step(d)
        for d in both_ways(distance - 1):
            across_step(d)

    per_tile = LANES // strip

    def unpack(tile):
        for i in range(per_tile):
            @pl.when(lax.rem(tile * per_tile + i, 2) != core)
            def _():
                slot = tile * per_tile + i
                arrived(slots.at[slot], slot_recv.at[slot])

        where = pl.ds(pl.multiple_of(tile * LANES, LANES), LANES)
        parts = []
        for i in range(per_tile):
            code = slots[tile * per_tile + i].astype(jnp.int32).astype(jnp.float32)
            parts.append(jnp.exp(code * step + middle))
        for f in range(frames):
            for k in range(layer_count):
                at = f * layer_count + k
                for g in range(groups):
                    ratio = None
                    for i in range(per_tile):
                        part = parts[i][at * short : (at + 1) * short]
                        turn = (strip * (i - g)) % LANES
                        if turn:
                            part = pltpu.roll(part, turn, 1)
                        ratio = part if ratio is None else jnp.where(lane < strip * i, ratio, part)
                    span = slice(g * short, (g + 1) * short)
                    out_ref[f, k, span, where] = (
                        layers_ref[f, k, span, where].astype(jnp.float32) * ratio
                    )

    early = strip == 64

    def unpack_column(n, carry):
        unpack(n * across + x)
        return carry

    if early:
        lax.fori_loop(0, depth, unpack_column, 0)
    for d in both_ways(depth - 1):
        across_step(d)

    def unpack_rest(n, carry):
        zz, dx = n // (across - 1), lax.rem(n, across - 1) + 1
        unpack(zz * across + lax.rem(x + dx, across))
        return carry

    def unpack_any(n, carry):
        unpack(n)
        return carry

    if early:
        lax.fori_loop(0, depth * (across - 1), unpack_rest, 0)
    else:
        lax.fori_loop(0, tiles, unpack_any, 0)

    for distance in range(depth):
        for d in both_ways(distance):
            def act():
                each_copy(d, lambda copy: copy.wait_send())
                for dx in range(1, across):
                    to_core(d, dx).wait_send()

            visit(d, act)

    @pl.when(above)
    def _():
        layer_copy(True).wait_send()

    @pl.when(below)
    def _():
        layer_copy(False).wait_send()

    def finish(j, carry):
        @pl.when(j > 0)
        def _():
            shift_copy(j).wait_send()
            win_copy(j).wait_send()

        @pl.when(above)
        def _():
            up_copy(j).wait_send()

        @pl.when(below)
        def _():
            down_copy(j).wait_send()

        return carry

    lax.fori_loop(0, views, finish, 0)


def body(views, rows_of, layers, target, shifts):
    frames, layer_count, rows, cols = layers.shape
    planes = frames * layer_count
    strip = cols // views
    groups = 2 if strip == 64 else 1
    depth, across = split_views(views)
    packed_rows = -(-planes * (rows // groups) // 16) * 16
    height, inner = rows + 2 * EDGE, rows + 2 * HALO
    dma = pltpu.SemaphoreType.DMA
    f32, bf16 = jnp.float32, jnp.bfloat16
    return pl.pallas_call(
        functools.partial(kernel, views, rows_of),
        out_shape=jax.ShapeDtypeStruct(layers.shape, f32),
        in_specs=[
            pl.BlockSpec(memory_space=pl.ANY),
            pl.BlockSpec(memory_space=pl.ANY),
            pl.BlockSpec(memory_space=pl.ANY),
        ],
        out_specs=pl.BlockSpec(memory_space=pltpu.VMEM),
        scratch_shapes=[
            pltpu.SMEM((1, 2, layer_count), jnp.int32),
            pltpu.VMEM(layers.shape, bf16),
            pltpu.VMEM(target.shape, bf16),
            dma((3,)),
            pltpu.VMEM((views, rows, LANES), bf16),
            pltpu.VMEM((views, height, LANES), bf16),
            pltpu.VMEM((8, LANES), jnp.int32),
            pltpu.VMEM((views, 8, LANES), jnp.int32),
            pltpu.SMEM((views, 8, LANES), jnp.int32),
            pltpu.VMEM((2, planes, EDGE, LANES), bf16),
            pltpu.VMEM((2, planes, EDGE, LANES), bf16),
            pltpu.VMEM((planes, height, LANES), f32),
            pltpu.VMEM((height, LANES), f32),
            pltpu.VMEM((planes, inner, LANES), f32),
            pltpu.VMEM((inner, LANES), f32),
            pltpu.VMEM((inner, LANES), f32),
            pltpu.VMEM((planes, rows, LANES), f32),
            pltpu.VMEM((planes, rows, LANES), f32),
            pltpu.VMEM((packed_rows, LANES), f32),
            pltpu.VMEM((views, packed_rows, LANES), jnp.int16),
            dma((views,)), dma((views,)), dma((views,)), dma((views,)), dma((views,)), dma((views,)),
            dma((views,)), dma((views,)), dma, dma((2,)), dma((2,)),
            dma((2 * depth, 2)), dma((2 * depth, across)), dma((2 * depth, across)), dma((views,)),
        ],
        compiler_params=pltpu.CompilerParams(
            collective_id=0, has_side_effects=True, vmem_limit_bytes=40 * 1024 * 1024
        ),
        name="light_field_update",
    )(jnp.swapaxes(shifts, 1, 2), layers, target)


def solution(mesh):
    placed = (P(None, None, "row", None), P("view", "row", None), P("view", None, None))
    return jax.shard_map(
        functools.partial(body, mesh.shape["view"], mesh.shape["row"]),
        mesh=mesh, in_specs=placed, out_specs=P(None, None, "row", None), check_vma=False,
    )
```

```python
import functools
import math

import jax
import jax.numpy as jnp
from jax import lax
from jax.experimental import pallas as pl
from jax.experimental.pallas import tpu as pltpu
from jax.sharding import PartitionSpec as P

HALO = 8
LANES = 128
EDGE = 16
MARGIN = 32
REGULAR = 0.05
MESH = pl.DeviceIdType.MESH


def split_views(views):
    across = 1
    while (2 * across) ** 2 * 2 <= views:
        across *= 2
    return views // (2 * across), across


def code_range(views):
    low = math.log(REGULAR / (views + REGULAR))
    high = math.log((0.5 * views + REGULAR) / REGULAR)
    return 0.5 * (low + high), (high - low) / 65000.0


def kernel(
    views, rows_of, shifts_hbm, layers_hbm, target_hbm, out_hbm,
    shifts_ref, layers_ref, target_ref, out_ref, fetch_sem, store_sem,
    send_win, recv_win, shift_out, shift_in, shift_smem, halo_out, halo_in,
    layer_win, target_win, others_win, shown_win, third_win, upper, lower, packed, slots,
    win_send, win_recv, up_send, up_recv, down_send, down_recv,
    shift_send, shift_recv, smem_sem, lh_send, lh_recv,
    col_send, x_send, core_send, slot_recv,
):
    fetch_shifts = pltpu.make_async_copy(shifts_hbm, shifts_ref, fetch_sem.at[0])
    fetch_target = pltpu.make_async_copy(target_hbm, target_ref, fetch_sem.at[1])
    fetch_layers = pltpu.make_async_copy(layers_hbm, layers_ref, fetch_sem.at[2])
    fetch_shifts.start()
    fetch_target.start()
    fetch_layers.start()

    frames, layer_count, rows, cols = layers_ref.shape
    strip = cols // views
    planes = frames * layer_count
    height = rows + 2 * EDGE
    inner = rows + 2 * HALO
    depth, across = split_views(views)
    groups = 2 if strip == 64 else 1
    short = rows // groups
    tiles = cols // LANES
    middle, step = code_range(views)

    me = lax.axis_index("view")
    row = lax.axis_index("row")
    above, below = row > 0, row < rows_of - 1

    barrier = pltpu.get_barrier_semaphore()

    def greet(j, carry):
        partner = lax.rem(me + j, views)

        @pl.when(j > 0)
        def _():
            pl.semaphore_signal(barrier, inc=1, device_id=(partner, row), device_id_type=MESH)

        @pl.when(above)
        def _():
            pl.semaphore_signal(barrier, inc=1, device_id=(partner, row - 1), device_id_type=MESH)

        @pl.when(below)
        def _():
            pl.semaphore_signal(barrier, inc=1, device_id=(partner, row + 1), device_id_type=MESH)

        return carry

    lax.fori_loop(0, views, greet, 0)

    lane = lax.broadcasted_iota(jnp.int32, (1, LANES), 1)

    def window(load, index):
        start = strip * index - MARGIN
        tile = (start + LANES) // LANES - 1
        offset = start - tile * LANES
        first = load(jnp.maximum(tile, 0))
        second = load(jnp.minimum(tile + 1, tiles - 1))
        turn = lax.rem(LANES - offset, LANES)
        first = pltpu.roll(first, turn, 1)
        second = pltpu.roll(second, turn, 1)
        both = jnp.where(lane < LANES - offset, first, second)
        col = start + lane
        return jnp.where((col >= 0) & (col < cols), both, 0.0)

    fetch_shifts.wait()
    place = lax.broadcasted_iota(jnp.int32, (8, LANES), 1)
    block = jnp.zeros((8, LANES), jnp.int32)
    for k in range(layer_count):
        for axis in range(2):
            block = jnp.where(place == 2 * k + axis, shifts_ref[0, axis, k], block)
    shift_out[...] = block
    shift_in[me] = block

    fetch_target.wait()

    def fill(c, carry):
        def load(tile):
            where = pl.ds(pl.multiple_of(tile * LANES, LANES), LANES)
            return target_ref[0, :, where].astype(jnp.float32)

        send_win[c] = window(load, c).astype(jnp.bfloat16)
        return carry

    lax.fori_loop(0, views, fill, 0, unroll=4)
    recv_win[me, EDGE : EDGE + rows, :] = send_win[me]

    fetch_layers.wait()
    for f in range(frames):
        for k in range(layer_count):
            def load(tile):
                where = pl.ds(pl.multiple_of(tile * LANES, LANES), LANES)
                return layers_ref[f, k, :, where].astype(jnp.float32)

            plane = window(load, me)
            at = f * layer_count + k
            layer_win[at, EDGE : EDGE + rows, :] = plane
            halo_out[0, at] = plane[:EDGE].astype(jnp.bfloat16)
            halo_out[1, at] = plane[rows - EDGE :].astype(jnp.bfloat16)

    def shift_copy(j):
        partner = lax.rem(me + j, views)
        return pltpu.make_async_remote_copy(
            src_ref=shift_out, dst_ref=shift_in.at[me], send_sem=shift_send.at[j],
            recv_sem=shift_recv.at[me], device_id=(partner, row), device_id_type=MESH,
        )

    def win_copy(j):
        partner = lax.rem(me + j, views)
        return pltpu.make_async_remote_copy(
            src_ref=send_win.at[partner], dst_ref=recv_win.at[me, pl.ds(EDGE, rows)],
            send_sem=win_send.at[j], recv_sem=win_recv.at[me],
            device_id=(partner, row), device_id_type=MESH,
        )

    def up_copy(j):
        partner = lax.rem(me + j, views)
        return pltpu.make_async_remote_copy(
            src_ref=send_win.at[partner, pl.ds(0, EDGE)],
            dst_ref=recv_win.at[me, pl.ds(EDGE + rows, EDGE)],
            send_sem=up_send.at[j], recv_sem=up_recv.at[me],
            device_id=(partner, row - 1), device_id_type=MESH,
        )

    def down_copy(j):
        partner = lax.rem(me + j, views)
        return pltpu.make_async_remote_copy(
            src_ref=send_win.at[partner, pl.ds(rows - EDGE, EDGE)],
            dst_ref=recv_win.at[me, pl.ds(0, EDGE)],
            send_sem=down_send.at[j], recv_sem=down_recv.at[me],
            device_id=(partner, row + 1), device_id_type=MESH,
        )

    def layer_copy(up):
        return pltpu.make_async_remote_copy(
            src_ref=halo_out.at[0 if up else 1], dst_ref=halo_in.at[1 if up else 0],
            send_sem=lh_send.at[0 if up else 1], recv_sem=lh_recv.at[1 if up else 0],
            device_id=(me, row - 1 if up else row + 1), device_id_type=MESH,
        )

    def arrived(dst, sem):
        return pltpu.make_async_remote_copy(
            src_ref=dst, dst_ref=dst, send_sem=sem, recv_sem=sem,
            device_id=(me, row), device_id_type=MESH,
        ).wait_recv()

    pl.semaphore_wait(
        barrier, views - 1 + views * (above.astype(jnp.int32) + below.astype(jnp.int32))
    )

    def send_shift(j, carry):
        shift_copy(j).start()
        return carry

    lax.fori_loop(1, views, send_shift, 0)

    @pl.when(above)
    def _():
        layer_copy(True).start()

    @pl.when(below)
    def _():
        layer_copy(False).start()

    def send_all(j, carry):
        @pl.when(j > 0)
        def _():
            win_copy(j).start()

        @pl.when(above)
        def _():
            up_copy(j).start()

        @pl.when(below)
        def _():
            down_copy(j).start()

        return carry

    lax.fori_loop(0, views, send_all, 0)

    @pl.when(jnp.logical_not(above))
    def _():
        recv_win[:, :EDGE, :] = jnp.zeros((views, EDGE, LANES), jnp.bfloat16)
        layer_win[:, :EDGE, :] = jnp.zeros((planes, EDGE, LANES), jnp.float32)

    @pl.when(jnp.logical_not(below))
    def _():
        recv_win[:, EDGE + rows :, :] = jnp.zeros((views, EDGE, LANES), jnp.bfloat16)
        layer_win[:, EDGE + rows :, :] = jnp.zeros((planes, EDGE, LANES), jnp.float32)

    at_row = rows * row - HALO + lax.broadcasted_iota(jnp.int32, (inner, LANES), 0)
    at_col = strip * me - MARGIN + lax.broadcasted_iota(jnp.int32, (inner, LANES), 1)
    inside = (at_row >= 0) & (at_row < rows * rows_of) & (at_col >= 0) & (at_col < cols)
    third_win[...] = jnp.where(inside, 1.0 / frames, 0.0)
    upper[...] = jnp.zeros_like(upper)
    lower[...] = jnp.zeros_like(lower)

    def wait_shift(j, carry):
        source = lax.rem(me + views - j, views)
        arrived(shift_in.at[source], shift_recv.at[source])
        return carry

    lax.fori_loop(1, views, wait_shift, 0)
    to_smem = pltpu.make_async_copy(shift_in, shift_smem, smem_sem)
    to_smem.start()

    @pl.when(above)
    def _():
        arrived(halo_in.at[0], lh_recv.at[0])
        layer_win[:, :EDGE, :] = halo_in[0].astype(jnp.float32)

    @pl.when(below)
    def _():
        arrived(halo_in.at[1], lh_recv.at[1])
        layer_win[:, EDGE + rows :, :] = halo_in[1].astype(jnp.float32)

    to_smem.wait()

    def one_view(j, carry):
        view = lax.rem(me + views - j, views)

        @pl.when(j > 0)
        def _():
            arrived(recv_win.at[view, pl.ds(EDGE, rows)], win_recv.at[view])

        @pl.when(above)
        def _():
            arrived(recv_win.at[view, pl.ds(0, EDGE)], down_recv.at[view])

        @pl.when(below)
        def _():
            arrived(recv_win.at[view, pl.ds(EDGE + rows, EDGE)], up_recv.at[view])

        target_win[...] = recv_win[view].astype(jnp.float32)
        row_shift = [shift_smem[view, 0, 2 * k] for k in range(layer_count)]
        col_shift = [shift_smem[view, 0, 2 * k + 1] for k in range(layer_count)]
        there = [lax.rem(LANES - c, LANES) for c in col_shift]
        back = [lax.rem(LANES + c, LANES) for c in col_shift]

        total = None
        for f in range(frames):
            seen = [
                pltpu.roll(
                    layer_win[f * layer_count + k, pl.ds(EDGE - HALO + row_shift[k], inner), :],
                    there[k], 1,
                )
                for k in range(layer_count)
            ]
            for k in range(layer_count):
                rest = None
                for i in range(layer_count):
                    if i != k:
                        rest = seen[i] if rest is None else rest * seen[i]
                others_win[f * layer_count + k] = rest
                if k == layer_count - 1:
                    whole = rest * seen[k]
                    total = whole if total is None else total + whole
        shown_win[...] = total * third_win[...]

        for k in range(layer_count):
            image = pltpu.roll(target_win[pl.ds(EDGE - row_shift[k], rows), :], back[k], 1)
            model = pltpu.roll(shown_win[pl.ds(HALO - row_shift[k], rows), :], back[k], 1)
            for f in range(frames):
                at = f * layer_count + k
                rest = pltpu.roll(
                    others_win[at, pl.ds(HALO - row_shift[k], rows), :], back[k], 1
                )
                upper[at] += image * rest
                lower[at] += model * rest
        return carry

    lax.fori_loop(0, views, one_view, 0)

    spare = packed.shape[0] - planes * short
    if spare:
        packed[planes * short :, :] = jnp.zeros((spare, LANES), jnp.float32)
    for at in range(planes):
        ratio = (upper[at] + REGULAR) / (lower[at] + REGULAR)
        value = (jnp.log(ratio) - middle) * (1.0 / step)
        merged = pltpu.roll(value[:short], LANES - MARGIN, 1)
        if groups == 2:
            merged = jnp.where(lane < strip, merged, pltpu.roll(value[short:], strip - MARGIN, 1))
        packed[at * short : (at + 1) * short, :] = merged
    slots[me] = jnp.round(packed[...]).astype(jnp.int32).astype(jnp.int16)

    core = lax.rem(me, 2)
    x = lax.rem(me // 2, across)
    z = me // (2 * across)

    def index(zz, xx, cc):
        return (zz * across + xx) * 2 + cc

    def slot_copy(slot, to, sem):
        return pltpu.make_async_remote_copy(
            src_ref=slots.at[slot], dst_ref=slots.at[slot], send_sem=sem,
            recv_sem=slot_recv.at[slot], device_id=(to, row), device_id_type=MESH,
        )

    def along(d):
        return index(z + d, x, core)

    def to_column(d):
        return slot_copy(me, index(z + d, x, core), col_send.at[depth + d])

    def to_across(d, dx):
        return slot_copy(
            along(d), index(z, lax.rem(x + dx, across), core), x_send.at[depth + d, dx]
        )

    def to_core(d, dx):
        slot = index(z + d, lax.rem(x + across - dx, across), core)
        return slot_copy(slot, index(z, x, 1 - core), core_send.at[depth + d, dx])

    def exists(d):
        return (z + d >= 0) & (z + d < depth)

    def visit(d, act):
        if d:
            pl.when(exists(d))(act)
        else:
            act()

    def both_ways(d):
        return (-d, d) if d else (0,)

    def each_copy(d, act):
        if d:
            act(to_column(d))
        for dx in range(1, across):
            act(to_across(d, dx))
        act(to_core(d, 0))

    def spread(d):
        for dx in range(1, across):
            to_across(d, dx).start()
        to_core(d, 0).start()

    def column_step(d):
        def act():
            slot = along(d)
            arrived(slots.at[slot], slot_recv.at[slot])
            spread(d)

        visit(d, act)

    def across_step(d):
        def act():
            for dx in range(1, across):
                slot = index(z + d, lax.rem(x + across - dx, across), core)
                arrived(slots.at[slot], slot_recv.at[slot])
                to_core(d, dx).start()

        visit(d, act)

    for distance in range(depth - 1, 0, -1):
        for d in both_ways(distance):
            def act():
                to_column(d).start()

            visit(d, act)
    spread(0)
    for distance in range(1, depth):
        for d in both_ways(distance):
            column_step(d)
        for d in both_ways(distance - 1):
            across_step(d)

    per_tile = LANES // strip

    def store_tile(tile):
        where = pl.ds(pl.multiple_of(tile * LANES, LANES), LANES)
        return pltpu.make_async_copy(
            out_ref.at[:, :, :, where], out_hbm.at[:, :, :, where], store_sem.at[tile]
        )

    def unpack(tile):
        for i in range(per_tile):
            @pl.when(lax.rem(tile * per_tile + i, 2) != core)
            def _():
                slot = tile * per_tile + i
                arrived(slots.at[slot], slot_recv.at[slot])

        where = pl.ds(pl.multiple_of(tile * LANES, LANES), LANES)
        parts = []
        for i in range(per_tile):
            code = slots[tile * per_tile + i].astype(jnp.int32).astype(jnp.float32)
            parts.append(jnp.exp(code * step + middle))
        for f in range(frames):
            for k in range(layer_count):
                at = f * layer_count + k
                for g in range(groups):
                    ratio = None
                    for i in range(per_tile):
                        part = parts[i][at * short : (at + 1) * short]
                        turn = (strip * (i - g)) % LANES
                        if turn:
                            part = pltpu.roll(part, turn, 1)
                        ratio = part if ratio is None else jnp.where(lane < strip * i, ratio, part)
                    span = slice(g * short, (g + 1) * short)
                    out_ref[f, k, span, where] = (
                        layers_ref[f, k, span, where].astype(jnp.float32) * ratio
                    )
        store_tile(tile).start()

    early = strip == 64

    def unpack_column(n, carry):
        unpack(n * across + x)
        return carry

    if early:
        lax.fori_loop(0, depth, unpack_column, 0)
    for d in both_ways(depth - 1):
        across_step(d)

    def unpack_rest(n, carry):
        zz, dx = n // (across - 1), lax.rem(n, across - 1) + 1
        unpack(zz * across + lax.rem(x + dx, across))
        return carry

    def unpack_any(n, carry):
        unpack(n)
        return carry

    if early:
        lax.fori_loop(0, depth * (across - 1), unpack_rest, 0)
    else:
        lax.fori_loop(0, tiles, unpack_any, 0)

    for distance in range(depth):
        for d in both_ways(distance):
            def act():
                each_copy(d, lambda copy: copy.wait_send())
                for dx in range(1, across):
                    to_core(d, dx).wait_send()

            visit(d, act)

    @pl.when(above)
    def _():
        layer_copy(True).wait_send()

    @pl.when(below)
    def _():
        layer_copy(False).wait_send()

    def finish(j, carry):
        @pl.when(j > 0)
        def _():
            shift_copy(j).wait_send()
            win_copy(j).wait_send()

        @pl.when(above)
        def _():
            up_copy(j).wait_send()

        @pl.when(below)
        def _():
            down_copy(j).wait_send()

        return carry

    lax.fori_loop(0, views, finish, 0)

    def wait_store(tile, carry):
        store_tile(tile).wait()
        return carry

    lax.fori_loop(0, tiles, wait_store, 0)


def body(views, rows_of, layers, target, shifts):
    frames, layer_count, rows, cols = layers.shape
    planes = frames * layer_count
    strip = cols // views
    groups = 2 if strip == 64 else 1
    depth, across = split_views(views)
    packed_rows = -(-planes * (rows // groups) // 16) * 16
    height, inner = rows + 2 * EDGE, rows + 2 * HALO
    dma = pltpu.SemaphoreType.DMA
    f32, bf16 = jnp.float32, jnp.bfloat16
    return pl.pallas_call(
        functools.partial(kernel, views, rows_of),
        out_shape=jax.ShapeDtypeStruct(layers.shape, f32),
        in_specs=[
            pl.BlockSpec(memory_space=pltpu.HBM),
            pl.BlockSpec(memory_space=pltpu.HBM),
            pl.BlockSpec(memory_space=pltpu.HBM),
        ],
        out_specs=pl.BlockSpec(memory_space=pltpu.HBM),
        scratch_shapes=[
            pltpu.SMEM((1, 2, layer_count), jnp.int32),
            pltpu.VMEM(layers.shape, bf16),
            pltpu.VMEM(target.shape, bf16),
            pltpu.VMEM(layers.shape, f32),
            dma((3,)),
            dma((cols // LANES,)),
            pltpu.VMEM((views, rows, LANES), bf16),
            pltpu.VMEM((views, height, LANES), bf16),
            pltpu.VMEM((8, LANES), jnp.int32),
            pltpu.VMEM((views, 8, LANES), jnp.int32),
            pltpu.SMEM((views, 8, LANES), jnp.int32),
            pltpu.VMEM((2, planes, EDGE, LANES), bf16),
            pltpu.VMEM((2, planes, EDGE, LANES), bf16),
            pltpu.VMEM((planes, height, LANES), f32),
            pltpu.VMEM((height, LANES), f32),
            pltpu.VMEM((planes, inner, LANES), f32),
            pltpu.VMEM((inner, LANES), f32),
            pltpu.VMEM((inner, LANES), f32),
            pltpu.VMEM((planes, rows, LANES), f32),
            pltpu.VMEM((planes, rows, LANES), f32),
            pltpu.VMEM((packed_rows, LANES), f32),
            pltpu.VMEM((views, packed_rows, LANES), jnp.int16),
            dma((views,)), dma((views,)), dma((views,)), dma((views,)), dma((views,)), dma((views,)),
            dma((views,)), dma((views,)), dma, dma((2,)), dma((2,)),
            dma((2 * depth,)), dma((2 * depth, across)), dma((2 * depth, across)), dma((views,)),
        ],
        compiler_params=pltpu.CompilerParams(
            collective_id=0, has_side_effects=True, vmem_limit_bytes=62 * 1024 * 1024
        ),
        name="light_field_update",
    )(jnp.swapaxes(shifts, 1, 2), layers, target)


def solution(mesh):
    placed = (P(None, None, "row", None), P("view", "row", None), P("view", None, None))
    return jax.shard_map(
        functools.partial(body, mesh.shape["view"], mesh.shape["row"]),
        mesh=mesh, in_specs=placed, out_specs=P(None, None, "row", None), check_vma=False,
    )
```

```python
import functools
import math

import jax
import jax.numpy as jnp
from jax import lax
from jax.experimental import pallas as pl
from jax.experimental.pallas import tpu as pltpu
from jax.sharding import PartitionSpec as P

HALO = 8
LANES = 128
EDGE = 16
MARGIN = 32
REGULAR = 0.05
MESH = pl.DeviceIdType.MESH


def split_views(views):
    across = 1
    while (2 * across) ** 2 * 2 <= views:
        across *= 2
    return views // (2 * across), across


def code_range(views):
    low = math.log(REGULAR / (views + REGULAR))
    high = math.log((0.5 * views + REGULAR) / REGULAR)
    return 0.5 * (low + high), (high - low) / 65000.0


def kernel(
    views, rows_of, shifts_hbm, layers_hbm, target_hbm, out_hbm,
    shifts_ref, layers_ref, target_ref, out_ref, fetch_sem, store_sem,
    send_win, recv_win, shift_out, shift_in, shift_smem, halo_out, halo_in,
    layer_win, target_win, others_win, shown_win, third_win, upper, lower, packed, slots,
    win_send, win_recv, up_send, up_recv, down_send, down_recv,
    shift_send, shift_recv, smem_sem, lh_send, lh_recv,
    col_send, x_send, core_send, slot_recv,
):
    fetch_shifts = pltpu.make_async_copy(shifts_hbm, shifts_ref, fetch_sem.at[0])
    fetch_target = pltpu.make_async_copy(target_hbm, target_ref, fetch_sem.at[1])
    fetch_layers = pltpu.make_async_copy(layers_hbm, layers_ref, fetch_sem.at[2])
    fetch_shifts.start()
    fetch_target.start()
    fetch_layers.start()

    frames, layer_count, rows, cols = layers_ref.shape
    strip = cols // views
    planes = frames * layer_count
    height = rows + 2 * EDGE
    inner = rows + 2 * HALO
    depth, across = split_views(views)
    groups = 2 if strip == 64 else 1
    short = rows // groups
    tiles = cols // LANES
    middle, step = code_range(views)

    me = lax.axis_index("view")
    row = lax.axis_index("row")
    above, below = row > 0, row < rows_of - 1

    barrier = pltpu.get_barrier_semaphore()

    def greet(j, carry):
        partner = lax.rem(me + j, views)

        @pl.when(j > 0)
        def _():
            pl.semaphore_signal(barrier, inc=1, device_id=(partner, row), device_id_type=MESH)

        @pl.when(above)
        def _():
            pl.semaphore_signal(barrier, inc=1, device_id=(partner, row - 1), device_id_type=MESH)

        @pl.when(below)
        def _():
            pl.semaphore_signal(barrier, inc=1, device_id=(partner, row + 1), device_id_type=MESH)

        return carry

    lax.fori_loop(0, views, greet, 0)

    lane = lax.broadcasted_iota(jnp.int32, (1, LANES), 1)

    def window(load, index):
        start = strip * index - MARGIN
        tile = (start + LANES) // LANES - 1
        offset = start - tile * LANES
        first = load(jnp.maximum(tile, 0))
        second = load(jnp.minimum(tile + 1, tiles - 1))
        turn = lax.rem(LANES - offset, LANES)
        first = pltpu.roll(first, turn, 1)
        second = pltpu.roll(second, turn, 1)
        both = jnp.where(lane < LANES - offset, first, second)
        col = start + lane
        return jnp.where((col >= 0) & (col < cols), both, 0.0)

    fetch_shifts.wait()
    place = lax.broadcasted_iota(jnp.int32, (8, LANES), 1)
    block = jnp.zeros((8, LANES), jnp.int32)
    for k in range(layer_count):
        for axis in range(2):
            block = jnp.where(place == 2 * k + axis, shifts_ref[0, axis, k], block)
    shift_out[...] = block
    shift_in[me] = block

    fetch_target.wait()

    def fill(c, carry):
        def load(tile):
            where = pl.ds(pl.multiple_of(tile * LANES, LANES), LANES)
            return target_ref[0, :, where].astype(jnp.float32)

        send_win[c] = window(load, c).astype(jnp.bfloat16)
        return carry

    lax.fori_loop(0, views, fill, 0, unroll=4)
    recv_win[me, EDGE : EDGE + rows, :] = send_win[me]

    def shift_copy(j):
        partner = lax.rem(me + j, views)
        return pltpu.make_async_remote_copy(
            src_ref=shift_out, dst_ref=shift_in.at[me], send_sem=shift_send.at[j],
            recv_sem=shift_recv.at[me], device_id=(partner, row), device_id_type=MESH,
        )

    def win_copy(j):
        partner = lax.rem(me + j, views)
        return pltpu.make_async_remote_copy(
            src_ref=send_win.at[partner], dst_ref=recv_win.at[me, pl.ds(EDGE, rows)],
            send_sem=win_send.at[j], recv_sem=win_recv.at[me],
            device_id=(partner, row), device_id_type=MESH,
        )

    def up_copy(j):
        partner = lax.rem(me + j, views)
        return pltpu.make_async_remote_copy(
            src_ref=send_win.at[partner, pl.ds(0, EDGE)],
            dst_ref=recv_win.at[me, pl.ds(EDGE + rows, EDGE)],
            send_sem=up_send.at[j], recv_sem=up_recv.at[me],
            device_id=(partner, row - 1), device_id_type=MESH,
        )

    def down_copy(j):
        partner = lax.rem(me + j, views)
        return pltpu.make_async_remote_copy(
            src_ref=send_win.at[partner, pl.ds(rows - EDGE, EDGE)],
            dst_ref=recv_win.at[me, pl.ds(0, EDGE)],
            send_sem=down_send.at[j], recv_sem=down_recv.at[me],
            device_id=(partner, row + 1), device_id_type=MESH,
        )

    def layer_copy(up):
        return pltpu.make_async_remote_copy(
            src_ref=halo_out.at[0 if up else 1], dst_ref=halo_in.at[1 if up else 0],
            send_sem=lh_send.at[0 if up else 1], recv_sem=lh_recv.at[1 if up else 0],
            device_id=(me, row - 1 if up else row + 1), device_id_type=MESH,
        )

    def arrived(dst, sem):
        return pltpu.make_async_remote_copy(
            src_ref=dst, dst_ref=dst, send_sem=sem, recv_sem=sem,
            device_id=(me, row), device_id_type=MESH,
        ).wait_recv()

    pl.semaphore_wait(
        barrier, views - 1 + views * (above.astype(jnp.int32) + below.astype(jnp.int32))
    )

    def send_shift(j, carry):
        shift_copy(j).start()
        return carry

    lax.fori_loop(1, views, send_shift, 0)

    def send_all(j, carry):
        @pl.when(j > 0)
        def _():
            win_copy(j).start()

        @pl.when(above)
        def _():
            up_copy(j).start()

        @pl.when(below)
        def _():
            down_copy(j).start()

        return carry

    lax.fori_loop(0, views, send_all, 0)

    fetch_layers.wait()
    for f in range(frames):
        for k in range(layer_count):
            def load(tile):
                where = pl.ds(pl.multiple_of(tile * LANES, LANES), LANES)
                return layers_ref[f, k, :, where].astype(jnp.float32)

            plane = window(load, me)
            at = f * layer_count + k
            layer_win[at, EDGE : EDGE + rows, :] = plane
            halo_out[0, at] = plane[:EDGE].astype(jnp.bfloat16)
            halo_out[1, at] = plane[rows - EDGE :].astype(jnp.bfloat16)

    @pl.when(above)
    def _():
        layer_copy(True).start()

    @pl.when(below)
    def _():
        layer_copy(False).start()

    @pl.when(jnp.logical_not(above))
    def _():
        recv_win[:, :EDGE, :] = jnp.zeros((views, EDGE, LANES), jnp.bfloat16)
        layer_win[:, :EDGE, :] = jnp.zeros((planes, EDGE, LANES), jnp.float32)

    @pl.when(jnp.logical_not(below))
    def _():
        recv_win[:, EDGE + rows :, :] = jnp.zeros((views, EDGE, LANES), jnp.bfloat16)
        layer_win[:, EDGE + rows :, :] = jnp.zeros((planes, EDGE, LANES), jnp.float32)

    at_row = rows * row - HALO + lax.broadcasted_iota(jnp.int32, (inner, LANES), 0)
    at_col = strip * me - MARGIN + lax.broadcasted_iota(jnp.int32, (inner, LANES), 1)
    inside = (at_row >= 0) & (at_row < rows * rows_of) & (at_col >= 0) & (at_col < cols)
    third_win[...] = jnp.where(inside, 1.0 / frames, 0.0)
    upper[...] = jnp.zeros_like(upper)
    lower[...] = jnp.zeros_like(lower)

    def wait_shift(j, carry):
        source = lax.rem(me + views - j, views)
        arrived(shift_in.at[source], shift_recv.at[source])
        return carry

    lax.fori_loop(1, views, wait_shift, 0)
    to_smem = pltpu.make_async_copy(shift_in, shift_smem, smem_sem)
    to_smem.start()

    @pl.when(above)
    def _():
        arrived(halo_in.at[0], lh_recv.at[0])
        layer_win[:, :EDGE, :] = halo_in[0].astype(jnp.float32)

    @pl.when(below)
    def _():
        arrived(halo_in.at[1], lh_recv.at[1])
        layer_win[:, EDGE + rows :, :] = halo_in[1].astype(jnp.float32)

    to_smem.wait()

    def one_view(j, carry):
        view = lax.rem(me + views - j, views)

        @pl.when(j > 0)
        def _():
            arrived(recv_win.at[view, pl.ds(EDGE, rows)], win_recv.at[view])

        @pl.when(above)
        def _():
            arrived(recv_win.at[view, pl.ds(0, EDGE)], down_recv.at[view])

        @pl.when(below)
        def _():
            arrived(recv_win.at[view, pl.ds(EDGE + rows, EDGE)], up_recv.at[view])

        target_win[...] = recv_win[view].astype(jnp.float32)
        row_shift = [shift_smem[view, 0, 2 * k] for k in range(layer_count)]
        col_shift = [shift_smem[view, 0, 2 * k + 1] for k in range(layer_count)]
        there = [lax.rem(LANES - c, LANES) for c in col_shift]
        back = [lax.rem(LANES + c, LANES) for c in col_shift]

        total = None
        for f in range(frames):
            seen = [
                pltpu.roll(
                    layer_win[f * layer_count + k, pl.ds(EDGE - HALO + row_shift[k], inner), :],
                    there[k], 1,
                )
                for k in range(layer_count)
            ]
            for k in range(layer_count):
                rest = None
                for i in range(layer_count):
                    if i != k:
                        rest = seen[i] if rest is None else rest * seen[i]
                others_win[f * layer_count + k] = rest
                if k == layer_count - 1:
                    whole = rest * seen[k]
                    total = whole if total is None else total + whole
        shown_win[...] = total * third_win[...]

        for k in range(layer_count):
            image = pltpu.roll(target_win[pl.ds(EDGE - row_shift[k], rows), :], back[k], 1)
            model = pltpu.roll(shown_win[pl.ds(HALO - row_shift[k], rows), :], back[k], 1)
            for f in range(frames):
                at = f * layer_count + k
                rest = pltpu.roll(
                    others_win[at, pl.ds(HALO - row_shift[k], rows), :], back[k], 1
                )
                upper[at] += image * rest
                lower[at] += model * rest
        return carry

    lax.fori_loop(0, views, one_view, 0)

    spare = packed.shape[0] - planes * short
    if spare:
        packed[planes * short :, :] = jnp.zeros((spare, LANES), jnp.float32)
    for at in range(planes):
        ratio = (upper[at] + REGULAR) / (lower[at] + REGULAR)
        value = (jnp.log(ratio) - middle) * (1.0 / step)
        merged = pltpu.roll(value[:short], LANES - MARGIN, 1)
        if groups == 2:
            merged = jnp.where(lane < strip, merged, pltpu.roll(value[short:], strip - MARGIN, 1))
        packed[at * short : (at + 1) * short, :] = merged
    slots[me] = jnp.round(packed[...]).astype(jnp.int32).astype(jnp.int16)

    core = lax.rem(me, 2)
    x = lax.rem(me // 2, across)
    z = me // (2 * across)

    def index(zz, xx, cc):
        return (zz * across + xx) * 2 + cc

    def slot_copy(slot, to, sem):
        return pltpu.make_async_remote_copy(
            src_ref=slots.at[slot], dst_ref=slots.at[slot], send_sem=sem,
            recv_sem=slot_recv.at[slot], device_id=(to, row), device_id_type=MESH,
        )

    def along(d):
        return index(z + d, x, core)

    def to_column(d):
        return slot_copy(me, index(z + d, x, core), col_send.at[depth + d])

    def to_across(d, dx):
        return slot_copy(
            along(d), index(z, lax.rem(x + dx, across), core), x_send.at[depth + d, dx]
        )

    def to_core(d, dx):
        slot = index(z + d, lax.rem(x + across - dx, across), core)
        return slot_copy(slot, index(z, x, 1 - core), core_send.at[depth + d, dx])

    def exists(d):
        return (z + d >= 0) & (z + d < depth)

    def visit(d, act):
        if d:
            pl.when(exists(d))(act)
        else:
            act()

    def both_ways(d):
        return (-d, d) if d else (0,)

    def each_copy(d, act):
        if d:
            act(to_column(d))
        for dx in range(1, across):
            act(to_across(d, dx))
        act(to_core(d, 0))

    def spread(d):
        for dx in range(1, across):
            to_across(d, dx).start()
        to_core(d, 0).start()

    def column_step(d):
        def act():
            slot = along(d)
            arrived(slots.at[slot], slot_recv.at[slot])
            spread(d)

        visit(d, act)

    def across_step(d):
        def act():
            for dx in range(1, across):
                slot = index(z + d, lax.rem(x + across - dx, across), core)
                arrived(slots.at[slot], slot_recv.at[slot])
                to_core(d, dx).start()

        visit(d, act)

    for distance in range(depth - 1, 0, -1):
        for d in both_ways(distance):
            def act():
                to_column(d).start()

            visit(d, act)
    spread(0)
    for distance in range(1, depth):
        for d in both_ways(distance):
            column_step(d)
        for d in both_ways(distance - 1):
            across_step(d)

    per_tile = LANES // strip

    def store_tile(tile):
        where = pl.ds(pl.multiple_of(tile * LANES, LANES), LANES)
        return pltpu.make_async_copy(
            out_ref.at[:, :, :, where], out_hbm.at[:, :, :, where], store_sem.at[tile]
        )

    def unpack(tile):
        for i in range(per_tile):
            @pl.when(lax.rem(tile * per_tile + i, 2) != core)
            def _():
                slot = tile * per_tile + i
                arrived(slots.at[slot], slot_recv.at[slot])

        where = pl.ds(pl.multiple_of(tile * LANES, LANES), LANES)
        parts = [slots[tile * per_tile + i].astype(jnp.int32) for i in range(per_tile)]
        for f in range(frames):
            for k in range(layer_count):
                at = f * layer_count + k
                spans = []
                for g in range(groups):
                    code = None
                    for i in range(per_tile):
                        part = parts[i][at * short : (at + 1) * short]
                        turn = (strip * (i - g)) % LANES
                        if turn:
                            part = pltpu.roll(part, turn, 1)
                        code = part if code is None else jnp.where(lane < strip * i, code, part)
                    spans.append(code)
                whole = jnp.concatenate(spans, axis=0) if groups > 1 else spans[0]
                out_ref[f, k, :, where] = whole.astype(jnp.int16)
        store_tile(tile).start()

    early = strip == 64

    def unpack_column(n, carry):
        unpack(n * across + x)
        return carry

    if early:
        lax.fori_loop(0, depth, unpack_column, 0)
    for d in both_ways(depth - 1):
        across_step(d)

    def unpack_rest(n, carry):
        zz, dx = n // (across - 1), lax.rem(n, across - 1) + 1
        unpack(zz * across + lax.rem(x + dx, across))
        return carry

    def unpack_any(n, carry):
        unpack(n)
        return carry

    if early:
        lax.fori_loop(0, depth * (across - 1), unpack_rest, 0)
    else:
        lax.fori_loop(0, tiles, unpack_any, 0)

    for distance in range(depth):
        for d in both_ways(distance):
            def act():
                each_copy(d, lambda copy: copy.wait_send())
                for dx in range(1, across):
                    to_core(d, dx).wait_send()

            visit(d, act)

    @pl.when(above)
    def _():
        layer_copy(True).wait_send()

    @pl.when(below)
    def _():
        layer_copy(False).wait_send()

    def finish(j, carry):
        @pl.when(j > 0)
        def _():
            shift_copy(j).wait_send()
            win_copy(j).wait_send()

        @pl.when(above)
        def _():
            up_copy(j).wait_send()

        @pl.when(below)
        def _():
            down_copy(j).wait_send()

        return carry

    lax.fori_loop(0, views, finish, 0)

    def wait_store(tile, carry):
        store_tile(tile).wait()
        return carry

    lax.fori_loop(0, tiles, wait_store, 0)


def body(views, rows_of, layers, target, shifts):
    frames, layer_count, rows, cols = layers.shape
    planes = frames * layer_count
    strip = cols // views
    groups = 2 if strip == 64 else 1
    depth, across = split_views(views)
    packed_rows = -(-planes * (rows // groups) // 16) * 16
    height, inner = rows + 2 * EDGE, rows + 2 * HALO
    dma = pltpu.SemaphoreType.DMA
    f32, bf16 = jnp.float32, jnp.bfloat16
    codes = pl.pallas_call(
        functools.partial(kernel, views, rows_of),
        out_shape=jax.ShapeDtypeStruct(layers.shape, jnp.int16),
        in_specs=[
            pl.BlockSpec(memory_space=pltpu.HBM),
            pl.BlockSpec(memory_space=pltpu.HBM),
            pl.BlockSpec(memory_space=pltpu.HBM),
        ],
        out_specs=pl.BlockSpec(memory_space=pltpu.HBM),
        scratch_shapes=[
            pltpu.SMEM((1, 2, layer_count), jnp.int32),
            pltpu.VMEM(layers.shape, bf16),
            pltpu.VMEM(target.shape, bf16),
            pltpu.VMEM(layers.shape, jnp.int16),
            dma((3,)),
            dma((cols // LANES,)),
            pltpu.VMEM((views, rows, LANES), bf16),
            pltpu.VMEM((views, height, LANES), bf16),
            pltpu.VMEM((8, LANES), jnp.int32),
            pltpu.VMEM((views, 8, LANES), jnp.int32),
            pltpu.SMEM((views, 8, LANES), jnp.int32),
            pltpu.VMEM((2, planes, EDGE, LANES), bf16),
            pltpu.VMEM((2, planes, EDGE, LANES), bf16),
            pltpu.VMEM((planes, height, LANES), f32),
            pltpu.VMEM((height, LANES), f32),
            pltpu.VMEM((planes, inner, LANES), f32),
            pltpu.VMEM((inner, LANES), f32),
            pltpu.VMEM((inner, LANES), f32),
            pltpu.VMEM((planes, rows, LANES), f32),
            pltpu.VMEM((planes, rows, LANES), f32),
            pltpu.VMEM((packed_rows, LANES), f32),
            pltpu.VMEM((views, packed_rows, LANES), jnp.int16),
            dma((views,)), dma((views,)), dma((views,)), dma((views,)), dma((views,)), dma((views,)),
            dma((views,)), dma((views,)), dma, dma((2,)), dma((2,)),
            dma((2 * depth,)), dma((2 * depth, across)), dma((2 * depth, across)), dma((views,)),
        ],
        compiler_params=pltpu.CompilerParams(
            collective_id=0, has_side_effects=True, vmem_limit_bytes=62 * 1024 * 1024
        ),
        name="light_field_update",
    )(jnp.swapaxes(shifts, 1, 2), layers, target)
    middle, step = code_range(views)
    return layers.astype(f32) * jnp.exp(codes.astype(f32) * step + middle)


def solution(mesh):
    placed = (P(None, None, "row", None), P("view", "row", None), P("view", None, None))
    return jax.shard_map(
        functools.partial(body, mesh.shape["view"], mesh.shape["row"]),
        mesh=mesh, in_specs=placed, out_specs=P(None, None, "row", None), check_vma=False,
    )
```

```python
import functools
import math

import jax
import jax.numpy as jnp
from jax import lax
from jax.experimental import pallas as pl
from jax.experimental.pallas import tpu as pltpu
from jax.sharding import PartitionSpec as P

HALO = 8
LANES = 128
EDGE = 16
MARGIN = 32
REGULAR = 0.05
BATCH = 2
MESH = pl.DeviceIdType.MESH


def split_views(views):
    across = 1
    while (2 * across) ** 2 * 2 <= views:
        across *= 2
    return views // (2 * across), across


def code_range(views):
    low = math.log(REGULAR / (views + REGULAR))
    high = math.log((0.5 * views + REGULAR) / REGULAR)
    return 0.5 * (low + high), (high - low) / 65000.0


def kernel(
    views, rows_of, shifts_hbm, layers_hbm, target_hbm, out_hbm,
    shifts_ref, layers_ref, target_ref, out_ref, fetch_sem, store_sem,
    send_win, recv_win, shift_out, shift_in, shift_smem, halo_out, halo_in,
    layer_win, target_win, others_win, shown_win, third_win, upper, lower, packed, slots,
    win_send, win_recv, up_send, up_recv, down_send, down_recv,
    shift_send, shift_recv, smem_sem, lh_send, lh_recv,
    col_send, x_send, core_send, slot_recv,
):
    fetch_shifts = pltpu.make_async_copy(shifts_hbm, shifts_ref, fetch_sem.at[0])
    fetch_target = pltpu.make_async_copy(target_hbm, target_ref, fetch_sem.at[1])
    fetch_layers = pltpu.make_async_copy(layers_hbm, layers_ref, fetch_sem.at[2])
    fetch_shifts.start()
    fetch_target.start()
    fetch_layers.start()

    frames, layer_count, rows, cols = layers_ref.shape
    strip = cols // views
    planes = frames * layer_count
    height = rows + 2 * EDGE
    inner = rows + 2 * HALO
    depth, across = split_views(views)
    groups = 2 if strip == 64 else 1
    short = rows // groups
    tiles = cols // LANES
    middle, step = code_range(views)

    me = lax.axis_index("view")
    row = lax.axis_index("row")
    above, below = row > 0, row < rows_of - 1

    barrier = pltpu.get_barrier_semaphore()

    def greet(j, carry):
        partner = lax.rem(me + j, views)

        @pl.when(j > 0)
        def _():
            pl.semaphore_signal(barrier, inc=1, device_id=(partner, row), device_id_type=MESH)

        @pl.when(above)
        def _():
            pl.semaphore_signal(barrier, inc=1, device_id=(partner, row - 1), device_id_type=MESH)

        @pl.when(below)
        def _():
            pl.semaphore_signal(barrier, inc=1, device_id=(partner, row + 1), device_id_type=MESH)

        return carry

    lax.fori_loop(0, views, greet, 0)

    lane = lax.broadcasted_iota(jnp.int32, (1, LANES), 1)

    def window(load, index):
        start = strip * index - MARGIN
        tile = (start + LANES) // LANES - 1
        offset = start - tile * LANES
        first = load(jnp.maximum(tile, 0))
        second = load(jnp.minimum(tile + 1, tiles - 1))
        turn = lax.rem(LANES - offset, LANES)
        first = pltpu.roll(first, turn, 1)
        second = pltpu.roll(second, turn, 1)
        both = jnp.where(lane < LANES - offset, first, second)
        col = start + lane
        return jnp.where((col >= 0) & (col < cols), both, 0.0)

    fetch_shifts.wait()
    place = lax.broadcasted_iota(jnp.int32, (8, LANES), 1)
    block = jnp.zeros((8, LANES), jnp.int32)
    for k in range(layer_count):
        for axis in range(2):
            block = jnp.where(place == 2 * k + axis, shifts_ref[0, axis, k], block)
    shift_out[...] = block
    shift_in[me] = block

    fetch_target.wait()

    def fill(c, carry):
        def load(tile):
            where = pl.ds(pl.multiple_of(tile * LANES, LANES), LANES)
            return target_ref[0, :, where].astype(jnp.float32)

        send_win[c] = window(load, c).astype(jnp.bfloat16)
        return carry

    lax.fori_loop(0, views, fill, 0, unroll=4)
    recv_win[me, EDGE : EDGE + rows, :] = send_win[me]

    def shift_copy(j):
        partner = lax.rem(me + j, views)
        return pltpu.make_async_remote_copy(
            src_ref=shift_out, dst_ref=shift_in.at[me], send_sem=shift_send.at[j],
            recv_sem=shift_recv.at[me], device_id=(partner, row), device_id_type=MESH,
        )

    def win_copy(j):
        partner = lax.rem(me + j, views)
        return pltpu.make_async_remote_copy(
            src_ref=send_win.at[partner], dst_ref=recv_win.at[me, pl.ds(EDGE, rows)],
            send_sem=win_send.at[j], recv_sem=win_recv.at[me],
            device_id=(partner, row), device_id_type=MESH,
        )

    def up_copy(j):
        partner = lax.rem(me + j, views)
        return pltpu.make_async_remote_copy(
            src_ref=send_win.at[partner, pl.ds(0, EDGE)],
            dst_ref=recv_win.at[me, pl.ds(EDGE + rows, EDGE)],
            send_sem=up_send.at[j], recv_sem=up_recv.at[me],
            device_id=(partner, row - 1), device_id_type=MESH,
        )

    def down_copy(j):
        partner = lax.rem(me + j, views)
        return pltpu.make_async_remote_copy(
            src_ref=send_win.at[partner, pl.ds(rows - EDGE, EDGE)],
            dst_ref=recv_win.at[me, pl.ds(0, EDGE)],
            send_sem=down_send.at[j], recv_sem=down_recv.at[me],
            device_id=(partner, row + 1), device_id_type=MESH,
        )

    def layer_copy(up):
        return pltpu.make_async_remote_copy(
            src_ref=halo_out.at[0 if up else 1], dst_ref=halo_in.at[1 if up else 0],
            send_sem=lh_send.at[0 if up else 1], recv_sem=lh_recv.at[1 if up else 0],
            device_id=(me, row - 1 if up else row + 1), device_id_type=MESH,
        )

    def arrived(dst, sem):
        return pltpu.make_async_remote_copy(
            src_ref=dst, dst_ref=dst, send_sem=sem, recv_sem=sem,
            device_id=(me, row), device_id_type=MESH,
        ).wait_recv()

    pl.semaphore_wait(
        barrier, views - 1 + views * (above.astype(jnp.int32) + below.astype(jnp.int32))
    )

    def send_shift(j, carry):
        shift_copy(j).start()
        return carry

    lax.fori_loop(1, views, send_shift, 0)

    def send_all(j, carry):
        @pl.when(j > 0)
        def _():
            win_copy(j).start()

        @pl.when(above)
        def _():
            up_copy(j).start()

        @pl.when(below)
        def _():
            down_copy(j).start()

        return carry

    lax.fori_loop(0, views, send_all, 0)

    fetch_layers.wait()
    for f in range(frames):
        for k in range(layer_count):
            def load(tile):
                where = pl.ds(pl.multiple_of(tile * LANES, LANES), LANES)
                return layers_ref[f, k, :, where].astype(jnp.float32)

            plane = window(load, me)
            at = f * layer_count + k
            layer_win[at, EDGE : EDGE + rows, :] = plane
            halo_out[0, at] = plane[:EDGE].astype(jnp.bfloat16)
            halo_out[1, at] = plane[rows - EDGE :].astype(jnp.bfloat16)

    @pl.when(above)
    def _():
        layer_copy(True).start()

    @pl.when(below)
    def _():
        layer_copy(False).start()

    @pl.when(jnp.logical_not(above))
    def _():
        recv_win[:, :EDGE, :] = jnp.zeros((views, EDGE, LANES), jnp.bfloat16)
        layer_win[:, :EDGE, :] = jnp.zeros((planes, EDGE, LANES), jnp.float32)

    @pl.when(jnp.logical_not(below))
    def _():
        recv_win[:, EDGE + rows :, :] = jnp.zeros((views, EDGE, LANES), jnp.bfloat16)
        layer_win[:, EDGE + rows :, :] = jnp.zeros((planes, EDGE, LANES), jnp.float32)

    at_row = rows * row - HALO + lax.broadcasted_iota(jnp.int32, (inner, LANES), 0)
    at_col = strip * me - MARGIN + lax.broadcasted_iota(jnp.int32, (inner, LANES), 1)
    inside = (at_row >= 0) & (at_row < rows * rows_of) & (at_col >= 0) & (at_col < cols)
    third_win[...] = jnp.where(inside, 1.0 / frames, 0.0)
    upper[...] = jnp.zeros_like(upper)
    lower[...] = jnp.zeros_like(lower)

    def wait_shift(j, carry):
        source = lax.rem(me + views - j, views)
        arrived(shift_in.at[source], shift_recv.at[source])
        return carry

    lax.fori_loop(1, views, wait_shift, 0)
    to_smem = pltpu.make_async_copy(shift_in, shift_smem, smem_sem)
    to_smem.start()

    @pl.when(above)
    def _():
        arrived(halo_in.at[0], lh_recv.at[0])
        layer_win[:, :EDGE, :] = halo_in[0].astype(jnp.float32)

    @pl.when(below)
    def _():
        arrived(halo_in.at[1], lh_recv.at[1])
        layer_win[:, EDGE + rows :, :] = halo_in[1].astype(jnp.float32)

    to_smem.wait()

    def some_views(n, carry):
        views_now = []
        for b in range(BATCH):
            j = n * BATCH + b
            view = lax.rem(me + views - j, views)
            views_now.append(view)

            @pl.when(j > 0)
            def _():
                arrived(recv_win.at[view, pl.ds(EDGE, rows)], win_recv.at[view])

            @pl.when(above)
            def _():
                arrived(recv_win.at[view, pl.ds(0, EDGE)], down_recv.at[view])

            @pl.when(below)
            def _():
                arrived(recv_win.at[view, pl.ds(EDGE + rows, EDGE)], up_recv.at[view])

        row_shift, back = [], []
        for b, view in enumerate(views_now):
            target_win[b] = recv_win[view].astype(jnp.float32)
            row_now = [shift_smem[view, 0, 2 * k] for k in range(layer_count)]
            col_now = [shift_smem[view, 0, 2 * k + 1] for k in range(layer_count)]
            there = [lax.rem(LANES - c, LANES) for c in col_now]
            row_shift.append(row_now)
            back.append([lax.rem(LANES + c, LANES) for c in col_now])
            total = None
            for f in range(frames):
                seen = [
                    pltpu.roll(
                        layer_win[f * layer_count + k, pl.ds(EDGE - HALO + row_now[k], inner), :],
                        there[k], 1,
                    )
                    for k in range(layer_count)
                ]
                for k in range(layer_count):
                    rest = None
                    for i in range(layer_count):
                        if i != k:
                            rest = seen[i] if rest is None else rest * seen[i]
                    others_win[b, f * layer_count + k] = rest
                    if k == layer_count - 1:
                        whole = rest * seen[k]
                        total = whole if total is None else total + whole
            shown_win[b] = total * third_win[...]

        for k in range(layer_count):
            image, model = [], []
            for b in range(BATCH):
                turn, by = back[b][k], row_shift[b][k]
                image.append(pltpu.roll(target_win[b, pl.ds(EDGE - by, rows), :], turn, 1))
                model.append(pltpu.roll(shown_win[b, pl.ds(HALO - by, rows), :], turn, 1))
            for f in range(frames):
                at = f * layer_count + k
                up, low = upper[at], lower[at]
                for b in range(BATCH):
                    rest = pltpu.roll(
                        others_win[b, at, pl.ds(HALO - row_shift[b][k], rows), :], back[b][k], 1
                    )
                    up += image[b] * rest
                    low += model[b] * rest
                upper[at] = up
                lower[at] = low
        return carry

    lax.fori_loop(0, views // BATCH, some_views, 0)

    spare = packed.shape[0] - planes * short
    if spare:
        packed[planes * short :, :] = jnp.zeros((spare, LANES), jnp.float32)
    for at in range(planes):
        ratio = (upper[at] + REGULAR) / (lower[at] + REGULAR)
        value = (jnp.log(ratio) - middle) * (1.0 / step)
        merged = pltpu.roll(value[:short], LANES - MARGIN, 1)
        if groups == 2:
            merged = jnp.where(lane < strip, merged, pltpu.roll(value[short:], strip - MARGIN, 1))
        packed[at * short : (at + 1) * short, :] = merged
    slots[me] = jnp.round(packed[...]).astype(jnp.int32).astype(jnp.int16)

    core = lax.rem(me, 2)
    x = lax.rem(me // 2, across)
    z = me // (2 * across)

    def index(zz, xx, cc):
        return (zz * across + xx) * 2 + cc

    def slot_copy(slot, to, sem):
        return pltpu.make_async_remote_copy(
            src_ref=slots.at[slot], dst_ref=slots.at[slot], send_sem=sem,
            recv_sem=slot_recv.at[slot], device_id=(to, row), device_id_type=MESH,
        )

    def along(d):
        return index(z + d, x, core)

    def to_column(d):
        return slot_copy(me, index(z + d, x, core), col_send.at[depth + d])

    def to_across(d, dx):
        return slot_copy(
            along(d), index(z, lax.rem(x + dx, across), core), x_send.at[depth + d, dx]
        )

    def to_core(d, dx):
        slot = index(z + d, lax.rem(x + across - dx, across), core)
        return slot_copy(slot, index(z, x, 1 - core), core_send.at[depth + d, dx])

    def exists(d):
        return (z + d >= 0) & (z + d < depth)

    def visit(d, act):
        if d:
            pl.when(exists(d))(act)
        else:
            act()

    def both_ways(d):
        return (-d, d) if d else (0,)

    def each_copy(d, act):
        if d:
            act(to_column(d))
        for dx in range(1, across):
            act(to_across(d, dx))
        act(to_core(d, 0))

    def spread(d):
        for dx in range(1, across):
            to_across(d, dx).start()
        to_core(d, 0).start()

    def column_step(d):
        def act():
            slot = along(d)
            arrived(slots.at[slot], slot_recv.at[slot])
            spread(d)

        visit(d, act)

    def across_step(d):
        def act():
            for dx in range(1, across):
                slot = index(z + d, lax.rem(x + across - dx, across), core)
                arrived(slots.at[slot], slot_recv.at[slot])
                to_core(d, dx).start()

        visit(d, act)

    for distance in range(depth - 1, 0, -1):
        for d in both_ways(distance):
            def act():
                to_column(d).start()

            visit(d, act)
    spread(0)
    for distance in range(1, depth):
        for d in both_ways(distance):
            column_step(d)
        for d in both_ways(distance - 1):
            across_step(d)

    per_tile = LANES // strip

    def store_tile(tile):
        where = pl.ds(pl.multiple_of(tile * LANES, LANES), LANES)
        return pltpu.make_async_copy(
            out_ref.at[:, :, :, where], out_hbm.at[:, :, :, where], store_sem.at[tile]
        )

    def unpack(tile):
        for i in range(per_tile):
            @pl.when(lax.rem(tile * per_tile + i, 2) != core)
            def _():
                slot = tile * per_tile + i
                arrived(slots.at[slot], slot_recv.at[slot])

        where = pl.ds(pl.multiple_of(tile * LANES, LANES), LANES)
        parts = [slots[tile * per_tile + i].astype(jnp.int32) for i in range(per_tile)]
        for f in range(frames):
            for k in range(layer_count):
                at = f * layer_count + k
                spans = []
                for g in range(groups):
                    code = None
                    for i in range(per_tile):
                        part = parts[i][at * short : (at + 1) * short]
                        turn = (strip * (i - g)) % LANES
                        if turn:
                            part = pltpu.roll(part, turn, 1)
                        code = part if code is None else jnp.where(lane < strip * i, code, part)
                    spans.append(code)
                whole = jnp.concatenate(spans, axis=0) if groups > 1 else spans[0]
                out_ref[f, k, :, where] = whole.astype(jnp.int16)
        store_tile(tile).start()

    early = strip == 64

    def unpack_column(n, carry):
        unpack(n * across + x)
        return carry

    if early:
        lax.fori_loop(0, depth, unpack_column, 0)
    for d in both_ways(depth - 1):
        across_step(d)

    def unpack_rest(n, carry):
        zz, dx = n // (across - 1), lax.rem(n, across - 1) + 1
        unpack(zz * across + lax.rem(x + dx, across))
        return carry

    def unpack_any(n, carry):
        unpack(n)
        return carry

    if early:
        lax.fori_loop(0, depth * (across - 1), unpack_rest, 0)
    else:
        lax.fori_loop(0, tiles, unpack_any, 0)

    for distance in range(depth):
        for d in both_ways(distance):
            def act():
                each_copy(d, lambda copy: copy.wait_send())
                for dx in range(1, across):
                    to_core(d, dx).wait_send()

            visit(d, act)

    @pl.when(above)
    def _():
        layer_copy(True).wait_send()

    @pl.when(below)
    def _():
        layer_copy(False).wait_send()

    def finish(j, carry):
        @pl.when(j > 0)
        def _():
            shift_copy(j).wait_send()
            win_copy(j).wait_send()

        @pl.when(above)
        def _():
            up_copy(j).wait_send()

        @pl.when(below)
        def _():
            down_copy(j).wait_send()

        return carry

    lax.fori_loop(0, views, finish, 0)

    def wait_store(tile, carry):
        store_tile(tile).wait()
        return carry

    lax.fori_loop(0, tiles, wait_store, 0)


def body(views, rows_of, layers, target, shifts):
    frames, layer_count, rows, cols = layers.shape
    planes = frames * layer_count
    strip = cols // views
    groups = 2 if strip == 64 else 1
    depth, across = split_views(views)
    packed_rows = -(-planes * (rows // groups) // 16) * 16
    height, inner = rows + 2 * EDGE, rows + 2 * HALO
    dma = pltpu.SemaphoreType.DMA
    f32, bf16 = jnp.float32, jnp.bfloat16
    codes = pl.pallas_call(
        functools.partial(kernel, views, rows_of),
        out_shape=jax.ShapeDtypeStruct(layers.shape, jnp.int16),
        in_specs=[
            pl.BlockSpec(memory_space=pltpu.HBM),
            pl.BlockSpec(memory_space=pltpu.HBM),
            pl.BlockSpec(memory_space=pltpu.HBM),
        ],
        out_specs=pl.BlockSpec(memory_space=pltpu.HBM),
        scratch_shapes=[
            pltpu.SMEM((1, 2, layer_count), jnp.int32),
            pltpu.VMEM(layers.shape, bf16),
            pltpu.VMEM(target.shape, bf16),
            pltpu.VMEM(layers.shape, jnp.int16),
            dma((3,)),
            dma((cols // LANES,)),
            pltpu.VMEM((views, rows, LANES), bf16),
            pltpu.VMEM((views, height, LANES), bf16),
            pltpu.VMEM((8, LANES), jnp.int32),
            pltpu.VMEM((views, 8, LANES), jnp.int32),
            pltpu.SMEM((views, 8, LANES), jnp.int32),
            pltpu.VMEM((2, planes, EDGE, LANES), bf16),
            pltpu.VMEM((2, planes, EDGE, LANES), bf16),
            pltpu.VMEM((planes, height, LANES), f32),
            pltpu.VMEM((BATCH, height, LANES), f32),
            pltpu.VMEM((BATCH, planes, inner, LANES), f32),
            pltpu.VMEM((BATCH, inner, LANES), f32),
            pltpu.VMEM((inner, LANES), f32),
            pltpu.VMEM((planes, rows, LANES), f32),
            pltpu.VMEM((planes, rows, LANES), f32),
            pltpu.VMEM((packed_rows, LANES), f32),
            pltpu.VMEM((views, packed_rows, LANES), jnp.int16),
            dma((views,)), dma((views,)), dma((views,)), dma((views,)), dma((views,)), dma((views,)),
            dma((views,)), dma((views,)), dma, dma((2,)), dma((2,)),
            dma((2 * depth,)), dma((2 * depth, across)), dma((2 * depth, across)), dma((views,)),
        ],
        compiler_params=pltpu.CompilerParams(
            collective_id=0, has_side_effects=True, vmem_limit_bytes=62 * 1024 * 1024
        ),
        name="light_field_update",
    )(jnp.swapaxes(shifts, 1, 2), layers, target)
    middle, step = code_range(views)
    return layers.astype(f32) * jnp.exp(codes.astype(f32) * step + middle)


def solution(mesh):
    placed = (P(None, None, "row", None), P("view", "row", None), P("view", None, None))
    return jax.shard_map(
        functools.partial(body, mesh.shape["view"], mesh.shape["row"]),
        mesh=mesh, in_specs=placed, out_specs=P(None, None, "row", None), check_vma=False,
    )
```

```python
import functools
import math

import jax
import jax.numpy as jnp
from jax import lax
from jax.experimental import pallas as pl
from jax.experimental.pallas import tpu as pltpu
from jax.sharding import PartitionSpec as P

HALO = 8
LANES = 128
EDGE = 16
MARGIN = 32
REGULAR = 0.05
BATCH = 4
MESH = pl.DeviceIdType.MESH


def split_views(views):
    across = 1
    while (2 * across) ** 2 * 2 <= views:
        across *= 2
    return views // (2 * across), across


def code_range(views):
    low = math.log(REGULAR / (views + REGULAR))
    high = math.log((0.5 * views + REGULAR) / REGULAR)
    return 0.5 * (low + high), (high - low) / 65000.0


def kernel(
    views, rows_of, shifts_hbm, layers_hbm, target_hbm, out_hbm,
    shifts_ref, layers_ref, target_ref, out_ref, fetch_sem, store_sem,
    send_win, recv_win, shift_out, shift_in, shift_smem, halo_out, halo_in,
    layer_win, target_win, others_win, shown_win, third_win, upper, lower, packed, slots,
    win_send, win_recv, up_send, up_recv, down_send, down_recv,
    shift_send, shift_recv, smem_sem, lh_send, lh_recv,
    col_send, x_send, core_send, slot_recv,
):
    fetch_shifts = pltpu.make_async_copy(shifts_hbm, shifts_ref, fetch_sem.at[0])
    fetch_target = pltpu.make_async_copy(target_hbm, target_ref, fetch_sem.at[1])
    fetch_layers = pltpu.make_async_copy(layers_hbm, layers_ref, fetch_sem.at[2])
    fetch_shifts.start()
    fetch_target.start()
    fetch_layers.start()

    frames, layer_count, rows, cols = layers_ref.shape
    strip = cols // views
    planes = frames * layer_count
    height = rows + 2 * EDGE
    inner = rows + 2 * HALO
    depth, across = split_views(views)
    groups = 2 if strip == 64 else 1
    short = rows // groups
    tiles = cols // LANES
    middle, step = code_range(views)

    me = lax.axis_index("view")
    row = lax.axis_index("row")
    above, below = row > 0, row < rows_of - 1

    barrier = pltpu.get_barrier_semaphore()

    def greet(j, carry):
        partner = lax.rem(me + j, views)

        @pl.when(j > 0)
        def _():
            pl.semaphore_signal(barrier, inc=1, device_id=(partner, row), device_id_type=MESH)

        @pl.when(above)
        def _():
            pl.semaphore_signal(barrier, inc=1, device_id=(partner, row - 1), device_id_type=MESH)

        @pl.when(below)
        def _():
            pl.semaphore_signal(barrier, inc=1, device_id=(partner, row + 1), device_id_type=MESH)

        return carry

    lax.fori_loop(0, views, greet, 0)

    lane = lax.broadcasted_iota(jnp.int32, (1, LANES), 1)

    def window(load, index):
        start = strip * index - MARGIN
        tile = (start + LANES) // LANES - 1
        offset = start - tile * LANES
        first = load(jnp.maximum(tile, 0))
        second = load(jnp.minimum(tile + 1, tiles - 1))
        turn = lax.rem(LANES - offset, LANES)
        first = pltpu.roll(first, turn, 1)
        second = pltpu.roll(second, turn, 1)
        both = jnp.where(lane < LANES - offset, first, second)
        col = start + lane
        return jnp.where((col >= 0) & (col < cols), both, 0.0)

    fetch_shifts.wait()
    place = lax.broadcasted_iota(jnp.int32, (1, LANES), 1)
    block = jnp.zeros((1, LANES), jnp.int32)
    for k in range(layer_count):
        for axis in range(2):
            block = jnp.where(place == 2 * k + axis, shifts_ref[0, axis, k], block)
    shift_out[...] = block
    shift_in[me] = block

    fetch_target.wait()

    def fill(c, carry):
        def load(tile):
            where = pl.ds(pl.multiple_of(tile * LANES, LANES), LANES)
            return target_ref[0, :, where].astype(jnp.float32)

        send_win[c] = window(load, c).astype(jnp.bfloat16)
        return carry

    lax.fori_loop(0, views, fill, 0, unroll=4)
    recv_win[me, EDGE : EDGE + rows, :] = send_win[me]

    def shift_copy(j):
        partner = lax.rem(me + j, views)
        return pltpu.make_async_remote_copy(
            src_ref=shift_out, dst_ref=shift_in.at[me], send_sem=shift_send.at[j],
            recv_sem=shift_recv.at[me], device_id=(partner, row), device_id_type=MESH,
        )

    def win_copy(j):
        partner = lax.rem(me + j, views)
        return pltpu.make_async_remote_copy(
            src_ref=send_win.at[partner], dst_ref=recv_win.at[me, pl.ds(EDGE, rows)],
            send_sem=win_send.at[j], recv_sem=win_recv.at[me],
            device_id=(partner, row), device_id_type=MESH,
        )

    def up_copy(j):
        partner = lax.rem(me + j, views)
        return pltpu.make_async_remote_copy(
            src_ref=send_win.at[partner, pl.ds(0, EDGE)],
            dst_ref=recv_win.at[me, pl.ds(EDGE + rows, EDGE)],
            send_sem=up_send.at[j], recv_sem=up_recv.at[me],
            device_id=(partner, row - 1), device_id_type=MESH,
        )

    def down_copy(j):
        partner = lax.rem(me + j, views)
        return pltpu.make_async_remote_copy(
            src_ref=send_win.at[partner, pl.ds(rows - EDGE, EDGE)],
            dst_ref=recv_win.at[me, pl.ds(0, EDGE)],
            send_sem=down_send.at[j], recv_sem=down_recv.at[me],
            device_id=(partner, row + 1), device_id_type=MESH,
        )

    def layer_copy(up):
        return pltpu.make_async_remote_copy(
            src_ref=halo_out.at[0 if up else 1], dst_ref=halo_in.at[1 if up else 0],
            send_sem=lh_send.at[0 if up else 1], recv_sem=lh_recv.at[1 if up else 0],
            device_id=(me, row - 1 if up else row + 1), device_id_type=MESH,
        )

    def arrived(dst, sem):
        return pltpu.make_async_remote_copy(
            src_ref=dst, dst_ref=dst, send_sem=sem, recv_sem=sem,
            device_id=(me, row), device_id_type=MESH,
        ).wait_recv()

    pl.semaphore_wait(
        barrier, views - 1 + views * (above.astype(jnp.int32) + below.astype(jnp.int32))
    )

    def send_shift(j, carry):
        shift_copy(j).start()
        return carry

    lax.fori_loop(1, views, send_shift, 0)

    def send_all(j, carry):
        @pl.when(j > 0)
        def _():
            win_copy(j).start()

        @pl.when(above)
        def _():
            up_copy(j).start()

        @pl.when(below)
        def _():
            down_copy(j).start()

        return carry

    lax.fori_loop(0, views, send_all, 0)

    fetch_layers.wait()
    for f in range(frames):
        for k in range(layer_count):
            def load(tile):
                where = pl.ds(pl.multiple_of(tile * LANES, LANES), LANES)
                return layers_ref[f, k, :, where].astype(jnp.float32)

            plane = window(load, me)
            at = f * layer_count + k
            layer_win[at, EDGE : EDGE + rows, :] = plane
            halo_out[0, at] = plane[:EDGE].astype(jnp.bfloat16)
            halo_out[1, at] = plane[rows - EDGE :].astype(jnp.bfloat16)

    @pl.when(above)
    def _():
        layer_copy(True).start()

    @pl.when(below)
    def _():
        layer_copy(False).start()

    @pl.when(jnp.logical_not(above))
    def _():
        recv_win[:, :EDGE, :] = jnp.zeros((views, EDGE, LANES), jnp.bfloat16)
        layer_win[:, :EDGE, :] = jnp.zeros((planes, EDGE, LANES), jnp.float32)

    @pl.when(jnp.logical_not(below))
    def _():
        recv_win[:, EDGE + rows :, :] = jnp.zeros((views, EDGE, LANES), jnp.bfloat16)
        layer_win[:, EDGE + rows :, :] = jnp.zeros((planes, EDGE, LANES), jnp.float32)

    at_row = rows * row - HALO + lax.broadcasted_iota(jnp.int32, (inner, LANES), 0)
    at_col = strip * me - MARGIN + lax.broadcasted_iota(jnp.int32, (inner, LANES), 1)
    inside = (at_row >= 0) & (at_row < rows * rows_of) & (at_col >= 0) & (at_col < cols)
    third_win[...] = jnp.where(inside, 1.0 / frames, 0.0)
    upper[...] = jnp.zeros_like(upper)
    lower[...] = jnp.zeros_like(lower)

    def wait_shift(j, carry):
        source = lax.rem(me + views - j, views)
        arrived(shift_in.at[source], shift_recv.at[source])
        return carry

    lax.fori_loop(1, views, wait_shift, 0)
    to_smem = pltpu.make_async_copy(shift_in, shift_smem, smem_sem)
    to_smem.start()

    @pl.when(above)
    def _():
        arrived(halo_in.at[0], lh_recv.at[0])
        layer_win[:, :EDGE, :] = halo_in[0].astype(jnp.float32)

    @pl.when(below)
    def _():
        arrived(halo_in.at[1], lh_recv.at[1])
        layer_win[:, EDGE + rows :, :] = halo_in[1].astype(jnp.float32)

    to_smem.wait()

    def some_views(n, carry):
        views_now = []
        for b in range(BATCH):
            j = n * BATCH + b
            view = lax.rem(me + views - j, views)
            views_now.append(view)

            @pl.when(j > 0)
            def _():
                arrived(recv_win.at[view, pl.ds(EDGE, rows)], win_recv.at[view])

            @pl.when(above)
            def _():
                arrived(recv_win.at[view, pl.ds(0, EDGE)], down_recv.at[view])

            @pl.when(below)
            def _():
                arrived(recv_win.at[view, pl.ds(EDGE + rows, EDGE)], up_recv.at[view])

        row_shift, back = [], []
        for b, view in enumerate(views_now):
            target_win[b] = recv_win[view].astype(jnp.float32)
            row_now = [shift_smem[view, 0, 2 * k] for k in range(layer_count)]
            col_now = [shift_smem[view, 0, 2 * k + 1] for k in range(layer_count)]
            there = [lax.rem(LANES - c, LANES) for c in col_now]
            row_shift.append(row_now)
            back.append([lax.rem(LANES + c, LANES) for c in col_now])
            total = None
            for f in range(frames):
                seen = [
                    pltpu.roll(
                        layer_win[f * layer_count + k, pl.ds(EDGE - HALO + row_now[k], inner), :],
                        there[k], 1,
                    )
                    for k in range(layer_count)
                ]
                for k in range(layer_count):
                    rest = None
                    for i in range(layer_count):
                        if i != k:
                            rest = seen[i] if rest is None else rest * seen[i]
                    others_win[b, f * layer_count + k] = rest
                    if k == layer_count - 1:
                        whole = rest * seen[k]
                        total = whole if total is None else total + whole
            shown_win[b] = total * third_win[...]

        for k in range(layer_count):
            image, model = [], []
            for b in range(BATCH):
                turn, by = back[b][k], row_shift[b][k]
                image.append(pltpu.roll(target_win[b, pl.ds(EDGE - by, rows), :], turn, 1))
                model.append(pltpu.roll(shown_win[b, pl.ds(HALO - by, rows), :], turn, 1))
            for f in range(frames):
                at = f * layer_count + k
                up, low = upper[at], lower[at]
                for b in range(BATCH):
                    rest = pltpu.roll(
                        others_win[b, at, pl.ds(HALO - row_shift[b][k], rows), :], back[b][k], 1
                    )
                    up += image[b] * rest
                    low += model[b] * rest
                upper[at] = up
                lower[at] = low
        return carry

    lax.fori_loop(0, views // BATCH, some_views, 0)

    spare = packed.shape[0] - planes * short
    if spare:
        packed[planes * short :, :] = jnp.zeros((spare, LANES), jnp.float32)
    for at in range(planes):
        ratio = (upper[at] + REGULAR) / (lower[at] + REGULAR)
        value = (jnp.log(ratio) - middle) * (1.0 / step)
        merged = pltpu.roll(value[:short], LANES - MARGIN, 1)
        if groups == 2:
            merged = jnp.where(lane < strip, merged, pltpu.roll(value[short:], strip - MARGIN, 1))
        packed[at * short : (at + 1) * short, :] = merged
    slots[me] = jnp.round(packed[...]).astype(jnp.int32).astype(jnp.int16)

    core = lax.rem(me, 2)
    x = lax.rem(me // 2, across)
    z = me // (2 * across)

    def index(zz, xx, cc):
        return (zz * across + xx) * 2 + cc

    def slot_copy(slot, to, sem):
        return pltpu.make_async_remote_copy(
            src_ref=slots.at[slot], dst_ref=slots.at[slot], send_sem=sem,
            recv_sem=slot_recv.at[slot], device_id=(to, row), device_id_type=MESH,
        )

    def along(d):
        return index(z + d, x, core)

    def to_column(d):
        return slot_copy(me, index(z + d, x, core), col_send.at[depth + d])

    def to_across(d, dx):
        return slot_copy(
            along(d), index(z, lax.rem(x + dx, across), core), x_send.at[depth + d, dx]
        )

    def to_core(d, dx):
        slot = index(z + d, lax.rem(x + across - dx, across), core)
        return slot_copy(slot, index(z, x, 1 - core), core_send.at[depth + d, dx])

    def exists(d):
        return (z + d >= 0) & (z + d < depth)

    def visit(d, act):
        if d:
            pl.when(exists(d))(act)
        else:
            act()

    def both_ways(d):
        return (-d, d) if d else (0,)

    def each_copy(d, act):
        if d:
            act(to_column(d))
        for dx in range(1, across):
            act(to_across(d, dx))
        act(to_core(d, 0))

    def spread(d):
        for dx in range(1, across):
            to_across(d, dx).start()
        to_core(d, 0).start()

    def column_step(d):
        def act():
            slot = along(d)
            arrived(slots.at[slot], slot_recv.at[slot])
            spread(d)

        visit(d, act)

    def across_step(d):
        def act():
            for dx in range(1, across):
                slot = index(z + d, lax.rem(x + across - dx, across), core)
                arrived(slots.at[slot], slot_recv.at[slot])
                to_core(d, dx).start()

        visit(d, act)

    for distance in range(depth - 1, 0, -1):
        for d in both_ways(distance):
            def act():
                to_column(d).start()

            visit(d, act)
    spread(0)

    @pl.when(above)
    def _():
        layer_copy(True).wait_send()

    @pl.when(below)
    def _():
        layer_copy(False).wait_send()

    def finish(j, carry):
        @pl.when(j > 0)
        def _():
            shift_copy(j).wait_send()
            win_copy(j).wait_send()

        @pl.when(above)
        def _():
            up_copy(j).wait_send()

        @pl.when(below)
        def _():
            down_copy(j).wait_send()

        return carry

    lax.fori_loop(0, views, finish, 0)

    for distance in range(1, depth):
        for d in both_ways(distance):
            column_step(d)
        for d in both_ways(distance - 1):
            across_step(d)

    per_tile = LANES // strip

    def store_tile(tile):
        where = pl.ds(pl.multiple_of(tile * LANES, LANES), LANES)
        return pltpu.make_async_copy(
            out_ref.at[:, :, :, where], out_hbm.at[:, :, :, where], store_sem.at[tile]
        )

    def unpack(tile):
        for i in range(per_tile):
            @pl.when(lax.rem(tile * per_tile + i, 2) != core)
            def _():
                slot = tile * per_tile + i
                arrived(slots.at[slot], slot_recv.at[slot])

        where = pl.ds(pl.multiple_of(tile * LANES, LANES), LANES)
        parts = [slots[tile * per_tile + i].astype(jnp.int32) for i in range(per_tile)]
        for f in range(frames):
            for k in range(layer_count):
                at = f * layer_count + k
                spans = []
                for g in range(groups):
                    code = None
                    for i in range(per_tile):
                        part = parts[i][at * short : (at + 1) * short]
                        turn = (strip * (i - g)) % LANES
                        if turn:
                            part = pltpu.roll(part, turn, 1)
                        code = part if code is None else jnp.where(lane < strip * i, code, part)
                    spans.append(code)
                whole = jnp.concatenate(spans, axis=0) if groups > 1 else spans[0]
                out_ref[f, k, :, where] = whole.astype(jnp.int16)
        store_tile(tile).start()

    early = strip == 64

    def unpack_column(n, carry):
        unpack(n * across + x)
        return carry

    if early:
        lax.fori_loop(0, depth, unpack_column, 0)
    for d in both_ways(depth - 1):
        across_step(d)

    def unpack_rest(n, carry):
        zz, dx = n // (across - 1), lax.rem(n, across - 1) + 1
        unpack(zz * across + lax.rem(x + dx, across))
        return carry

    def unpack_any(n, carry):
        unpack(n)
        return carry

    if early:
        lax.fori_loop(0, depth * (across - 1), unpack_rest, 0)
    else:
        lax.fori_loop(0, tiles, unpack_any, 0)

    for distance in range(depth):
        for d in both_ways(distance):
            def act():
                each_copy(d, lambda copy: copy.wait_send())
                for dx in range(1, across):
                    to_core(d, dx).wait_send()

            visit(d, act)

    def wait_store(tile, carry):
        store_tile(tile).wait()
        return carry

    lax.fori_loop(0, tiles, wait_store, 0)


def body(views, rows_of, layers, target, shifts):
    frames, layer_count, rows, cols = layers.shape
    planes = frames * layer_count
    strip = cols // views
    groups = 2 if strip == 64 else 1
    depth, across = split_views(views)
    packed_rows = -(-planes * (rows // groups) // 16) * 16
    height, inner = rows + 2 * EDGE, rows + 2 * HALO
    dma = pltpu.SemaphoreType.DMA
    f32, bf16 = jnp.float32, jnp.bfloat16
    codes = pl.pallas_call(
        functools.partial(kernel, views, rows_of),
        out_shape=jax.ShapeDtypeStruct(layers.shape, jnp.int16),
        in_specs=[
            pl.BlockSpec(memory_space=pltpu.HBM),
            pl.BlockSpec(memory_space=pltpu.HBM),
            pl.BlockSpec(memory_space=pltpu.HBM),
        ],
        out_specs=pl.BlockSpec(memory_space=pltpu.HBM),
        scratch_shapes=[
            pltpu.SMEM((1, 2, layer_count), jnp.int32),
            pltpu.VMEM(layers.shape, bf16),
            pltpu.VMEM(target.shape, bf16),
            pltpu.VMEM(layers.shape, jnp.int16),
            dma((3,)),
            dma((cols // LANES,)),
            pltpu.VMEM((views, rows, LANES), bf16),
            pltpu.VMEM((views, height, LANES), bf16),
            pltpu.VMEM((1, LANES), jnp.int32),
            pltpu.VMEM((views, 1, LANES), jnp.int32),
            pltpu.SMEM((views, 1, LANES), jnp.int32),
            pltpu.VMEM((2, planes, EDGE, LANES), bf16),
            pltpu.VMEM((2, planes, EDGE, LANES), bf16),
            pltpu.VMEM((planes, height, LANES), f32),
            pltpu.VMEM((BATCH, height, LANES), f32),
            pltpu.VMEM((BATCH, planes, inner, LANES), f32),
            pltpu.VMEM((BATCH, inner, LANES), f32),
            pltpu.VMEM((inner, LANES), f32),
            pltpu.VMEM((planes, rows, LANES), f32),
            pltpu.VMEM((planes, rows, LANES), f32),
            pltpu.VMEM((packed_rows, LANES), f32),
            pltpu.VMEM((views, packed_rows, LANES), jnp.int16),
            dma((views,)), dma((views,)), dma((views,)), dma((views,)), dma((views,)), dma((views,)),
            dma((views,)), dma((views,)), dma, dma((2,)), dma((2,)),
            dma((2 * depth,)), dma((2 * depth, across)), dma((2 * depth, across)), dma((views,)),
        ],
        compiler_params=pltpu.CompilerParams(
            collective_id=0, has_side_effects=True, vmem_limit_bytes=62 * 1024 * 1024
        ),
        name="light_field_update",
    )(jnp.swapaxes(shifts, 1, 2), layers, target)
    middle, step = code_range(views)
    return layers.astype(f32) * jnp.exp(codes.astype(f32) * step + middle)


def solution(mesh):
    placed = (P(None, None, "row", None), P("view", "row", None), P("view", None, None))
    return jax.shard_map(
        functools.partial(body, mesh.shape["view"], mesh.shape["row"]),
        mesh=mesh, in_specs=placed, out_specs=P(None, None, "row", None), check_vma=False,
    )
```

```python
import functools
import math

import jax
import jax.numpy as jnp
from jax import lax
from jax.experimental import pallas as pl
from jax.experimental.pallas import tpu as pltpu
from jax.sharding import PartitionSpec as P

HALO = 8
LANES = 128
EDGE = 16
MARGIN = 32
REGULAR = 0.05
BATCH = 4
MESH = pl.DeviceIdType.MESH


def split_views(views):
    across = 1
    while (2 * across) ** 2 * 2 <= views:
        across *= 2
    return views // (2 * across), across


def code_range(views):
    low = math.log(REGULAR / (views + REGULAR))
    high = math.log((0.5 * views + REGULAR) / REGULAR)
    return 0.5 * (low + high), (high - low) / 65000.0


def kernel(
    views, rows_of, shifts_hbm, layers_hbm, target_hbm, out_hbm,
    shifts_ref, layers_ref, target_ref, out_ref, fetch_sem, store_sem,
    send_win, recv_win, shift_out, shift_in, shift_smem, halo_out, halo_in,
    layer_win, target_win, others_win, shown_win, third_win, upper, lower, packed, slots,
    win_send, win_recv, up_send, up_recv, down_send, down_recv,
    shift_send, shift_recv, smem_sem, lh_send, lh_recv,
    col_send, x_send, core_send, slot_recv,
):
    fetch_shifts = pltpu.make_async_copy(shifts_hbm, shifts_ref, fetch_sem.at[0])
    fetch_target = pltpu.make_async_copy(target_hbm, target_ref, fetch_sem.at[1])
    fetch_layers = pltpu.make_async_copy(layers_hbm, layers_ref, fetch_sem.at[2])
    fetch_shifts.start()
    fetch_target.start()
    fetch_layers.start()

    frames, layer_count, rows, cols = layers_ref.shape
    strip = cols // views
    planes = frames * layer_count
    height = rows + 2 * EDGE
    inner = rows + 2 * HALO
    depth, across = split_views(views)
    groups = 2 if strip == 64 else 1
    short = rows // groups
    tiles = cols // LANES
    middle, step = code_range(views)

    me = lax.axis_index("view")
    row = lax.axis_index("row")
    above, below = row > 0, row < rows_of - 1

    barrier = pltpu.get_barrier_semaphore()

    def greet(j, carry):
        partner = lax.rem(me + j, views)

        @pl.when(j > 0)
        def _():
            pl.semaphore_signal(barrier, inc=1, device_id=(partner, row), device_id_type=MESH)

        @pl.when(above)
        def _():
            pl.semaphore_signal(barrier, inc=1, device_id=(partner, row - 1), device_id_type=MESH)

        @pl.when(below)
        def _():
            pl.semaphore_signal(barrier, inc=1, device_id=(partner, row + 1), device_id_type=MESH)

        return carry

    lax.fori_loop(0, views, greet, 0, unroll=4)

    lane = lax.broadcasted_iota(jnp.int32, (1, LANES), 1)

    def window(load, index):
        start = strip * index - MARGIN
        tile = (start + LANES) // LANES - 1
        offset = start - tile * LANES
        first = load(jnp.maximum(tile, 0))
        second = load(jnp.minimum(tile + 1, tiles - 1))
        turn = lax.rem(LANES - offset, LANES)
        first = pltpu.roll(first, turn, 1)
        second = pltpu.roll(second, turn, 1)
        both = jnp.where(lane < LANES - offset, first, second)
        col = start + lane
        return jnp.where((col >= 0) & (col < cols), both, 0.0)

    fetch_shifts.wait()
    place = lax.broadcasted_iota(jnp.int32, (1, LANES), 1)
    block = jnp.zeros((1, LANES), jnp.int32)
    for k in range(layer_count):
        for axis in range(2):
            block = jnp.where(place == 2 * k + axis, shifts_ref[0, axis, k], block)
    shift_out[...] = block
    shift_in[me] = block

    fetch_target.wait()

    def fill(c, carry):
        def load(tile):
            where = pl.ds(pl.multiple_of(tile * LANES, LANES), LANES)
            return target_ref[0, :, where].astype(jnp.float32)

        send_win[c] = window(load, c).astype(jnp.bfloat16)
        return carry

    lax.fori_loop(0, views, fill, 0, unroll=8)
    recv_win[me, EDGE : EDGE + rows, :] = send_win[me]

    def shift_copy(j):
        partner = lax.rem(me + j, views)
        return pltpu.make_async_remote_copy(
            src_ref=shift_out, dst_ref=shift_in.at[me], send_sem=shift_send.at[j],
            recv_sem=shift_recv.at[me], device_id=(partner, row), device_id_type=MESH,
        )

    def win_copy(j):
        partner = lax.rem(me + j, views)
        return pltpu.make_async_remote_copy(
            src_ref=send_win.at[partner], dst_ref=recv_win.at[me, pl.ds(EDGE, rows)],
            send_sem=win_send.at[j], recv_sem=win_recv.at[me],
            device_id=(partner, row), device_id_type=MESH,
        )

    def up_copy(j):
        partner = lax.rem(me + j, views)
        return pltpu.make_async_remote_copy(
            src_ref=send_win.at[partner, pl.ds(0, EDGE)],
            dst_ref=recv_win.at[me, pl.ds(EDGE + rows, EDGE)],
            send_sem=up_send.at[j], recv_sem=up_recv.at[me],
            device_id=(partner, row - 1), device_id_type=MESH,
        )

    def down_copy(j):
        partner = lax.rem(me + j, views)
        return pltpu.make_async_remote_copy(
            src_ref=send_win.at[partner, pl.ds(rows - EDGE, EDGE)],
            dst_ref=recv_win.at[me, pl.ds(0, EDGE)],
            send_sem=down_send.at[j], recv_sem=down_recv.at[me],
            device_id=(partner, row + 1), device_id_type=MESH,
        )

    def layer_copy(up):
        return pltpu.make_async_remote_copy(
            src_ref=halo_out.at[0 if up else 1], dst_ref=halo_in.at[1 if up else 0],
            send_sem=lh_send.at[0 if up else 1], recv_sem=lh_recv.at[1 if up else 0],
            device_id=(me, row - 1 if up else row + 1), device_id_type=MESH,
        )

    def arrived(dst, sem):
        return pltpu.make_async_remote_copy(
            src_ref=dst, dst_ref=dst, send_sem=sem, recv_sem=sem,
            device_id=(me, row), device_id_type=MESH,
        ).wait_recv()

    pl.semaphore_wait(
        barrier, views - 1 + views * (above.astype(jnp.int32) + below.astype(jnp.int32))
    )

    def send_shift(j, carry):
        shift_copy(j).start()
        return carry

    lax.fori_loop(1, views, send_shift, 0)

    def send_all(j, carry):
        @pl.when(j > 0)
        def _():
            win_copy(j).start()

        @pl.when(above)
        def _():
            up_copy(j).start()

        @pl.when(below)
        def _():
            down_copy(j).start()

        return carry

    lax.fori_loop(0, views, send_all, 0)

    fetch_layers.wait()
    for f in range(frames):
        for k in range(layer_count):
            def load(tile):
                where = pl.ds(pl.multiple_of(tile * LANES, LANES), LANES)
                return layers_ref[f, k, :, where].astype(jnp.float32)

            plane = window(load, me)
            at = f * layer_count + k
            layer_win[at, EDGE : EDGE + rows, :] = plane
            halo_out[0, at] = plane[:EDGE].astype(jnp.bfloat16)
            halo_out[1, at] = plane[rows - EDGE :].astype(jnp.bfloat16)

    @pl.when(above)
    def _():
        layer_copy(True).start()

    @pl.when(below)
    def _():
        layer_copy(False).start()

    @pl.when(jnp.logical_not(above))
    def _():
        recv_win[:, :EDGE, :] = jnp.zeros((views, EDGE, LANES), jnp.bfloat16)
        layer_win[:, :EDGE, :] = jnp.zeros((planes, EDGE, LANES), jnp.float32)

    @pl.when(jnp.logical_not(below))
    def _():
        recv_win[:, EDGE + rows :, :] = jnp.zeros((views, EDGE, LANES), jnp.bfloat16)
        layer_win[:, EDGE + rows :, :] = jnp.zeros((planes, EDGE, LANES), jnp.float32)

    at_row = rows * row - HALO + lax.broadcasted_iota(jnp.int32, (inner, LANES), 0)
    at_col = strip * me - MARGIN + lax.broadcasted_iota(jnp.int32, (inner, LANES), 1)
    inside = (at_row >= 0) & (at_row < rows * rows_of) & (at_col >= 0) & (at_col < cols)
    third_win[...] = jnp.where(inside, 1.0 / frames, 0.0)
    upper[...] = jnp.zeros_like(upper)
    lower[...] = jnp.zeros_like(lower)

    def wait_shift(j, carry):
        source = lax.rem(me + views - j, views)
        arrived(shift_in.at[source], shift_recv.at[source])
        return carry

    lax.fori_loop(1, views, wait_shift, 0)
    to_smem = pltpu.make_async_copy(shift_in, shift_smem, smem_sem)
    to_smem.start()

    @pl.when(above)
    def _():
        arrived(halo_in.at[0], lh_recv.at[0])
        layer_win[:, :EDGE, :] = halo_in[0].astype(jnp.float32)

    @pl.when(below)
    def _():
        arrived(halo_in.at[1], lh_recv.at[1])
        layer_win[:, EDGE + rows :, :] = halo_in[1].astype(jnp.float32)

    to_smem.wait()

    def some_views(n, carry):
        views_now = []
        for b in range(BATCH):
            j = n * BATCH + b
            view = lax.rem(me + views - j, views)
            views_now.append(view)

            @pl.when(j > 0)
            def _():
                arrived(recv_win.at[view, pl.ds(EDGE, rows)], win_recv.at[view])

            @pl.when(above)
            def _():
                arrived(recv_win.at[view, pl.ds(0, EDGE)], down_recv.at[view])

            @pl.when(below)
            def _():
                arrived(recv_win.at[view, pl.ds(EDGE + rows, EDGE)], up_recv.at[view])

        row_shift, back = [], []
        for b, view in enumerate(views_now):
            target_win[b] = recv_win[view].astype(jnp.float32)
            row_now = [shift_smem[view, 0, 2 * k] for k in range(layer_count)]
            col_now = [shift_smem[view, 0, 2 * k + 1] for k in range(layer_count)]
            there = [lax.rem(LANES - c, LANES) for c in col_now]
            row_shift.append(row_now)
            back.append([lax.rem(LANES + c, LANES) for c in col_now])
            total = None
            for f in range(frames):
                seen = [
                    pltpu.roll(
                        layer_win[f * layer_count + k, pl.ds(EDGE - HALO + row_now[k], inner), :],
                        there[k], 1,
                    )
                    for k in range(layer_count)
                ]
                for k in range(layer_count):
                    rest = None
                    for i in range(layer_count):
                        if i != k:
                            rest = seen[i] if rest is None else rest * seen[i]
                    others_win[b, f * layer_count + k] = rest
                    if k == layer_count - 1:
                        whole = rest * seen[k]
                        total = whole if total is None else total + whole
            shown_win[b] = total * third_win[...]

        for k in range(layer_count):
            image, model = [], []
            for b in range(BATCH):
                turn, by = back[b][k], row_shift[b][k]
                image.append(pltpu.roll(target_win[b, pl.ds(EDGE - by, rows), :], turn, 1))
                model.append(pltpu.roll(shown_win[b, pl.ds(HALO - by, rows), :], turn, 1))
            for f in range(frames):
                at = f * layer_count + k
                up, low = upper[at], lower[at]
                for b in range(BATCH):
                    rest = pltpu.roll(
                        others_win[b, at, pl.ds(HALO - row_shift[b][k], rows), :], back[b][k], 1
                    )
                    up += image[b] * rest
                    low += model[b] * rest
                upper[at] = up
                lower[at] = low
        return carry

    lax.fori_loop(0, views // BATCH, some_views, 0)

    spare = packed.shape[0] - planes * short
    if spare:
        packed[planes * short :, :] = jnp.zeros((spare, LANES), jnp.float32)
    for at in range(planes):
        ratio = (upper[at] + REGULAR) / (lower[at] + REGULAR)
        value = (jnp.log(ratio) - middle) * (1.0 / step)
        merged = pltpu.roll(value[:short], LANES - MARGIN, 1)
        if groups == 2:
            merged = jnp.where(lane < strip, merged, pltpu.roll(value[short:], strip - MARGIN, 1))
        packed[at * short : (at + 1) * short, :] = merged
    slots[me] = jnp.round(packed[...]).astype(jnp.int32).astype(jnp.int16)

    core = lax.rem(me, 2)
    x = lax.rem(me // 2, across)
    z = me // (2 * across)

    def index(zz, xx, cc):
        return (zz * across + xx) * 2 + cc

    def slot_copy(slot, to, sem):
        return pltpu.make_async_remote_copy(
            src_ref=slots.at[slot], dst_ref=slots.at[slot], send_sem=sem,
            recv_sem=slot_recv.at[slot], device_id=(to, row), device_id_type=MESH,
        )

    def along(d):
        return index(z + d, x, core)

    def to_column(d):
        return slot_copy(me, index(z + d, x, core), col_send.at[depth + d])

    def to_across(d, dx):
        return slot_copy(
            along(d), index(z, lax.rem(x + dx, across), core), x_send.at[depth + d, dx]
        )

    def to_core(d, dx):
        slot = index(z + d, lax.rem(x + across - dx, across), core)
        return slot_copy(slot, index(z, x, 1 - core), core_send.at[depth + d, dx])

    def exists(d):
        return (z + d >= 0) & (z + d < depth)

    def visit(d, act):
        if d:
            pl.when(exists(d))(act)
        else:
            act()

    def both_ways(d):
        return (-d, d) if d else (0,)

    def each_copy(d, act):
        if d:
            act(to_column(d))
        for dx in range(1, across):
            act(to_across(d, dx))
        act(to_core(d, 0))

    def spread(d):
        for dx in range(1, across):
            to_across(d, dx).start()
        to_core(d, 0).start()

    def column_step(d):
        def act():
            slot = along(d)
            arrived(slots.at[slot], slot_recv.at[slot])
            spread(d)

        visit(d, act)

    def across_step(d):
        def act():
            for dx in range(1, across):
                slot = index(z + d, lax.rem(x + across - dx, across), core)
                arrived(slots.at[slot], slot_recv.at[slot])
                to_core(d, dx).start()

        visit(d, act)

    for distance in range(depth - 1, 0, -1):
        for d in both_ways(distance):
            def act():
                to_column(d).start()

            visit(d, act)
    spread(0)

    @pl.when(above)
    def _():
        layer_copy(True).wait_send()

    @pl.when(below)
    def _():
        layer_copy(False).wait_send()

    def finish(j, carry):
        @pl.when(j > 0)
        def _():
            shift_copy(j).wait_send()
            win_copy(j).wait_send()

        @pl.when(above)
        def _():
            up_copy(j).wait_send()

        @pl.when(below)
        def _():
            down_copy(j).wait_send()

        return carry

    lax.fori_loop(0, views, finish, 0)

    for distance in range(1, depth):
        for d in both_ways(distance):
            column_step(d)
        for d in both_ways(distance - 1):
            across_step(d)

    per_tile = LANES // strip

    def store_tile(tile):
        where = pl.ds(pl.multiple_of(tile * LANES, LANES), LANES)
        return pltpu.make_async_copy(
            out_ref.at[:, :, :, where], out_hbm.at[:, :, :, where], store_sem.at[tile]
        )

    def unpack(tile):
        for i in range(per_tile):
            @pl.when(lax.rem(tile * per_tile + i, 2) != core)
            def _():
                slot = tile * per_tile + i
                arrived(slots.at[slot], slot_recv.at[slot])

        where = pl.ds(pl.multiple_of(tile * LANES, LANES), LANES)
        parts = [slots[tile * per_tile + i].astype(jnp.int32) for i in range(per_tile)]
        for f in range(frames):
            for k in range(layer_count):
                at = f * layer_count + k
                spans = []
                for g in range(groups):
                    code = None
                    for i in range(per_tile):
                        part = parts[i][at * short : (at + 1) * short]
                        turn = (strip * (i - g)) % LANES
                        if turn:
                            part = pltpu.roll(part, turn, 1)
                        code = part if code is None else jnp.where(lane < strip * i, code, part)
                    spans.append(code)
                whole = jnp.concatenate(spans, axis=0) if groups > 1 else spans[0]
                out_ref[f, k, :, where] = whole.astype(jnp.int16)
        store_tile(tile).start()

    early = strip == 64

    def unpack_column(n, carry):
        unpack(n * across + x)
        return carry

    if early:
        lax.fori_loop(0, depth, unpack_column, 0)
    for d in both_ways(depth - 1):
        across_step(d)

    def unpack_rest(n, carry):
        zz, dx = n // (across - 1), lax.rem(n, across - 1) + 1
        unpack(zz * across + lax.rem(x + dx, across))
        return carry

    def unpack_any(n, carry):
        unpack(n)
        return carry

    if early:
        lax.fori_loop(0, depth * (across - 1), unpack_rest, 0)
    else:
        lax.fori_loop(0, tiles, unpack_any, 0)

    for distance in range(depth):
        for d in both_ways(distance):
            def act():
                each_copy(d, lambda copy: copy.wait_send())
                for dx in range(1, across):
                    to_core(d, dx).wait_send()

            visit(d, act)

    def wait_store(tile, carry):
        store_tile(tile).wait()
        return carry

    lax.fori_loop(0, tiles, wait_store, 0)


def decode(views, codes_hbm, layers_hbm, out_hbm, codes, layers, out, sems):
    frames, layer_count = layers.shape[:2]
    middle, step = code_range(views)
    moves = []
    for f in range(frames):
        for k in range(layer_count):
            at = f * layer_count + k
            moves.append((
                pltpu.make_async_copy(codes_hbm.at[f, k], codes.at[f, k], sems.at[0, at]),
                pltpu.make_async_copy(layers_hbm.at[f, k], layers.at[f, k], sems.at[1, at]),
                pltpu.make_async_copy(out.at[f, k], out_hbm.at[f, k], sems.at[2, at]),
            ))
    for code_in, layer_in, _ in moves:
        code_in.start()
        layer_in.start()
    for at, (code_in, layer_in, store) in enumerate(moves):
        f, k = at // layer_count, at % layer_count
        code_in.wait()
        layer_in.wait()
        ratio = jnp.exp(codes[f, k].astype(jnp.int32).astype(jnp.float32) * step + middle)
        out[f, k] = layers[f, k].astype(jnp.float32) * ratio
        store.start()
    for _, _, store in moves:
        store.wait()


def body(views, rows_of, layers, target, shifts):
    frames, layer_count, rows, cols = layers.shape
    planes = frames * layer_count
    strip = cols // views
    groups = 2 if strip == 64 else 1
    depth, across = split_views(views)
    packed_rows = -(-planes * (rows // groups) // 16) * 16
    height, inner = rows + 2 * EDGE, rows + 2 * HALO
    dma = pltpu.SemaphoreType.DMA
    f32, bf16 = jnp.float32, jnp.bfloat16
    codes = pl.pallas_call(
        functools.partial(kernel, views, rows_of),
        out_shape=jax.ShapeDtypeStruct(layers.shape, jnp.int16),
        in_specs=[
            pl.BlockSpec(memory_space=pltpu.HBM),
            pl.BlockSpec(memory_space=pltpu.HBM),
            pl.BlockSpec(memory_space=pltpu.HBM),
        ],
        out_specs=pl.BlockSpec(memory_space=pltpu.HBM),
        scratch_shapes=[
            pltpu.SMEM((1, 2, layer_count), jnp.int32),
            pltpu.VMEM(layers.shape, bf16),
            pltpu.VMEM(target.shape, bf16),
            pltpu.VMEM(layers.shape, jnp.int16),
            dma((3,)),
            dma((cols // LANES,)),
            pltpu.VMEM((views, rows, LANES), bf16),
            pltpu.VMEM((views, height, LANES), bf16),
            pltpu.VMEM((1, LANES), jnp.int32),
            pltpu.VMEM((views, 1, LANES), jnp.int32),
            pltpu.SMEM((views, 1, LANES), jnp.int32),
            pltpu.VMEM((2, planes, EDGE, LANES), bf16),
            pltpu.VMEM((2, planes, EDGE, LANES), bf16),
            pltpu.VMEM((planes, height, LANES), f32),
            pltpu.VMEM((BATCH, height, LANES), f32),
            pltpu.VMEM((BATCH, planes, inner, LANES), f32),
            pltpu.VMEM((BATCH, inner, LANES), f32),
            pltpu.VMEM((inner, LANES), f32),
            pltpu.VMEM((planes, rows, LANES), f32),
            pltpu.VMEM((planes, rows, LANES), f32),
            pltpu.VMEM((packed_rows, LANES), f32),
            pltpu.VMEM((views, packed_rows, LANES), jnp.int16),
            dma((views,)), dma((views,)), dma((views,)), dma((views,)), dma((views,)), dma((views,)),
            dma((views,)), dma((views,)), dma, dma((2,)), dma((2,)),
            dma((2 * depth,)), dma((2 * depth, across)), dma((2 * depth, across)), dma((views,)),
        ],
        compiler_params=pltpu.CompilerParams(
            collective_id=0, has_side_effects=True, vmem_limit_bytes=62 * 1024 * 1024
        ),
        name="light_field_update",
    )(jnp.swapaxes(shifts, 1, 2), layers, target)
    return pl.pallas_call(
        functools.partial(decode, views),
        out_shape=jax.ShapeDtypeStruct(layers.shape, f32),
        in_specs=[pl.BlockSpec(memory_space=pltpu.HBM)] * 2,
        out_specs=pl.BlockSpec(memory_space=pltpu.HBM),
        scratch_shapes=[
            pltpu.VMEM(layers.shape, jnp.int16),
            pltpu.VMEM(layers.shape, bf16),
            pltpu.VMEM(layers.shape, f32),
            dma((3, planes)),
        ],
        compiler_params=pltpu.CompilerParams(vmem_limit_bytes=62 * 1024 * 1024),
        name="decode_ratio",
    )(codes, layers)


def solution(mesh):
    placed = (P(None, None, "row", None), P("view", "row", None), P("view", None, None))
    return jax.shard_map(
        functools.partial(body, mesh.shape["view"], mesh.shape["row"]),
        mesh=mesh, in_specs=placed, out_specs=P(None, None, "row", None), check_vma=False,
    )
```

```python
import functools
import math

import jax
import jax.numpy as jnp
from jax import lax
from jax.experimental import pallas as pl
from jax.experimental.pallas import tpu as pltpu
from jax.sharding import PartitionSpec as P

HALO = 8
LANES = 128
EDGE = 16
MARGIN = 32
REGULAR = 0.05
BATCH = 4
MESH = pl.DeviceIdType.MESH


def split_views(views):
    across = 1
    while (2 * across) ** 2 * 2 <= views:
        across *= 2
    return views // (2 * across), across


def code_range(views):
    low = math.log(REGULAR / (views + REGULAR))
    high = math.log((0.5 * views + REGULAR) / REGULAR)
    return 0.5 * (low + high), (high - low) / 65000.0


def kernel(
    views, rows_of, shifts_hbm, layers_hbm, target_hbm, out_hbm,
    shifts_ref, layers_ref, target_ref, out_ref, fetch_sem, store_sem,
    send_win, recv_win, shift_out, shift_in, shift_smem, halo_out, halo_in,
    layer_win, target_win, others_win, shown_win, third_win, upper, lower, packed, slots,
    win_send, win_recv, up_send, up_recv, down_send, down_recv,
    shift_send, shift_recv, smem_sem, lh_send, lh_recv,
    col_send, x_send, core_send, slot_recv,
):
    fetch_shifts = pltpu.make_async_copy(shifts_hbm, shifts_ref, fetch_sem.at[0])
    fetch_target = pltpu.make_async_copy(target_hbm, target_ref, fetch_sem.at[1])
    fetch_layers = pltpu.make_async_copy(layers_hbm, layers_ref, fetch_sem.at[2])
    fetch_shifts.start()
    fetch_target.start()
    fetch_layers.start()

    frames, layer_count, rows, cols = layers_ref.shape
    strip = cols // views
    planes = frames * layer_count
    height = rows + 2 * EDGE
    inner = rows + 2 * HALO
    depth, across = split_views(views)
    groups = 2 if strip == 64 else 1
    short = rows // groups
    tiles = cols // LANES
    middle, step = code_range(views)

    me = lax.axis_index("view")
    row = lax.axis_index("row")
    above, below = row > 0, row < rows_of - 1

    barrier = pltpu.get_barrier_semaphore()

    def greet(j, carry):
        partner = lax.rem(me + j, views)

        @pl.when(j > 0)
        def _():
            pl.semaphore_signal(barrier, inc=1, device_id=(partner, row), device_id_type=MESH)

        @pl.when(above)
        def _():
            pl.semaphore_signal(barrier, inc=1, device_id=(partner, row - 1), device_id_type=MESH)

        @pl.when(below)
        def _():
            pl.semaphore_signal(barrier, inc=1, device_id=(partner, row + 1), device_id_type=MESH)

        return carry

    lax.fori_loop(0, views, greet, 0, unroll=4)

    lane = lax.broadcasted_iota(jnp.int32, (1, LANES), 1)

    def window(load, index):
        start = strip * index - MARGIN
        tile = (start + LANES) // LANES - 1
        offset = start - tile * LANES
        first = load(jnp.maximum(tile, 0))
        second = load(jnp.minimum(tile + 1, tiles - 1))
        turn = lax.rem(LANES - offset, LANES)
        first = pltpu.roll(first, turn, 1)
        second = pltpu.roll(second, turn, 1)
        both = jnp.where(lane < LANES - offset, first, second)
        col = start + lane
        return jnp.where((col >= 0) & (col < cols), both, 0.0)

    fetch_shifts.wait()
    place = lax.broadcasted_iota(jnp.int32, (1, LANES), 1)
    block = jnp.zeros((1, LANES), jnp.int32)
    for k in range(layer_count):
        for axis in range(2):
            block = jnp.where(place == 2 * k + axis, shifts_ref[0, axis, k], block)
    shift_out[...] = block
    shift_in[me] = block

    fetch_target.wait()

    def fill(c, carry):
        def load(tile):
            where = pl.ds(pl.multiple_of(tile * LANES, LANES), LANES)
            return target_ref[0, :, where].astype(jnp.float32)

        send_win[c] = window(load, c).astype(jnp.bfloat16)
        return carry

    lax.fori_loop(0, views, fill, 0, unroll=8)
    recv_win[me, EDGE : EDGE + rows, :] = send_win[me]

    def shift_copy(j):
        partner = lax.rem(me + j, views)
        return pltpu.make_async_remote_copy(
            src_ref=shift_out, dst_ref=shift_in.at[me], send_sem=shift_send.at[j],
            recv_sem=shift_recv.at[me], device_id=(partner, row), device_id_type=MESH,
        )

    def win_copy(j):
        partner = lax.rem(me + j, views)
        return pltpu.make_async_remote_copy(
            src_ref=send_win.at[partner], dst_ref=recv_win.at[me, pl.ds(EDGE, rows)],
            send_sem=win_send.at[j], recv_sem=win_recv.at[me],
            device_id=(partner, row), device_id_type=MESH,
        )

    def up_copy(j):
        partner = lax.rem(me + j, views)
        return pltpu.make_async_remote_copy(
            src_ref=send_win.at[partner, pl.ds(0, EDGE)],
            dst_ref=recv_win.at[me, pl.ds(EDGE + rows, EDGE)],
            send_sem=up_send.at[j], recv_sem=up_recv.at[me],
            device_id=(partner, row - 1), device_id_type=MESH,
        )

    def down_copy(j):
        partner = lax.rem(me + j, views)
        return pltpu.make_async_remote_copy(
            src_ref=send_win.at[partner, pl.ds(rows - EDGE, EDGE)],
            dst_ref=recv_win.at[me, pl.ds(0, EDGE)],
            send_sem=down_send.at[j], recv_sem=down_recv.at[me],
            device_id=(partner, row + 1), device_id_type=MESH,
        )

    def layer_copy(up):
        return pltpu.make_async_remote_copy(
            src_ref=halo_out.at[0 if up else 1], dst_ref=halo_in.at[1 if up else 0],
            send_sem=lh_send.at[0 if up else 1], recv_sem=lh_recv.at[1 if up else 0],
            device_id=(me, row - 1 if up else row + 1), device_id_type=MESH,
        )

    def arrived(dst, sem):
        return pltpu.make_async_remote_copy(
            src_ref=dst, dst_ref=dst, send_sem=sem, recv_sem=sem,
            device_id=(me, row), device_id_type=MESH,
        ).wait_recv()

    pl.semaphore_wait(
        barrier, views - 1 + views * (above.astype(jnp.int32) + below.astype(jnp.int32))
    )

    def send_shift(j, carry):
        shift_copy(j).start()
        return carry

    lax.fori_loop(1, views, send_shift, 0)

    def send_all(j, carry):
        @pl.when(j > 0)
        def _():
            win_copy(j).start()

        @pl.when(above)
        def _():
            up_copy(j).start()

        @pl.when(below)
        def _():
            down_copy(j).start()

        return carry

    lax.fori_loop(0, views, send_all, 0)

    fetch_layers.wait()
    for f in range(frames):
        for k in range(layer_count):
            def load(tile):
                where = pl.ds(pl.multiple_of(tile * LANES, LANES), LANES)
                return layers_ref[f, k, :, where].astype(jnp.float32)

            plane = window(load, me)
            at = f * layer_count + k
            layer_win[at, EDGE : EDGE + rows, :] = plane
            halo_out[0, at] = plane[:EDGE].astype(jnp.bfloat16)
            halo_out[1, at] = plane[rows - EDGE :].astype(jnp.bfloat16)

    @pl.when(above)
    def _():
        layer_copy(True).start()

    @pl.when(below)
    def _():
        layer_copy(False).start()

    @pl.when(jnp.logical_not(above))
    def _():
        recv_win[:, :EDGE, :] = jnp.zeros((views, EDGE, LANES), jnp.bfloat16)
        layer_win[:, :EDGE, :] = jnp.zeros((planes, EDGE, LANES), jnp.float32)

    @pl.when(jnp.logical_not(below))
    def _():
        recv_win[:, EDGE + rows :, :] = jnp.zeros((views, EDGE, LANES), jnp.bfloat16)
        layer_win[:, EDGE + rows :, :] = jnp.zeros((planes, EDGE, LANES), jnp.float32)

    at_row = rows * row - HALO + lax.broadcasted_iota(jnp.int32, (inner, LANES), 0)
    at_col = strip * me - MARGIN + lax.broadcasted_iota(jnp.int32, (inner, LANES), 1)
    inside = (at_row >= 0) & (at_row < rows * rows_of) & (at_col >= 0) & (at_col < cols)
    third_win[...] = jnp.where(inside, 1.0 / frames, 0.0)
    upper[...] = jnp.zeros_like(upper)
    lower[...] = jnp.zeros_like(lower)

    def wait_shift(j, carry):
        source = lax.rem(me + views - j, views)
        arrived(shift_in.at[source], shift_recv.at[source])
        return carry

    lax.fori_loop(1, views, wait_shift, 0)
    to_smem = pltpu.make_async_copy(shift_in, shift_smem, smem_sem)
    to_smem.start()

    @pl.when(above)
    def _():
        arrived(halo_in.at[0], lh_recv.at[0])
        layer_win[:, :EDGE, :] = halo_in[0].astype(jnp.float32)

    @pl.when(below)
    def _():
        arrived(halo_in.at[1], lh_recv.at[1])
        layer_win[:, EDGE + rows :, :] = halo_in[1].astype(jnp.float32)

    to_smem.wait()

    def some_views(n, carry):
        views_now = []
        for b in range(BATCH):
            j = n * BATCH + b
            view = lax.rem(me + views - j, views)
            views_now.append(view)

            @pl.when(j > 0)
            def _():
                arrived(recv_win.at[view, pl.ds(EDGE, rows)], win_recv.at[view])

            @pl.when(above)
            def _():
                arrived(recv_win.at[view, pl.ds(0, EDGE)], down_recv.at[view])

            @pl.when(below)
            def _():
                arrived(recv_win.at[view, pl.ds(EDGE + rows, EDGE)], up_recv.at[view])

        row_shift, back = [], []
        for b, view in enumerate(views_now):
            target_win[b] = recv_win[view].astype(jnp.float32)
            row_now = [shift_smem[view, 0, 2 * k] for k in range(layer_count)]
            col_now = [shift_smem[view, 0, 2 * k + 1] for k in range(layer_count)]
            there = [lax.rem(LANES - c, LANES) for c in col_now]
            row_shift.append(row_now)
            back.append([lax.rem(LANES + c, LANES) for c in col_now])
            total = None
            for f in range(frames):
                seen = [
                    pltpu.roll(
                        layer_win[f * layer_count + k, pl.ds(EDGE - HALO + row_now[k], inner), :],
                        there[k], 1,
                    )
                    for k in range(layer_count)
                ]
                for k in range(layer_count):
                    rest = None
                    for i in range(layer_count):
                        if i != k:
                            rest = seen[i] if rest is None else rest * seen[i]
                    others_win[b, f * layer_count + k] = rest
                    if k == layer_count - 1:
                        whole = rest * seen[k]
                        total = whole if total is None else total + whole
            shown_win[b] = total * third_win[...]

        for k in range(layer_count):
            image, model = [], []
            for b in range(BATCH):
                turn, by = back[b][k], row_shift[b][k]
                image.append(pltpu.roll(target_win[b, pl.ds(EDGE - by, rows), :], turn, 1))
                model.append(pltpu.roll(shown_win[b, pl.ds(HALO - by, rows), :], turn, 1))
            for f in range(frames):
                at = f * layer_count + k
                up, low = upper[at], lower[at]
                for b in range(BATCH):
                    rest = pltpu.roll(
                        others_win[b, at, pl.ds(HALO - row_shift[b][k], rows), :], back[b][k], 1
                    )
                    up += image[b] * rest
                    low += model[b] * rest
                upper[at] = up
                lower[at] = low
        return carry

    lax.fori_loop(0, views // BATCH, some_views, 0)

    core = lax.rem(me, 2)
    x = lax.rem(me // 2, across)
    z = me // (2 * across)

    def index(zz, xx, cc):
        return (zz * across + xx) * 2 + cc

    chunks = 2 if packed.shape[0] % 32 == 0 else 1
    size = packed.shape[0] // chunks

    def part_of(slot, c):
        return slots.at[slot, pl.ds(c * size, size)]

    def slot_copy(slot, to, sem, c):
        return pltpu.make_async_remote_copy(
            src_ref=part_of(slot, c), dst_ref=part_of(slot, c), send_sem=sem,
            recv_sem=slot_recv.at[c, slot], device_id=(to, row), device_id_type=MESH,
        )

    def slot_here(slot, c):
        arrived(part_of(slot, c), slot_recv.at[c, slot])

    def along(d):
        return index(z + d, x, core)

    def to_column(d, c):
        return slot_copy(me, index(z + d, x, core), col_send.at[c, depth + d], c)

    def to_across(d, dx, c):
        to = index(z, lax.rem(x + dx, across), core)
        return slot_copy(along(d), to, x_send.at[c, depth + d, dx], c)

    def to_core(d, dx, c):
        slot = index(z + d, lax.rem(x + across - dx, across), core)
        return slot_copy(slot, index(z, x, 1 - core), core_send.at[c, depth + d, dx], c)

    def exists(d):
        return (z + d >= 0) & (z + d < depth)

    def visit(d, act):
        if d:
            pl.when(exists(d))(act)
        else:
            act()

    def both_ways(d):
        return (-d, d) if d else (0,)

    def each_copy(d, act, c):
        if d:
            act(to_column(d, c))
        for dx in range(1, across):
            act(to_across(d, dx, c))
        act(to_core(d, 0, c))

    def spread(d, c):
        for dx in range(1, across):
            to_across(d, dx, c).start()
        to_core(d, 0, c).start()

    def column_step(d, c):
        def act():
            slot_here(along(d), c)
            spread(d, c)

        visit(d, act)

    def across_step(d, c):
        def act():
            for dx in range(1, across):
                slot_here(index(z + d, lax.rem(x + across - dx, across), core), c)
                to_core(d, dx, c).start()

        visit(d, act)

    spare = packed.shape[0] - planes * short
    if spare:
        packed[planes * short :, :] = jnp.zeros((spare, LANES), jnp.float32)
    done = 0
    for c in range(chunks):
        while done < planes and done * short < (c + 1) * size:
            ratio = (upper[done] + REGULAR) / (lower[done] + REGULAR)
            value = (jnp.log(ratio) - middle) * (1.0 / step)
            merged = pltpu.roll(value[:short], LANES - MARGIN, 1)
            if groups == 2:
                other = pltpu.roll(value[short:], strip - MARGIN, 1)
                merged = jnp.where(lane < strip, merged, other)
            packed[done * short : (done + 1) * short, :] = merged
            done += 1
        span = slice(c * size, (c + 1) * size)
        slots[me, span, :] = jnp.round(packed[span, :]).astype(jnp.int32).astype(jnp.int16)
        for distance in range(depth - 1, 0, -1):
            for d in both_ways(distance):
                def act():
                    to_column(d, c).start()

                visit(d, act)
        spread(0, c)

    @pl.when(above)
    def _():
        layer_copy(True).wait_send()

    @pl.when(below)
    def _():
        layer_copy(False).wait_send()

    def finish(j, carry):
        @pl.when(j > 0)
        def _():
            shift_copy(j).wait_send()
            win_copy(j).wait_send()

        @pl.when(above)
        def _():
            up_copy(j).wait_send()

        @pl.when(below)
        def _():
            down_copy(j).wait_send()

        return carry

    lax.fori_loop(0, views, finish, 0)

    for distance in range(1, depth):
        for c in range(chunks):
            for d in both_ways(distance):
                column_step(d, c)
            for d in both_ways(distance - 1):
                across_step(d, c)

    per_tile = LANES // strip

    def store_tile(tile):
        where = pl.ds(pl.multiple_of(tile * LANES, LANES), LANES)
        return pltpu.make_async_copy(
            out_ref.at[:, :, :, where], out_hbm.at[:, :, :, where], store_sem.at[tile]
        )

    def unpack(tile):
        for i in range(per_tile):
            @pl.when(lax.rem(tile * per_tile + i, 2) != core)
            def _():
                for c in range(chunks):
                    slot_here(tile * per_tile + i, c)

        where = pl.ds(pl.multiple_of(tile * LANES, LANES), LANES)
        parts = [slots[tile * per_tile + i].astype(jnp.int32) for i in range(per_tile)]
        for f in range(frames):
            for k in range(layer_count):
                at = f * layer_count + k
                spans = []
                for g in range(groups):
                    code = None
                    for i in range(per_tile):
                        part = parts[i][at * short : (at + 1) * short]
                        turn = (strip * (i - g)) % LANES
                        if turn:
                            part = pltpu.roll(part, turn, 1)
                        code = part if code is None else jnp.where(lane < strip * i, code, part)
                    spans.append(code)
                whole = jnp.concatenate(spans, axis=0) if groups > 1 else spans[0]
                out_ref[f, k, :, where] = whole.astype(jnp.int16)
        store_tile(tile).start()

    early = strip == 64

    def unpack_column(n, carry):
        unpack(n * across + x)
        return carry

    if early:
        lax.fori_loop(0, depth, unpack_column, 0)
    for c in range(chunks):
        for d in both_ways(depth - 1):
            across_step(d, c)

    def unpack_rest(n, carry):
        zz, dx = n // (across - 1), lax.rem(n, across - 1) + 1
        unpack(zz * across + lax.rem(x + dx, across))
        return carry

    def unpack_any(n, carry):
        unpack(n)
        return carry

    if early:
        lax.fori_loop(0, depth * (across - 1), unpack_rest, 0)
    else:
        lax.fori_loop(0, tiles, unpack_any, 0)

    for distance in range(depth):
        for d in both_ways(distance):
            def act():
                for c in range(chunks):
                    each_copy(d, lambda copy: copy.wait_send(), c)
                    for dx in range(1, across):
                        to_core(d, dx, c).wait_send()

            visit(d, act)

    def wait_store(tile, carry):
        store_tile(tile).wait()
        return carry

    lax.fori_loop(0, tiles, wait_store, 0)


def decode(views, codes_hbm, layers_hbm, out_hbm, codes, layers, out, sems):
    frames, layer_count = layers.shape[:2]
    middle, step = code_range(views)
    moves = []
    for f in range(frames):
        for k in range(layer_count):
            at = f * layer_count + k
            moves.append((
                pltpu.make_async_copy(codes_hbm.at[f, k], codes.at[f, k], sems.at[0, at]),
                pltpu.make_async_copy(layers_hbm.at[f, k], layers.at[f, k], sems.at[1, at]),
                pltpu.make_async_copy(out.at[f, k], out_hbm.at[f, k], sems.at[2, at]),
            ))
    for code_in, layer_in, _ in moves:
        code_in.start()
        layer_in.start()
    for at, (code_in, layer_in, store) in enumerate(moves):
        f, k = at // layer_count, at % layer_count
        code_in.wait()
        layer_in.wait()
        ratio = jnp.exp(codes[f, k].astype(jnp.int32).astype(jnp.float32) * step + middle)
        out[f, k] = layers[f, k].astype(jnp.float32) * ratio
        store.start()
    for _, _, store in moves:
        store.wait()


def body(views, rows_of, layers, target, shifts):
    frames, layer_count, rows, cols = layers.shape
    planes = frames * layer_count
    strip = cols // views
    groups = 2 if strip == 64 else 1
    depth, across = split_views(views)
    packed_rows = -(-planes * (rows // groups) // 16) * 16
    height, inner = rows + 2 * EDGE, rows + 2 * HALO
    dma = pltpu.SemaphoreType.DMA
    f32, bf16 = jnp.float32, jnp.bfloat16
    codes = pl.pallas_call(
        functools.partial(kernel, views, rows_of),
        out_shape=jax.ShapeDtypeStruct(layers.shape, jnp.int16),
        in_specs=[
            pl.BlockSpec(memory_space=pltpu.HBM),
            pl.BlockSpec(memory_space=pltpu.HBM),
            pl.BlockSpec(memory_space=pltpu.HBM),
        ],
        out_specs=pl.BlockSpec(memory_space=pltpu.HBM),
        scratch_shapes=[
            pltpu.SMEM((1, 2, layer_count), jnp.int32),
            pltpu.VMEM(layers.shape, bf16),
            pltpu.VMEM(target.shape, bf16),
            pltpu.VMEM(layers.shape, jnp.int16),
            dma((3,)),
            dma((cols // LANES,)),
            pltpu.VMEM((views, rows, LANES), bf16),
            pltpu.VMEM((views, height, LANES), bf16),
            pltpu.VMEM((1, LANES), jnp.int32),
            pltpu.VMEM((views, 1, LANES), jnp.int32),
            pltpu.SMEM((views, 1, LANES), jnp.int32),
            pltpu.VMEM((2, planes, EDGE, LANES), bf16),
            pltpu.VMEM((2, planes, EDGE, LANES), bf16),
            pltpu.VMEM((planes, height, LANES), f32),
            pltpu.VMEM((BATCH, height, LANES), f32),
            pltpu.VMEM((BATCH, planes, inner, LANES), f32),
            pltpu.VMEM((BATCH, inner, LANES), f32),
            pltpu.VMEM((inner, LANES), f32),
            pltpu.VMEM((planes, rows, LANES), f32),
            pltpu.VMEM((planes, rows, LANES), f32),
            pltpu.VMEM((packed_rows, LANES), f32),
            pltpu.VMEM((views, packed_rows, LANES), jnp.int16),
            dma((views,)), dma((views,)), dma((views,)), dma((views,)), dma((views,)), dma((views,)),
            dma((views,)), dma((views,)), dma, dma((2,)), dma((2,)),
            dma((2, 2 * depth)), dma((2, 2 * depth, across)), dma((2, 2 * depth, across)), dma((2, views)),
        ],
        compiler_params=pltpu.CompilerParams(
            collective_id=0, has_side_effects=True, vmem_limit_bytes=62 * 1024 * 1024
        ),
        name="light_field_update",
    )(jnp.swapaxes(shifts, 1, 2), layers, target)
    return pl.pallas_call(
        functools.partial(decode, views),
        out_shape=jax.ShapeDtypeStruct(layers.shape, f32),
        in_specs=[pl.BlockSpec(memory_space=pltpu.HBM)] * 2,
        out_specs=pl.BlockSpec(memory_space=pltpu.HBM),
        scratch_shapes=[
            pltpu.VMEM(layers.shape, jnp.int16),
            pltpu.VMEM(layers.shape, bf16),
            pltpu.VMEM(layers.shape, f32),
            dma((3, planes)),
        ],
        compiler_params=pltpu.CompilerParams(vmem_limit_bytes=62 * 1024 * 1024),
        name="decode_ratio",
    )(codes, layers)


def solution(mesh):
    placed = (P(None, None, "row", None), P("view", "row", None), P("view", None, None))
    return jax.shard_map(
        functools.partial(body, mesh.shape["view"], mesh.shape["row"]),
        mesh=mesh, in_specs=placed, out_specs=P(None, None, "row", None), check_vma=False,
    )
```

```python
import functools
import math

import jax
import jax.numpy as jnp
from jax import lax
from jax.experimental import pallas as pl
from jax.experimental.pallas import tpu as pltpu
from jax.sharding import PartitionSpec as P

HALO = 8
LANES = 128
EDGE = 16
MARGIN = 32
REGULAR = 0.05
BATCH = 4
MESH = pl.DeviceIdType.MESH


def split_views(views):
    across = 1
    while (2 * across) ** 2 * 2 <= views:
        across *= 2
    return views // (2 * across), across


def code_range(views):
    low = math.log(REGULAR / (views + REGULAR))
    high = math.log((0.5 * views + REGULAR) / REGULAR)
    return 0.5 * (low + high), (high - low) / 65000.0


def kernel(
    views, rows_of, shifts_hbm, layers_hbm, target_hbm, out_hbm,
    shifts_ref, layers_ref, target_ref, out_ref, fetch_sem, store_sem,
    send_win, recv_win, shift_out, shift_in, shift_smem, halo_out, halo_in,
    layer_win, target_win, others_win, shown_win, third_win, upper, lower, packed, slots,
    win_send, win_recv, up_send, up_recv, down_send, down_recv,
    shift_send, shift_recv, smem_sem, lh_send, lh_recv,
    col_send, x_send, core_send, slot_recv,
):
    fetch_shifts = pltpu.make_async_copy(shifts_hbm, shifts_ref, fetch_sem.at[0])
    fetch_target = pltpu.make_async_copy(target_hbm, target_ref, fetch_sem.at[1])
    fetch_layers = pltpu.make_async_copy(layers_hbm, layers_ref, fetch_sem.at[2])
    fetch_shifts.start()
    fetch_target.start()
    fetch_layers.start()

    frames, layer_count, rows, cols = layers_ref.shape
    strip = cols // views
    planes = frames * layer_count
    height = rows + 2 * EDGE
    inner = rows + 2 * HALO
    depth, across = split_views(views)
    groups = 2 if strip == 64 else 1
    short = rows // groups
    tiles = cols // LANES
    middle, step = code_range(views)

    me = lax.axis_index("view")
    row = lax.axis_index("row")
    above, below = row > 0, row < rows_of - 1

    barrier = pltpu.get_barrier_semaphore()

    def greet(j, carry):
        partner = lax.rem(me + j, views)

        @pl.when(j > 0)
        def _():
            pl.semaphore_signal(barrier, inc=1, device_id=(partner, row), device_id_type=MESH)

        @pl.when(above)
        def _():
            pl.semaphore_signal(barrier, inc=1, device_id=(partner, row - 1), device_id_type=MESH)

        @pl.when(below)
        def _():
            pl.semaphore_signal(barrier, inc=1, device_id=(partner, row + 1), device_id_type=MESH)

        return carry

    lax.fori_loop(0, views, greet, 0, unroll=4)

    lane = lax.broadcasted_iota(jnp.int32, (1, LANES), 1)

    def window(load, index):
        start = strip * index - MARGIN
        tile = (start + LANES) // LANES - 1
        offset = start - tile * LANES
        first = load(jnp.maximum(tile, 0))
        second = load(jnp.minimum(tile + 1, tiles - 1))
        turn = lax.rem(LANES - offset, LANES)
        first = pltpu.roll(first, turn, 1)
        second = pltpu.roll(second, turn, 1)
        both = jnp.where(lane < LANES - offset, first, second)
        col = start + lane
        return jnp.where((col >= 0) & (col < cols), both, 0.0)

    fetch_shifts.wait()
    place = lax.broadcasted_iota(jnp.int32, (1, LANES), 1)
    block = jnp.zeros((1, LANES), jnp.int32)
    for k in range(layer_count):
        for axis in range(2):
            block = jnp.where(place == 2 * k + axis, shifts_ref[0, axis, k], block)
    shift_out[...] = block
    shift_in[me] = block

    fetch_target.wait()

    def fill(c, carry):
        def load(tile):
            where = pl.ds(pl.multiple_of(tile * LANES, LANES), LANES)
            return target_ref[0, :, where].astype(jnp.float32)

        send_win[c] = window(load, c).astype(jnp.bfloat16)
        return carry

    lax.fori_loop(0, views, fill, 0, unroll=8)
    recv_win[me, EDGE : EDGE + rows, :] = send_win[me]

    def shift_copy(j):
        partner = lax.rem(me + j, views)
        return pltpu.make_async_remote_copy(
            src_ref=shift_out, dst_ref=shift_in.at[me], send_sem=shift_send.at[j],
            recv_sem=shift_recv.at[me], device_id=(partner, row), device_id_type=MESH,
        )

    def win_copy(j):
        partner = lax.rem(me + j, views)
        return pltpu.make_async_remote_copy(
            src_ref=send_win.at[partner], dst_ref=recv_win.at[me, pl.ds(EDGE, rows)],
            send_sem=win_send.at[j], recv_sem=win_recv.at[me],
            device_id=(partner, row), device_id_type=MESH,
        )

    def up_copy(j):
        partner = lax.rem(me + j, views)
        return pltpu.make_async_remote_copy(
            src_ref=send_win.at[partner, pl.ds(0, EDGE)],
            dst_ref=recv_win.at[me, pl.ds(EDGE + rows, EDGE)],
            send_sem=up_send.at[j], recv_sem=up_recv.at[me],
            device_id=(partner, row - 1), device_id_type=MESH,
        )

    def down_copy(j):
        partner = lax.rem(me + j, views)
        return pltpu.make_async_remote_copy(
            src_ref=send_win.at[partner, pl.ds(rows - EDGE, EDGE)],
            dst_ref=recv_win.at[me, pl.ds(0, EDGE)],
            send_sem=down_send.at[j], recv_sem=down_recv.at[me],
            device_id=(partner, row + 1), device_id_type=MESH,
        )

    def layer_copy(up):
        return pltpu.make_async_remote_copy(
            src_ref=halo_out.at[0 if up else 1], dst_ref=halo_in.at[1 if up else 0],
            send_sem=lh_send.at[0 if up else 1], recv_sem=lh_recv.at[1 if up else 0],
            device_id=(me, row - 1 if up else row + 1), device_id_type=MESH,
        )

    def arrived(dst, sem):
        return pltpu.make_async_remote_copy(
            src_ref=dst, dst_ref=dst, send_sem=sem, recv_sem=sem,
            device_id=(me, row), device_id_type=MESH,
        ).wait_recv()

    pl.semaphore_wait(
        barrier, views - 1 + views * (above.astype(jnp.int32) + below.astype(jnp.int32))
    )

    def send_shift(j, carry):
        shift_copy(j).start()
        return carry

    lax.fori_loop(1, views, send_shift, 0)

    def send_all(j, carry):
        @pl.when(j > 0)
        def _():
            win_copy(j).start()

        @pl.when(above)
        def _():
            up_copy(j).start()

        @pl.when(below)
        def _():
            down_copy(j).start()

        return carry

    lax.fori_loop(0, views, send_all, 0)

    fetch_layers.wait()
    for f in range(frames):
        for k in range(layer_count):
            def load(tile):
                where = pl.ds(pl.multiple_of(tile * LANES, LANES), LANES)
                return layers_ref[f, k, :, where].astype(jnp.float32)

            plane = window(load, me)
            at = f * layer_count + k
            layer_win[at, EDGE : EDGE + rows, :] = plane
            halo_out[0, at] = plane[:EDGE].astype(jnp.bfloat16)
            halo_out[1, at] = plane[rows - EDGE :].astype(jnp.bfloat16)

    @pl.when(above)
    def _():
        layer_copy(True).start()

    @pl.when(below)
    def _():
        layer_copy(False).start()

    @pl.when(jnp.logical_not(above))
    def _():
        recv_win[:, :EDGE, :] = jnp.zeros((views, EDGE, LANES), jnp.bfloat16)
        layer_win[:, :EDGE, :] = jnp.zeros((planes, EDGE, LANES), jnp.float32)

    @pl.when(jnp.logical_not(below))
    def _():
        recv_win[:, EDGE + rows :, :] = jnp.zeros((views, EDGE, LANES), jnp.bfloat16)
        layer_win[:, EDGE + rows :, :] = jnp.zeros((planes, EDGE, LANES), jnp.float32)

    at_row = rows * row - HALO + lax.broadcasted_iota(jnp.int32, (inner, LANES), 0)
    at_col = strip * me - MARGIN + lax.broadcasted_iota(jnp.int32, (inner, LANES), 1)
    inside = (at_row >= 0) & (at_row < rows * rows_of) & (at_col >= 0) & (at_col < cols)
    third_win[...] = jnp.where(inside, 1.0 / frames, 0.0)
    upper[...] = jnp.zeros_like(upper)
    lower[...] = jnp.zeros_like(lower)

    def wait_shift(j, carry):
        source = lax.rem(me + views - j, views)
        arrived(shift_in.at[source], shift_recv.at[source])
        return carry

    lax.fori_loop(1, views, wait_shift, 0)
    to_smem = pltpu.make_async_copy(shift_in, shift_smem, smem_sem)
    to_smem.start()

    @pl.when(above)
    def _():
        arrived(halo_in.at[0], lh_recv.at[0])
        layer_win[:, :EDGE, :] = halo_in[0].astype(jnp.float32)

    @pl.when(below)
    def _():
        arrived(halo_in.at[1], lh_recv.at[1])
        layer_win[:, EDGE + rows :, :] = halo_in[1].astype(jnp.float32)

    to_smem.wait()

    def some_views(n, carry):
        views_now = []
        for b in range(BATCH):
            j = n * BATCH + b
            view = lax.rem(me + views - j, views)
            views_now.append(view)

            @pl.when(j > 0)
            def _():
                arrived(recv_win.at[view, pl.ds(EDGE, rows)], win_recv.at[view])

            @pl.when(above)
            def _():
                arrived(recv_win.at[view, pl.ds(0, EDGE)], down_recv.at[view])

            @pl.when(below)
            def _():
                arrived(recv_win.at[view, pl.ds(EDGE + rows, EDGE)], up_recv.at[view])

        row_shift, back = [], []
        for b, view in enumerate(views_now):
            target_win[b] = recv_win[view].astype(jnp.float32)
            row_now = [shift_smem[view, 0, 2 * k] for k in range(layer_count)]
            col_now = [shift_smem[view, 0, 2 * k + 1] for k in range(layer_count)]
            there = [lax.rem(LANES - c, LANES) for c in col_now]
            row_shift.append(row_now)
            back.append([lax.rem(LANES + c, LANES) for c in col_now])
            total = None
            for f in range(frames):
                seen = [
                    pltpu.roll(
                        layer_win[f * layer_count + k, pl.ds(EDGE - HALO + row_now[k], inner), :],
                        there[k], 1,
                    )
                    for k in range(layer_count)
                ]
                for k in range(layer_count):
                    rest = None
                    for i in range(layer_count):
                        if i != k:
                            rest = seen[i] if rest is None else rest * seen[i]
                    others_win[b, f * layer_count + k] = rest
                    if k == layer_count - 1:
                        whole = rest * seen[k]
                        total = whole if total is None else total + whole
            shown_win[b] = total * third_win[...]

        for k in range(layer_count):
            image, model = [], []
            for b in range(BATCH):
                turn, by = back[b][k], row_shift[b][k]
                image.append(pltpu.roll(target_win[b, pl.ds(EDGE - by, rows), :], turn, 1))
                model.append(pltpu.roll(shown_win[b, pl.ds(HALO - by, rows), :], turn, 1))
            for f in range(frames):
                at = f * layer_count + k
                up, low = upper[at], lower[at]
                for b in range(BATCH):
                    rest = pltpu.roll(
                        others_win[b, at, pl.ds(HALO - row_shift[b][k], rows), :], back[b][k], 1
                    )
                    up += image[b] * rest
                    low += model[b] * rest
                upper[at] = up
                lower[at] = low
        return carry

    lax.fori_loop(0, views // BATCH, some_views, 0)

    core = lax.rem(me, 2)
    x = lax.rem(me // 2, across)
    z = me // (2 * across)

    def index(zz, xx, cc):
        return (zz * across + xx) * 2 + cc

    chunks = 2 if packed.shape[0] % 32 == 0 else 1
    size = packed.shape[0] // chunks

    def part_of(slot, c):
        return slots.at[slot, pl.ds(c * size, size)]

    def slot_copy(slot, to, sem, c):
        return pltpu.make_async_remote_copy(
            src_ref=part_of(slot, c), dst_ref=part_of(slot, c), send_sem=sem,
            recv_sem=slot_recv.at[c, slot], device_id=(to, row), device_id_type=MESH,
        )

    def slot_here(slot, c):
        arrived(part_of(slot, c), slot_recv.at[c, slot])

    def along(d):
        return index(z + d, x, core)

    def to_column(d, c):
        return slot_copy(me, index(z + d, x, core), col_send.at[c, depth + d], c)

    def to_across(d, dx, c):
        to = index(z, lax.rem(x + dx, across), core)
        return slot_copy(along(d), to, x_send.at[c, depth + d, dx], c)

    def to_core(d, dx, c):
        slot = index(z + d, lax.rem(x + across - dx, across), core)
        return slot_copy(slot, index(z, x, 1 - core), core_send.at[c, depth + d, dx], c)

    def exists(d):
        return (z + d >= 0) & (z + d < depth)

    def visit(d, act):
        if d:
            pl.when(exists(d))(act)
        else:
            act()

    def both_ways(d):
        return (-d, d) if d else (0,)

    def each_copy(d, act, c):
        if d:
            act(to_column(d, c))
        for dx in range(1, across):
            act(to_across(d, dx, c))
        act(to_core(d, 0, c))

    def spread(d, c):
        for dx in range(1, across):
            to_across(d, dx, c).start()
        to_core(d, 0, c).start()

    def column_step(d, c):
        def act():
            slot_here(along(d), c)
            spread(d, c)

        visit(d, act)

    def across_step(d, c):
        def act():
            for dx in range(1, across):
                slot_here(index(z + d, lax.rem(x + across - dx, across), core), c)
                to_core(d, dx, c).start()

        visit(d, act)

    spare = packed.shape[0] - planes * short
    if spare:
        packed[planes * short :, :] = jnp.zeros((spare, LANES), jnp.float32)
    done = 0
    for c in range(chunks):
        while done < planes and done * short < (c + 1) * size:
            ratio = (upper[done] + REGULAR) / (lower[done] + REGULAR)
            value = (jnp.log(ratio) - middle) * (1.0 / step)
            merged = pltpu.roll(value[:short], LANES - MARGIN, 1)
            if groups == 2:
                other = pltpu.roll(value[short:], strip - MARGIN, 1)
                merged = jnp.where(lane < strip, merged, other)
            packed[done * short : (done + 1) * short, :] = merged
            done += 1
        span = slice(c * size, (c + 1) * size)
        slots[me, span, :] = jnp.round(packed[span, :]).astype(jnp.int32).astype(jnp.int16)
        spread(0, c)
        for distance in range(1, depth):
            for d in both_ways(distance):
                def act():
                    to_column(d, c).start()

                visit(d, act)

    @pl.when(above)
    def _():
        layer_copy(True).wait_send()

    @pl.when(below)
    def _():
        layer_copy(False).wait_send()

    def finish(j, carry):
        @pl.when(j > 0)
        def _():
            shift_copy(j).wait_send()
            win_copy(j).wait_send()

        @pl.when(above)
        def _():
            up_copy(j).wait_send()

        @pl.when(below)
        def _():
            down_copy(j).wait_send()

        return carry

    lax.fori_loop(0, views, finish, 0)

    for distance in range(1, depth):
        for c in range(chunks):
            for d in both_ways(distance):
                column_step(d, c)
            for d in both_ways(distance - 1):
                across_step(d, c)

    per_tile = LANES // strip

    def store_tile(tile):
        where = pl.ds(pl.multiple_of(tile * LANES, LANES), LANES)
        return pltpu.make_async_copy(
            out_ref.at[:, :, :, where], out_hbm.at[:, :, :, where], store_sem.at[tile]
        )

    def unpack(tile):
        for i in range(per_tile):
            @pl.when(lax.rem(tile * per_tile + i, 2) != core)
            def _():
                for c in range(chunks):
                    slot_here(tile * per_tile + i, c)

        where = pl.ds(pl.multiple_of(tile * LANES, LANES), LANES)
        parts = [slots[tile * per_tile + i].astype(jnp.int32) for i in range(per_tile)]
        for f in range(frames):
            for k in range(layer_count):
                at = f * layer_count + k
                spans = []
                for g in range(groups):
                    code = None
                    for i in range(per_tile):
                        part = parts[i][at * short : (at + 1) * short]
                        turn = (strip * (i - g)) % LANES
                        if turn:
                            part = pltpu.roll(part, turn, 1)
                        code = part if code is None else jnp.where(lane < strip * i, code, part)
                    spans.append(code)
                whole = jnp.concatenate(spans, axis=0) if groups > 1 else spans[0]
                out_ref[f, k, :, where] = whole.astype(jnp.int16)
        store_tile(tile).start()

    early = strip == 64

    def unpack_column(n, carry):
        unpack(n * across + x)
        return carry

    if early:
        lax.fori_loop(0, depth, unpack_column, 0)
    for c in range(chunks):
        for d in both_ways(depth - 1):
            across_step(d, c)

    def unpack_rest(n, carry):
        zz, dx = n // (across - 1), lax.rem(n, across - 1) + 1
        unpack(zz * across + lax.rem(x + dx, across))
        return carry

    def unpack_any(n, carry):
        unpack(n)
        return carry

    if early:
        lax.fori_loop(0, depth * (across - 1), unpack_rest, 0)
    else:
        lax.fori_loop(0, tiles, unpack_any, 0)

    for distance in range(depth):
        for d in both_ways(distance):
            def act():
                for c in range(chunks):
                    each_copy(d, lambda copy: copy.wait_send(), c)
                    for dx in range(1, across):
                        to_core(d, dx, c).wait_send()

            visit(d, act)

    def wait_store(tile, carry):
        store_tile(tile).wait()
        return carry

    lax.fori_loop(0, tiles, wait_store, 0)


def decode(views, codes_hbm, layers_hbm, out_hbm, codes, layers, out, sems):
    frames, layer_count = layers.shape[:2]
    middle, step = code_range(views)
    moves = []
    for f in range(frames):
        for k in range(layer_count):
            at = f * layer_count + k
            moves.append((
                pltpu.make_async_copy(codes_hbm.at[f, k], codes.at[f, k], sems.at[0, at]),
                pltpu.make_async_copy(layers_hbm.at[f, k], layers.at[f, k], sems.at[1, at]),
                pltpu.make_async_copy(out.at[f, k], out_hbm.at[f, k], sems.at[2, at]),
            ))
    for code_in, layer_in, _ in moves:
        code_in.start()
        layer_in.start()
    for at, (code_in, layer_in, store) in enumerate(moves):
        f, k = at // layer_count, at % layer_count
        code_in.wait()
        layer_in.wait()
        ratio = jnp.exp(codes[f, k].astype(jnp.int32).astype(jnp.float32) * step + middle)
        out[f, k] = layers[f, k].astype(jnp.float32) * ratio
        store.start()
    for _, _, store in moves:
        store.wait()


def body(views, rows_of, layers, target, shifts):
    frames, layer_count, rows, cols = layers.shape
    planes = frames * layer_count
    strip = cols // views
    groups = 2 if strip == 64 else 1
    depth, across = split_views(views)
    packed_rows = -(-planes * (rows // groups) // 16) * 16
    height, inner = rows + 2 * EDGE, rows + 2 * HALO
    dma = pltpu.SemaphoreType.DMA
    f32, bf16 = jnp.float32, jnp.bfloat16
    codes = pl.pallas_call(
        functools.partial(kernel, views, rows_of),
        out_shape=jax.ShapeDtypeStruct(layers.shape, jnp.int16),
        in_specs=[
            pl.BlockSpec(memory_space=pltpu.HBM),
            pl.BlockSpec(memory_space=pltpu.HBM),
            pl.BlockSpec(memory_space=pltpu.HBM),
        ],
        out_specs=pl.BlockSpec(memory_space=pltpu.HBM),
        scratch_shapes=[
            pltpu.SMEM((1, 2, layer_count), jnp.int32),
            pltpu.VMEM(layers.shape, bf16),
            pltpu.VMEM(target.shape, bf16),
            pltpu.VMEM(layers.shape, jnp.int16),
            dma((3,)),
            dma((cols // LANES,)),
            pltpu.VMEM((views, rows, LANES), bf16),
            pltpu.VMEM((views, height, LANES), bf16),
            pltpu.VMEM((1, LANES), jnp.int32),
            pltpu.VMEM((views, 1, LANES), jnp.int32),
            pltpu.SMEM((views, 1, LANES), jnp.int32),
            pltpu.VMEM((2, planes, EDGE, LANES), bf16),
            pltpu.VMEM((2, planes, EDGE, LANES), bf16),
            pltpu.VMEM((planes, height, LANES), f32),
            pltpu.VMEM((BATCH, height, LANES), f32),
            pltpu.VMEM((BATCH, planes, inner, LANES), f32),
            pltpu.VMEM((BATCH, inner, LANES), f32),
            pltpu.VMEM((inner, LANES), f32),
            pltpu.VMEM((planes, rows, LANES), f32),
            pltpu.VMEM((planes, rows, LANES), f32),
            pltpu.VMEM((packed_rows, LANES), f32),
            pltpu.VMEM((views, packed_rows, LANES), jnp.int16),
            dma((views,)), dma((views,)), dma((views,)), dma((views,)), dma((views,)), dma((views,)),
            dma((views,)), dma((views,)), dma, dma((2,)), dma((2,)),
            dma((2, 2 * depth)), dma((2, 2 * depth, across)), dma((2, 2 * depth, across)), dma((2, views)),
        ],
        compiler_params=pltpu.CompilerParams(
            collective_id=0, has_side_effects=True, vmem_limit_bytes=62 * 1024 * 1024
        ),
        name="light_field_update",
    )(jnp.swapaxes(shifts, 1, 2), layers, target)
    return pl.pallas_call(
        functools.partial(decode, views),
        out_shape=jax.ShapeDtypeStruct(layers.shape, f32),
        in_specs=[pl.BlockSpec(memory_space=pltpu.HBM)] * 2,
        out_specs=pl.BlockSpec(memory_space=pltpu.HBM),
        scratch_shapes=[
            pltpu.VMEM(layers.shape, jnp.int16),
            pltpu.VMEM(layers.shape, bf16),
            pltpu.VMEM(layers.shape, f32),
            dma((3, planes)),
        ],
        compiler_params=pltpu.CompilerParams(vmem_limit_bytes=62 * 1024 * 1024),
        name="decode_ratio",
    )(codes, layers)


def solution(mesh):
    placed = (P(None, None, "row", None), P("view", "row", None), P("view", None, None))
    return jax.shard_map(
        functools.partial(body, mesh.shape["view"], mesh.shape["row"]),
        mesh=mesh, in_specs=placed, out_specs=P(None, None, "row", None), check_vma=False,
    )
```

```python
import functools
import math

import jax
import jax.numpy as jnp
from jax import lax
from jax.experimental import pallas as pl
from jax.experimental.pallas import tpu as pltpu
from jax.sharding import PartitionSpec as P

HALO = 8
LANES = 128
EDGE = 16
MARGIN = 32
REGULAR = 0.05
BATCH = 4
MESH = pl.DeviceIdType.MESH


def split_views(views):
    across = 1
    while (2 * across) ** 2 * 2 <= views:
        across *= 2
    return views // (2 * across), across


def code_range(views):
    low = math.log(REGULAR / (views + REGULAR))
    high = math.log((0.5 * views + REGULAR) / REGULAR)
    return 0.5 * (low + high), (high - low) / 65000.0


def kernel(
    views, rows_of, shifts_hbm, layers_hbm, target_hbm, out_hbm,
    shifts_ref, layers_ref, target_ref, out_ref, fetch_sem, store_sem,
    send_win, recv_win, shift_out, shift_in, shift_smem, halo_out, halo_in,
    layer_win, target_win, others_win, shown_win, third_win, upper, lower, packed, slots,
    win_send, win_recv, up_send, up_recv, down_send, down_recv,
    shift_send, shift_recv, smem_sem, lh_send, lh_recv,
    col_send, x_send, core_send, slot_recv,
):
    fetch_shifts = pltpu.make_async_copy(shifts_hbm, shifts_ref, fetch_sem.at[0])
    fetch_target = pltpu.make_async_copy(target_hbm, target_ref, fetch_sem.at[1])
    fetch_layers = pltpu.make_async_copy(layers_hbm, layers_ref, fetch_sem.at[2])
    fetch_shifts.start()
    fetch_target.start()
    fetch_layers.start()

    frames, layer_count, rows, cols = layers_ref.shape
    strip = cols // views
    planes = frames * layer_count
    height = rows + 2 * EDGE
    inner = rows + 2 * HALO
    depth, across = split_views(views)
    groups = 2 if strip == 64 else 1
    short = rows // groups
    tiles = cols // LANES
    middle, step = code_range(views)

    me = lax.axis_index("view")
    row = lax.axis_index("row")
    above, below = row > 0, row < rows_of - 1

    barrier = pltpu.get_barrier_semaphore()

    def greet(j, carry):
        partner = lax.rem(me + j, views)

        @pl.when(j > 0)
        def _():
            pl.semaphore_signal(barrier, inc=1, device_id=(partner, row), device_id_type=MESH)

        @pl.when(above)
        def _():
            pl.semaphore_signal(barrier, inc=1, device_id=(partner, row - 1), device_id_type=MESH)

        @pl.when(below)
        def _():
            pl.semaphore_signal(barrier, inc=1, device_id=(partner, row + 1), device_id_type=MESH)

        return carry

    lax.fori_loop(0, views, greet, 0, unroll=4)

    lane = lax.broadcasted_iota(jnp.int32, (1, LANES), 1)

    def window(load, index):
        start = strip * index - MARGIN
        tile = (start + LANES) // LANES - 1
        offset = start - tile * LANES
        first = load(jnp.maximum(tile, 0))
        second = load(jnp.minimum(tile + 1, tiles - 1))
        turn = lax.rem(LANES - offset, LANES)
        first = pltpu.roll(first, turn, 1)
        second = pltpu.roll(second, turn, 1)
        both = jnp.where(lane < LANES - offset, first, second)
        col = start + lane
        return jnp.where((col >= 0) & (col < cols), both, 0.0)

    fetch_shifts.wait()
    place = lax.broadcasted_iota(jnp.int32, (1, LANES), 1)
    block = jnp.zeros((1, LANES), jnp.int32)
    for k in range(layer_count):
        for axis in range(2):
            block = jnp.where(place == 2 * k + axis, shifts_ref[0, axis, k], block)
    shift_out[...] = block
    shift_in[me] = block

    fetch_target.wait()

    def fill(c, carry):
        def load(tile):
            where = pl.ds(pl.multiple_of(tile * LANES, LANES), LANES)
            return target_ref[0, :, where].astype(jnp.float32)

        send_win[c] = window(load, c).astype(jnp.bfloat16)
        return carry

    lax.fori_loop(0, views, fill, 0, unroll=8)
    recv_win[me, EDGE : EDGE + rows, :] = send_win[me]

    def shift_copy(j):
        partner = lax.rem(me + j, views)
        return pltpu.make_async_remote_copy(
            src_ref=shift_out, dst_ref=shift_in.at[me], send_sem=shift_send.at[j],
            recv_sem=shift_recv.at[me], device_id=(partner, row), device_id_type=MESH,
        )

    def win_copy(j):
        partner = lax.rem(me + j, views)
        return pltpu.make_async_remote_copy(
            src_ref=send_win.at[partner], dst_ref=recv_win.at[me, pl.ds(EDGE, rows)],
            send_sem=win_send.at[j], recv_sem=win_recv.at[me],
            device_id=(partner, row), device_id_type=MESH,
        )

    def up_copy(j):
        partner = lax.rem(me + j, views)
        return pltpu.make_async_remote_copy(
            src_ref=send_win.at[partner, pl.ds(0, EDGE)],
            dst_ref=recv_win.at[me, pl.ds(EDGE + rows, EDGE)],
            send_sem=up_send.at[j], recv_sem=up_recv.at[me],
            device_id=(partner, row - 1), device_id_type=MESH,
        )

    def down_copy(j):
        partner = lax.rem(me + j, views)
        return pltpu.make_async_remote_copy(
            src_ref=send_win.at[partner, pl.ds(rows - EDGE, EDGE)],
            dst_ref=recv_win.at[me, pl.ds(0, EDGE)],
            send_sem=down_send.at[j], recv_sem=down_recv.at[me],
            device_id=(partner, row + 1), device_id_type=MESH,
        )

    def layer_copy(up):
        return pltpu.make_async_remote_copy(
            src_ref=halo_out.at[0 if up else 1], dst_ref=halo_in.at[1 if up else 0],
            send_sem=lh_send.at[0 if up else 1], recv_sem=lh_recv.at[1 if up else 0],
            device_id=(me, row - 1 if up else row + 1), device_id_type=MESH,
        )

    def arrived(dst, sem):
        return pltpu.make_async_remote_copy(
            src_ref=dst, dst_ref=dst, send_sem=sem, recv_sem=sem,
            device_id=(me, row), device_id_type=MESH,
        ).wait_recv()

    pl.semaphore_wait(
        barrier, views - 1 + views * (above.astype(jnp.int32) + below.astype(jnp.int32))
    )

    def send_shift(j, carry):
        shift_copy(j).start()
        return carry

    lax.fori_loop(1, views, send_shift, 0, unroll=5)

    def send_all(j, carry):
        @pl.when(j > 0)
        def _():
            win_copy(j).start()

        @pl.when(above)
        def _():
            up_copy(j).start()

        @pl.when(below)
        def _():
            down_copy(j).start()

        return carry

    lax.fori_loop(0, views, send_all, 0, unroll=4)

    fetch_layers.wait()
    for f in range(frames):
        for k in range(layer_count):
            def load(tile):
                where = pl.ds(pl.multiple_of(tile * LANES, LANES), LANES)
                return layers_ref[f, k, :, where].astype(jnp.float32)

            plane = window(load, me)
            at = f * layer_count + k
            layer_win[at, EDGE : EDGE + rows, :] = plane
            halo_out[0, at] = plane[:EDGE].astype(jnp.bfloat16)
            halo_out[1, at] = plane[rows - EDGE :].astype(jnp.bfloat16)

    @pl.when(above)
    def _():
        layer_copy(True).start()

    @pl.when(below)
    def _():
        layer_copy(False).start()

    @pl.when(jnp.logical_not(above))
    def _():
        recv_win[:, :EDGE, :] = jnp.zeros((views, EDGE, LANES), jnp.bfloat16)
        layer_win[:, :EDGE, :] = jnp.zeros((planes, EDGE, LANES), jnp.float32)

    @pl.when(jnp.logical_not(below))
    def _():
        recv_win[:, EDGE + rows :, :] = jnp.zeros((views, EDGE, LANES), jnp.bfloat16)
        layer_win[:, EDGE + rows :, :] = jnp.zeros((planes, EDGE, LANES), jnp.float32)

    at_row = rows * row - HALO + lax.broadcasted_iota(jnp.int32, (inner, LANES), 0)
    at_col = strip * me - MARGIN + lax.broadcasted_iota(jnp.int32, (inner, LANES), 1)
    inside = (at_row >= 0) & (at_row < rows * rows_of) & (at_col >= 0) & (at_col < cols)
    third_win[...] = jnp.where(inside, 1.0 / frames, 0.0)
    upper[...] = jnp.zeros_like(upper)
    lower[...] = jnp.zeros_like(lower)

    def wait_shift(j, carry):
        source = lax.rem(me + views - j, views)
        arrived(shift_in.at[source], shift_recv.at[source])
        return carry

    lax.fori_loop(1, views, wait_shift, 0, unroll=5)
    to_smem = pltpu.make_async_copy(shift_in, shift_smem, smem_sem)
    to_smem.start()

    @pl.when(above)
    def _():
        arrived(halo_in.at[0], lh_recv.at[0])
        layer_win[:, :EDGE, :] = halo_in[0].astype(jnp.float32)

    @pl.when(below)
    def _():
        arrived(halo_in.at[1], lh_recv.at[1])
        layer_win[:, EDGE + rows :, :] = halo_in[1].astype(jnp.float32)

    to_smem.wait()

    def some_views(n, carry):
        views_now = []
        for b in range(BATCH):
            j = n * BATCH + b
            view = lax.rem(me + views - j, views)
            views_now.append(view)

            @pl.when(j > 0)
            def _():
                arrived(recv_win.at[view, pl.ds(EDGE, rows)], win_recv.at[view])

            @pl.when(above)
            def _():
                arrived(recv_win.at[view, pl.ds(0, EDGE)], down_recv.at[view])

            @pl.when(below)
            def _():
                arrived(recv_win.at[view, pl.ds(EDGE + rows, EDGE)], up_recv.at[view])

        row_shift, back = [], []
        for b, view in enumerate(views_now):
            target_win[b] = recv_win[view].astype(jnp.float32)
            row_now = [shift_smem[view, 0, 2 * k] for k in range(layer_count)]
            col_now = [shift_smem[view, 0, 2 * k + 1] for k in range(layer_count)]
            there = [lax.rem(LANES - c, LANES) for c in col_now]
            row_shift.append(row_now)
            back.append([lax.rem(LANES + c, LANES) for c in col_now])
            total = None
            for f in range(frames):
                seen = [
                    pltpu.roll(
                        layer_win[f * layer_count + k, pl.ds(EDGE - HALO + row_now[k], inner), :],
                        there[k], 1,
                    )
                    for k in range(layer_count)
                ]
                for k in range(layer_count):
                    rest = None
                    for i in range(layer_count):
                        if i != k:
                            rest = seen[i] if rest is None else rest * seen[i]
                    others_win[b, f * layer_count + k] = rest
                    if k == layer_count - 1:
                        whole = rest * seen[k]
                        total = whole if total is None else total + whole
            shown_win[b] = total * third_win[...]

        for k in range(layer_count):
            image, model = [], []
            for b in range(BATCH):
                turn, by = back[b][k], row_shift[b][k]
                image.append(pltpu.roll(target_win[b, pl.ds(EDGE - by, rows), :], turn, 1))
                model.append(pltpu.roll(shown_win[b, pl.ds(HALO - by, rows), :], turn, 1))
            for f in range(frames):
                at = f * layer_count + k
                up, low = upper[at], lower[at]
                for b in range(BATCH):
                    rest = pltpu.roll(
                        others_win[b, at, pl.ds(HALO - row_shift[b][k], rows), :], back[b][k], 1
                    )
                    up += image[b] * rest
                    low += model[b] * rest
                upper[at] = up
                lower[at] = low
        return carry

    lax.fori_loop(0, views // BATCH, some_views, 0)

    core = lax.rem(me, 2)
    x = lax.rem(me // 2, across)
    z = me // (2 * across)

    def index(zz, xx, cc):
        return (zz * across + xx) * 2 + cc

    chunks = 2 if packed.shape[0] % 32 == 0 else 1
    size = packed.shape[0] // chunks

    def part_of(slot, c):
        return slots.at[slot, pl.ds(c * size, size)]

    def slot_copy(slot, to, sem, c):
        return pltpu.make_async_remote_copy(
            src_ref=part_of(slot, c), dst_ref=part_of(slot, c), send_sem=sem,
            recv_sem=slot_recv.at[c, slot], device_id=(to, row), device_id_type=MESH,
        )

    def slot_here(slot, c):
        arrived(part_of(slot, c), slot_recv.at[c, slot])

    def along(d):
        return index(z + d, x, core)

    def to_column(d, c):
        return slot_copy(me, index(z + d, x, core), col_send.at[c, depth + d], c)

    def to_across(d, dx, c):
        to = index(z, lax.rem(x + dx, across), core)
        return slot_copy(along(d), to, x_send.at[c, depth + d, dx], c)

    def to_core(d, dx, c):
        slot = index(z + d, lax.rem(x + across - dx, across), core)
        return slot_copy(slot, index(z, x, 1 - core), core_send.at[c, depth + d, dx], c)

    def exists(d):
        return (z + d >= 0) & (z + d < depth)

    def visit(d, act):
        if d:
            pl.when(exists(d))(act)
        else:
            act()

    def both_ways(d):
        return (-d, d) if d else (0,)

    def each_copy(d, act, c):
        if d:
            act(to_column(d, c))
        for dx in range(1, across):
            act(to_across(d, dx, c))
        act(to_core(d, 0, c))

    def spread(d, c):
        for dx in range(1, across):
            to_across(d, dx, c).start()
        to_core(d, 0, c).start()

    def column_step(d, c):
        def act():
            slot_here(along(d), c)
            spread(d, c)

        visit(d, act)

    def across_step(d, c):
        def act():
            for dx in range(1, across):
                slot_here(index(z + d, lax.rem(x + across - dx, across), core), c)
                to_core(d, dx, c).start()

        visit(d, act)

    spare = packed.shape[0] - planes * short
    if spare:
        packed[planes * short :, :] = jnp.zeros((spare, LANES), jnp.float32)
    done = 0
    for c in range(chunks):
        while done < planes and done * short < (c + 1) * size:
            ratio = (upper[done] + REGULAR) / (lower[done] + REGULAR)
            value = (jnp.log(ratio) - middle) * (1.0 / step)
            merged = pltpu.roll(value[:short], LANES - MARGIN, 1)
            if groups == 2:
                other = pltpu.roll(value[short:], strip - MARGIN, 1)
                merged = jnp.where(lane < strip, merged, other)
            packed[done * short : (done + 1) * short, :] = merged
            done += 1
        span = slice(c * size, (c + 1) * size)
        slots[me, span, :] = jnp.round(packed[span, :]).astype(jnp.int32).astype(jnp.int16)
        spread(0, c)
        for distance in range(1, depth):
            for d in both_ways(distance):
                def act():
                    to_column(d, c).start()

                visit(d, act)

    @pl.when(above)
    def _():
        layer_copy(True).wait_send()

    @pl.when(below)
    def _():
        layer_copy(False).wait_send()

    def finish(j, carry):
        @pl.when(j > 0)
        def _():
            shift_copy(j).wait_send()
            win_copy(j).wait_send()

        @pl.when(above)
        def _():
            up_copy(j).wait_send()

        @pl.when(below)
        def _():
            down_copy(j).wait_send()

        return carry

    lax.fori_loop(0, views, finish, 0)

    for distance in range(1, depth):
        for c in range(chunks):
            for d in both_ways(distance):
                column_step(d, c)
            for d in both_ways(distance - 1):
                across_step(d, c)

    per_tile = LANES // strip

    def store_tile(tile):
        where = pl.ds(pl.multiple_of(tile * LANES, LANES), LANES)
        return pltpu.make_async_copy(
            out_ref.at[:, :, :, where], out_hbm.at[:, :, :, where], store_sem.at[tile]
        )

    def unpack(tile):
        for i in range(per_tile):
            @pl.when(lax.rem(tile * per_tile + i, 2) != core)
            def _():
                for c in range(chunks):
                    slot_here(tile * per_tile + i, c)

        where = pl.ds(pl.multiple_of(tile * LANES, LANES), LANES)
        parts = [slots[tile * per_tile + i].astype(jnp.int32) for i in range(per_tile)]
        for f in range(frames):
            for k in range(layer_count):
                at = f * layer_count + k
                spans = []
                for g in range(groups):
                    code = None
                    for i in range(per_tile):
                        part = parts[i][at * short : (at + 1) * short]
                        turn = (strip * (i - g)) % LANES
                        if turn:
                            part = pltpu.roll(part, turn, 1)
                        code = part if code is None else jnp.where(lane < strip * i, code, part)
                    spans.append(code)
                whole = jnp.concatenate(spans, axis=0) if groups > 1 else spans[0]
                out_ref[f, k, :, where] = whole.astype(jnp.int16)
        store_tile(tile).start()

    early = strip == 64

    def unpack_column(n, carry):
        unpack(n * across + x)
        return carry

    if early:
        lax.fori_loop(0, depth, unpack_column, 0)
    for c in range(chunks):
        for d in both_ways(depth - 1):
            across_step(d, c)

    def unpack_rest(n, carry):
        zz, dx = n // (across - 1), lax.rem(n, across - 1) + 1
        unpack(zz * across + lax.rem(x + dx, across))
        return carry

    def unpack_any(n, carry):
        unpack(n)
        return carry

    if early:
        lax.fori_loop(0, depth * (across - 1), unpack_rest, 0)
    else:
        lax.fori_loop(0, tiles, unpack_any, 0)

    for distance in range(depth):
        for d in both_ways(distance):
            def act():
                for c in range(chunks):
                    each_copy(d, lambda copy: copy.wait_send(), c)
                    for dx in range(1, across):
                        to_core(d, dx, c).wait_send()

            visit(d, act)

    def wait_store(tile, carry):
        store_tile(tile).wait()
        return carry

    lax.fori_loop(0, tiles, wait_store, 0)


def decode(views, codes_hbm, layers_hbm, out_hbm, codes, layers, out, sems):
    frames, layer_count = layers.shape[:2]
    middle, step = code_range(views)
    moves = []
    for f in range(frames):
        for k in range(layer_count):
            at = f * layer_count + k
            moves.append((
                pltpu.make_async_copy(codes_hbm.at[f, k], codes.at[f, k], sems.at[0, at]),
                pltpu.make_async_copy(layers_hbm.at[f, k], layers.at[f, k], sems.at[1, at]),
                pltpu.make_async_copy(out.at[f, k], out_hbm.at[f, k], sems.at[2, at]),
            ))
    for code_in, layer_in, _ in moves:
        code_in.start()
        layer_in.start()
    for at, (code_in, layer_in, store) in enumerate(moves):
        f, k = at // layer_count, at % layer_count
        code_in.wait()
        layer_in.wait()
        ratio = jnp.exp(codes[f, k].astype(jnp.int32).astype(jnp.float32) * step + middle)
        out[f, k] = layers[f, k].astype(jnp.float32) * ratio
        store.start()
    for _, _, store in moves:
        store.wait()


def body(views, rows_of, layers, target, shifts):
    frames, layer_count, rows, cols = layers.shape
    planes = frames * layer_count
    strip = cols // views
    groups = 2 if strip == 64 else 1
    depth, across = split_views(views)
    packed_rows = -(-planes * (rows // groups) // 16) * 16
    height, inner = rows + 2 * EDGE, rows + 2 * HALO
    dma = pltpu.SemaphoreType.DMA
    f32, bf16 = jnp.float32, jnp.bfloat16
    codes = pl.pallas_call(
        functools.partial(kernel, views, rows_of),
        out_shape=jax.ShapeDtypeStruct(layers.shape, jnp.int16),
        in_specs=[
            pl.BlockSpec(memory_space=pltpu.HBM),
            pl.BlockSpec(memory_space=pltpu.HBM),
            pl.BlockSpec(memory_space=pltpu.HBM),
        ],
        out_specs=pl.BlockSpec(memory_space=pltpu.HBM),
        scratch_shapes=[
            pltpu.SMEM((1, 2, layer_count), jnp.int32),
            pltpu.VMEM(layers.shape, bf16),
            pltpu.VMEM(target.shape, bf16),
            pltpu.VMEM(layers.shape, jnp.int16),
            dma((3,)),
            dma((cols // LANES,)),
            pltpu.VMEM((views, rows, LANES), bf16),
            pltpu.VMEM((views, height, LANES), bf16),
            pltpu.VMEM((1, LANES), jnp.int32),
            pltpu.VMEM((views, 1, LANES), jnp.int32),
            pltpu.SMEM((views, 1, LANES), jnp.int32),
            pltpu.VMEM((2, planes, EDGE, LANES), bf16),
            pltpu.VMEM((2, planes, EDGE, LANES), bf16),
            pltpu.VMEM((planes, height, LANES), f32),
            pltpu.VMEM((BATCH, height, LANES), f32),
            pltpu.VMEM((BATCH, planes, inner, LANES), f32),
            pltpu.VMEM((BATCH, inner, LANES), f32),
            pltpu.VMEM((inner, LANES), f32),
            pltpu.VMEM((planes, rows, LANES), f32),
            pltpu.VMEM((planes, rows, LANES), f32),
            pltpu.VMEM((packed_rows, LANES), f32),
            pltpu.VMEM((views, packed_rows, LANES), jnp.int16),
            dma((views,)), dma((views,)), dma((views,)), dma((views,)), dma((views,)), dma((views,)),
            dma((views,)), dma((views,)), dma, dma((2,)), dma((2,)),
            dma((2, 2 * depth)), dma((2, 2 * depth, across)), dma((2, 2 * depth, across)), dma((2, views)),
        ],
        compiler_params=pltpu.CompilerParams(
            collective_id=0, has_side_effects=True, vmem_limit_bytes=62 * 1024 * 1024
        ),
        name="light_field_update",
    )(jnp.swapaxes(shifts, 1, 2), layers, target)
    return pl.pallas_call(
        functools.partial(decode, views),
        out_shape=jax.ShapeDtypeStruct(layers.shape, f32),
        in_specs=[pl.BlockSpec(memory_space=pltpu.HBM)] * 2,
        out_specs=pl.BlockSpec(memory_space=pltpu.HBM),
        scratch_shapes=[
            pltpu.VMEM(layers.shape, jnp.int16),
            pltpu.VMEM(layers.shape, bf16),
            pltpu.VMEM(layers.shape, f32),
            dma((3, planes)),
        ],
        compiler_params=pltpu.CompilerParams(vmem_limit_bytes=62 * 1024 * 1024),
        name="decode_ratio",
    )(codes, layers)


def solution(mesh):
    placed = (P(None, None, "row", None), P("view", "row", None), P("view", None, None))
    return jax.shard_map(
        functools.partial(body, mesh.shape["view"], mesh.shape["row"]),
        mesh=mesh, in_specs=placed, out_specs=P(None, None, "row", None), check_vma=False,
    )
```
